32 devices in a mesh: pair: 2 (over y), rows: 16 (over z, x, core).
Axes of the slice: x: 2, y: 2, z: 4, core: 2. Of those that a mesh axis runs over, the one named last changes fastest.
Arguments:
- inputs: bfloat16 [2, 16, 2, 256, 1024], P(None, 'rows', 'pair'), may hold values from -6 to 6
- cotangent: bfloat16 [2, 16, 2, 256, 1024], P(None, 'rows', 'pair'), may hold values from -6 to 6
- phone_len: int32 [2, 16, 2], P(None, 'rows'), may hold values from 1 to 96, as said below
- prompt_len: int32 [2, 16, 2], P(None, 'rows'), may hold values from 32 to 191, as said below
- target_len: int32 [2, 16, 2], P(None, 'rows'), may hold values from 64 to 192, as said below
- ln1_gain: bfloat16 [1024], P(('pair', 'rows')), may hold values from 0.5 to 1.5
- ln1_bias: bfloat16 [1024], P(('pair', 'rows')), may hold values from -3 to 3
- w_qkv: bfloat16 [1024, 3072], P(('pair', 'rows')), may hold values from -0.1875 to 0.1875
- w_out: bfloat16 [1024, 1024], P(('pair', 'rows')), may hold values from -0.5 to 0.5
- ln2_gain: bfloat16 [1024], P(('pair', 'rows')), may hold values from 0.5 to 1.5
- ln2_bias: bfloat16 [1024], P(('pair', 'rows')), may hold values from -3 to 3
- w_up: bfloat16 [1024, 4096], P(('pair', 'rows')), may hold values from -0.1875 to 0.1875
- up_bias: bfloat16 [4096], P(('pair', 'rows')), may hold values from -3 to 3
- w_down: bfloat16 [4096, 1024], P(('pair', 'rows')), may hold values from -0.09375 to 0.09375
Outputs:
- outputs: bfloat16 [2, 16, 2, 256, 1024], P(None, 'rows', 'pair')
- input_grad: float32 [2, 16, 2, 256, 1024], P(None, 'rows', 'pair')
- grad_ln1_gain: float32 [1024], P(('pair', 'rows'))
- grad_ln1_bias: float32 [1024], P(('pair', 'rows'))
- grad_qkv: float32 [1024, 3072], P(('pair', 'rows'))
- grad_out: float32 [1024, 1024], P(('pair', 'rows'))
- grad_ln2_gain: float32 [1024], P(('pair', 'rows'))
- grad_ln2_bias: float32 [1024], P(('pair', 'rows'))
- grad_up: float32 [1024, 4096], P(('pair', 'rows'))
- grad_up_bias: float32 [4096], P(('pair', 'rows'))
- grad_down: float32 [4096, 1024], P(('pair', 'rows'))
The draws below stay inside these ranges and needn't reach their ends.
Inputs may be any that keep to these rules, and one draw needn't show every extreme that they name: In each packed row, phone_len plus prompt_len summed over its 2 utterances is exactly 256, each utterance's phone_len plus prompt_len lies between 64 and 192, and phone_len is at most half of phone_len plus prompt_len. `prompt_len`: see phone_len for the row sums. `target_len`: in each packed row the target lengths of its 2 utterances sum to exactly 256.
All inputs are finite; a program needn't handle non-finite values.
Results may differ from the reference program's by a relative error of at most 0.011.
Values may be sent and summed in bfloat16 or wider, within the bound.
No kernel may reach another device: no remote copies, remote signals or barrier semaphores. Data moves between devices by JAX's collectives and lax.ppermute only.
A program may use at most 256 MiB of HBM per device.

```python
import jax
import jax.numpy as jnp
from jax import lax

D = 1024
HEADS = 16
HEAD = 64
FF = 4096
ROW = 256
MICRO = 2
SEGS = 2
NROWS = 16
HALVES = 2


def split_pair(key, forced_rows, lower, upper):
    row_count = MICRO * NROWS
    first = jax.random.randint(key, (row_count,), lower, upper + 1, dtype=jnp.int32)
    first = jnp.where(forced_rows, upper, first)
    return jnp.stack([first, ROW - first], -1)


def all_lengths(key):
    row_count = MICRO * NROWS
    key_pick = jax.random.fold_in(key, 10)
    key_prefix = jax.random.fold_in(key, 11)
    key_phone = jax.random.fold_in(key, 12)
    key_target = jax.random.fold_in(key, 13)
    lower = ROW // 4
    upper = ROW - ROW // 4
    chosen = jax.random.randint(key_pick, (), 0, row_count, dtype=jnp.int32)
    second = (chosen + 1) % row_count
    row_ids = jnp.arange(row_count, dtype=jnp.int32)
    is_first = row_ids == chosen
    is_second = row_ids == second
    prefix_len = split_pair(key_prefix, is_first | is_second, lower, upper)
    phone_part = jax.random.randint(key_phone, prefix_len.shape, 1, prefix_len // 2 + 1, dtype=jnp.int32)
    seg_ids = jnp.arange(SEGS, dtype=jnp.int32)[None, :]
    phone_part = jnp.where(is_first[:, None] & (seg_ids == 0), 1, phone_part)
    phone_part = jnp.where(is_second[:, None], prefix_len // 2, phone_part)
    target_part = split_pair(key_target, is_first, lower, upper)
    shape = (MICRO, NROWS, SEGS)
    return (phone_part.reshape(shape), (prefix_len - phone_part).reshape(shape), target_part.reshape(shape))


def draw_phone_len(key, part):
    return all_lengths(key)[0]


def draw_prompt_len(key, part):
    return all_lengths(key)[1]


def draw_target_len(key, part):
    return all_lengths(key)[2]


def level_of(stream_key, shape, pieces, least, high):
    def one(position, shards_of):
        steps = jax.random.uniform(jax.random.fold_in(jax.random.fold_in(stream_key, 6), position), (shards_of,), jnp.float32, least / len(pieces), high / len(pieces))
        return jnp.repeat(jnp.exp(steps), shape[position] // shards_of).reshape((-1,) + (1,) * (len(shape) - position - 1))

    level = one(*pieces[0])
    for cut in pieces[1:]:
        level = level * one(*cut)
    return level


def centred(stream_key, shape, scale, reach, cuts=(), held_as=jnp.bfloat16):
    drawn = scale * jax.random.normal(stream_key, shape, jnp.float32)
    if cuts:
        drawn = drawn * level_of(stream_key, shape, cuts, -0.22, 0.18)
    return jnp.clip(drawn, -reach, reach).astype(held_as)


def setup_inputs(seed: int = 0) -> dict:
    streams_of = jax.random.split(jax.random.key(seed), 15)
    return {
        "inputs": centred(streams_of[0], (MICRO, NROWS, HALVES, ROW, D), 1.0, 6.0, ((1, 16), (2, 2))),
        "cotangent": centred(streams_of[1], (MICRO, NROWS, HALVES, ROW, D), 1.0, 6.0, ((1, 16), (2, 2))),
        "phone_len": draw_phone_len(jax.random.fold_in(streams_of[14], 71), 0),
        "prompt_len": draw_prompt_len(jax.random.fold_in(streams_of[14], 71), 0),
        "target_len": draw_target_len(jax.random.fold_in(streams_of[14], 71), 0),
        "ln1_gain": jnp.clip(1.0 + 0.1 * jax.random.normal(streams_of[5], (D,), jnp.float32), 0.5, 1.5).astype(jnp.bfloat16),
        "ln1_bias": centred(streams_of[6], (D,), 0.5, 3.0, ((0, 32),)),
        "w_qkv": centred(streams_of[7], (D, 3 * D), D ** -0.5, 0.1875, ((0, 32),)),
        "w_out": centred(streams_of[8], (D, D), (D // 8) ** -0.5, 0.5, ((0, 32),)),
        "ln2_gain": jnp.clip(1.0 + 0.1 * jax.random.normal(streams_of[9], (D,), jnp.float32), 0.5, 1.5).astype(jnp.bfloat16),
        "ln2_bias": centred(streams_of[10], (D,), 0.5, 3.0, ((0, 32),)),
        "w_up": centred(streams_of[11], (D, FF), D ** -0.5, 0.1875, ((0, 32),)),
        "up_bias": centred(streams_of[12], (FF,), 0.5, 3.0, ((0, 32),)),
        "w_down": centred(streams_of[13], (FF, D), FF ** -0.5, 0.09375, ((0, 32),)),
    }


@jax.custom_vjp
def low(v):
    return lax.optimization_barrier(v.astype(jnp.bfloat16)).astype(jnp.float32)

@jax.custom_vjp
def low_back(v):
    return v

def low_keep(v):
    return (low(v), None)

def low_pass(kept, grad):
    return (grad,)

def back_keep(v):
    return (v, None)

def back_low(kept, grad):
    return (low(grad),)
low.defvjp(low_keep, low_pass)
low_back.defvjp(back_keep, back_low)

def matmul(left, right):
    return jnp.dot(left, right, precision=lax.Precision.HIGHEST)

def layer_norm(values, gain, bias):
    center = values - lax.optimization_barrier(jnp.mean(values, -1, keepdims=True))
    spread = lax.optimization_barrier(jnp.mean(center * center, -1, keepdims=True))
    return center * lax.rsqrt(spread + 1e-05) * gain + bias

def locate(lengths, slot_ids):
    seg_ends = jnp.cumsum(lengths, dtype=jnp.int32)
    seg_ids = lax.optimization_barrier(jnp.sum((slot_ids[:, None] >= seg_ends[None, :]).astype(jnp.int32), 1, dtype=jnp.int32))
    one_hot = (seg_ids[:, None] == jnp.arange(lengths.shape[0], dtype=jnp.int32)[None, :]).astype(jnp.int32)
    seg_start = lax.optimization_barrier(jnp.sum(one_hot * (seg_ends - lengths)[None, :], 1, dtype=jnp.int32))
    return (seg_ids, one_hot, slot_ids - seg_start)

def frame_meta(phone_lens, prompt_lens, target_lens, slot_count):
    slot_ids = jnp.arange(slot_count, dtype=jnp.int32)
    pre_seg, pre_hot, pre_off = locate(phone_lens + prompt_lens, slot_ids)
    pre_phone = lax.optimization_barrier(jnp.sum(pre_hot * phone_lens[None, :], 1, dtype=jnp.int32))
    prefix = (pre_seg, pre_off < pre_phone, pre_off - pre_phone)
    tgt_seg, tgt_hot, tgt_off = locate(target_lens, slot_ids)
    tgt_pos = lax.optimization_barrier(jnp.sum(tgt_hot * prompt_lens[None, :], 1, dtype=jnp.int32)) + tgt_off
    targets = (tgt_seg, tgt_off < 0, tgt_pos)
    return (prefix, targets)

def allowed(query_meta, key_meta):
    same_seg = query_meta[0][:, None] == key_meta[0][None, :]
    audio_ok = key_meta[1][None, :] | (key_meta[2][None, :] <= query_meta[2][:, None])
    return same_seg & jnp.where(query_meta[1][:, None], key_meta[1][None, :], audio_ok)

def forward(resident, params, allowed_mask):
    ln1_gain, ln1_bias, w_qkv, w_out, ln2_gain, ln2_bias, w_up, up_bias, w_down = params
    row_total = resident.shape[0]
    normed = low(layer_norm(resident, ln1_gain, ln1_bias))
    qkv_all = low_back(low(matmul(normed, w_qkv)))
    queries = qkv_all[:, :D].reshape(row_total, HEADS, HEAD)
    key_rows = qkv_all[:, D:2 * D].reshape(row_total, HEADS, HEAD)
    value_rows = qkv_all[:, 2 * D:].reshape(row_total, HEADS, HEAD)
    scores = low_back(jnp.einsum('qhd,khd->hqk', queries, key_rows, precision=lax.Precision.HIGHEST) * HEAD ** (-0.5))
    scores = jnp.where(allowed_mask[None], scores, -1e+30)
    peak = lax.optimization_barrier(jnp.max(scores, -1, keepdims=True))
    exp_scores = jnp.exp(scores - peak)
    probs = low(exp_scores / lax.optimization_barrier(jnp.sum(exp_scores, -1, keepdims=True)))
    mixed = jnp.einsum('hqk,khd->qhd', probs, value_rows, precision=lax.Precision.HIGHEST)
    mixed = low_back(low(mixed.reshape(row_total, D)))
    hidden_res = resident + low_back(matmul(mixed, w_out))
    normed_two = low(layer_norm(hidden_res, ln2_gain, ln2_bias))
    pre_act = low_back(matmul(normed_two, w_up) + up_bias)
    activ = low(jax.nn.gelu(pre_act, approximate=True))
    return hidden_res + low_back(matmul(activ, w_down))

def reference(inputs, cotangent, phone_len, prompt_len, target_len, ln1_gain, ln1_bias, w_qkv, w_out, ln2_gain, ln2_bias, w_up, up_bias, w_down):
    params = tuple((weight_arg.astype(jnp.float32) for weight_arg in (ln1_gain, ln1_bias, w_qkv, w_out, ln2_gain, ln2_bias, w_up, up_bias, w_down)))
    row_count = MICRO * NROWS
    flat_in = inputs.reshape(row_count, HALVES * ROW, D)
    flat_ct = cotangent.reshape(row_count, HALVES * ROW, D)
    phones = phone_len.reshape(row_count, SEGS)
    prompts = prompt_len.reshape(row_count, SEGS)
    target_rows = target_len.reshape(row_count, SEGS)

    def one_row(running, packed):
        row_in, row_ct, phone_row, prompt_row, target_row = packed
        prefix, targets = frame_meta(phone_row, prompt_row, target_row, ROW)
        merged = (jnp.concatenate([prefix[0], targets[0]]), jnp.concatenate([prefix[1], targets[1]]), jnp.concatenate([prefix[2], targets[2]]))
        allowed_mask = allowed(merged, merged)
        row_out, pullback = jax.vjp(lambda resident, params_in: forward(resident, params_in, allowed_mask), row_in.astype(jnp.float32), params)
        grad_in, grad_params = pullback(row_ct.astype(jnp.float32))
        running = jax.tree.map(lambda summed_part, fresh_part: summed_part + fresh_part, running, grad_params)
        return (running, (row_out.astype(jnp.bfloat16), grad_in))
    start_grads = tuple((jnp.zeros_like(weight_arg) for weight_arg in params))
    grads, (out_rows, grad_rows) = lax.scan(one_row, start_grads, (flat_in, flat_ct, phones, prompts, target_rows))
    full_shape = (MICRO, NROWS, HALVES, ROW, D)
    return (out_rows.reshape(full_shape), grad_rows.reshape(full_shape), grads[0], grads[1], grads[2], grads[3], grads[4], grads[5], grads[6], grads[7], grads[8])
```

```python
import functools

import jax
import jax.numpy as jnp
from jax import lax
from jax.experimental import pallas as pl
from jax.experimental.pallas import tpu as pltpu
from jax.sharding import PartitionSpec as P

D = 1024
HEADS = 16
HEAD = 64
FF = 4096
ROW = 256
MICRO = 2
BF = jnp.bfloat16
F32 = jnp.float32
NEG = -1e30


def position():
    row = lax.axis_index("rows")
    return lax.axis_index("pair"), row // 4, (row // 2) % 2, row % 2


def depth():
    return lax.axis_size("rows") // 4


def swap(block, way):
    if way == "y":
        return lax.ppermute(block, "pair", [(i, i ^ 1) for i in range(2)])
    count = lax.axis_size("rows")
    return lax.ppermute(block, "rows", [(i, i ^ way) for i in range(count)])


def after(block, *others):
    return lax.optimization_barrier((block, *others))[0]


def z_groups():
    count = lax.axis_size("rows")
    return [[z * 4 + low for z in range(count // 4)] for low in range(4)]


def gather_chips(block):
    count = depth()
    if count == 4:
        parts = [block[None]] + [swap(block[None], 4 * k) for k in range(1, 4)]
        first, second = jnp.concatenate(parts[:2], 0), jnp.concatenate(parts[2:], 0)
        done = parts[1:]
    else:
        column = lax.all_gather(block, "rows", axis_index_groups=z_groups())
        first, second = column[: count // 2], column[count // 2 :]
        done = [column]
    half = count // 2
    first_x, second_y = swap(first, 2), swap(second, "y")
    first_two = jnp.concatenate([first, first_x], 0)
    second_two = jnp.concatenate([second, second_y], 0)
    first_y, second_x = swap(first_two, "y"), swap(second_two, 2)
    ids = range(half)
    pieces = [
        (first_two, [(0, i, 0) for i in ids] + [(0, i, 1) for i in ids]),
        (first_y, [(1, i, 0) for i in ids] + [(1, i, 1) for i in ids]),
        (second_two, [(0, half + i, 0) for i in ids] + [(1, half + i, 0) for i in ids]),
        (second_x, [(0, half + i, 1) for i in ids] + [(1, half + i, 1) for i in ids]),
    ]
    return pieces, done


def chip_slot(rel, where, count):
    jy, jz, jx = rel
    y, z, x, _ = where
    z_at = (z ^ jz) if count == 4 else jz
    return ((y ^ jy) * count + z_at) * 2 + (x ^ jx)


def assemble(pieces, cores, cuts):
    count = depth()
    chips = 4 * count
    arrays = [p[0] for part in pieces for p in part]
    names = [(core, p[1]) for core, part in enumerate(pieces) for p in part]
    rows = arrays[0].shape[1]

    def kernel(*refs):
        ins = refs[: len(arrays)]
        outs, sems = refs[len(arrays) : -1], refs[-1]
        where = position()
        copies = []
        for ref, (core, rels) in zip(ins, names):
            for i, rel in enumerate(rels):
                slot = chip_slot(rel, where, count)
                at = (where[3] ^ core) if cores == 2 else 0
                for out, (start, width) in zip(outs, cuts):
                    copy = pltpu.make_async_copy(
                        ref.at[i, :, pl.ds(start, width)], out.at[slot, at], sems.at[len(copies)]
                    )
                    copy.start()
                    copies.append(copy)
        for copy in copies:
            copy.wait()

    return pl.pallas_call(
        kernel,
        out_shape=[
            jax.ShapeDtypeStruct((chips, cores, rows, width), arrays[0].dtype) for _, width in cuts
        ],
        in_specs=[pl.BlockSpec(memory_space=pl.ANY)] * len(arrays),
        out_specs=[pl.BlockSpec(memory_space=pltpu.VMEM)] * len(cuts),
        scratch_shapes=[pltpu.SemaphoreType.DMA((chips * cores * len(cuts),))],
        name="assemble",
    )(*arrays)


def layout():
    half = depth() // 2
    ids = range(half)
    return [
        [(1, i, jx) for jx in range(2) for i in ids],
        [(0, i, jx) for jx in range(2) for i in ids],
        [(jy, half + i, 1) for jy in range(2) for i in ids],
        [(jy, half + i, 0) for jy in range(2) for i in ids],
    ]


def disassemble(blocks):
    count = depth()
    shape = blocks.shape[1:]
    names = layout()

    def kernel(ref, *rest):
        outs, sems = rest[:4], rest[4]
        where = position()
        copies = []
        for out, rels in zip(outs, names):
            for i, rel in enumerate(rels):
                copy = pltpu.make_async_copy(
                    ref.at[chip_slot(rel, where, count)], out.at[i], sems.at[len(copies)]
                )
                copy.start()
                copies.append(copy)
        for copy in copies:
            copy.wait()

    return pl.pallas_call(
        kernel,
        out_shape=[jax.ShapeDtypeStruct((count, *shape), blocks.dtype)] * 4,
        in_specs=[pl.BlockSpec(memory_space=pltpu.VMEM)],
        out_specs=[pl.BlockSpec(memory_space=pl.ANY)] * 4,
        scratch_shapes=[pltpu.SemaphoreType.DMA((4 * count,))],
        name="disassemble",
    )(blocks)


def core_send(grads):
    chips, _, rows, _ = grads[0].shape
    widths = [g.shape[3] for g in grads]

    def kernel(*refs):
        ins, out, sems = refs[: len(grads)], refs[len(grads)], refs[-1]
        other = 1 - position()[3]
        copies, start = [], 0
        for n, (ref, width) in enumerate(zip(ins, widths)):
            copy = pltpu.make_async_copy(
                ref.at[:, other], out.at[:, :, pl.ds(start, width)], sems.at[n]
            )
            copy.start()
            copies.append(copy)
            start += width
        for copy in copies:
            copy.wait()

    return pl.pallas_call(
        kernel,
        out_shape=jax.ShapeDtypeStruct((chips, rows, sum(widths)), grads[0].dtype),
        in_specs=[pl.BlockSpec(memory_space=pltpu.VMEM)] * len(grads),
        out_specs=pl.BlockSpec(memory_space=pl.ANY),
        scratch_shapes=[pltpu.SemaphoreType.DMA((len(grads),))],
        name="core_send",
    )(*grads)


def core_sum(grads, arrived):
    count = depth()
    chips, _, rows, _ = grads[0].shape
    widths = [g.shape[3] for g in grads]
    names = layout()

    def kernel(*refs):
        ins, arr, outs = refs[: len(grads)], refs[len(grads)], refs[len(grads) + 1 :]
        where = position()
        for out, rels in zip(outs, names):
            for i, rel in enumerate(rels):
                slot = chip_slot(rel, where, count)
                start = 0
                for ref, width in zip(ins, widths):
                    own = ref[slot, where[3]].astype(F32)
                    other = arr[slot, :, start : start + width].astype(F32)
                    out[i, :, start : start + width] = (own + other).astype(BF)
                    start += width

    return pl.pallas_call(
        kernel,
        out_shape=[jax.ShapeDtypeStruct((count, rows, sum(widths)), grads[0].dtype)] * 4,
        in_specs=[pl.BlockSpec(memory_space=pltpu.VMEM)] * (len(grads) + 1),
        out_specs=[pl.BlockSpec(memory_space=pltpu.VMEM)] * 4,
        name="core_sum",
    )(*grads, arrived)


def plus(left, right):
    return (left.astype(F32) + right.astype(F32)).astype(left.dtype)


def scatter_chips(parts):
    count = depth()
    half = count // 2
    first_send, first_keep, second_send, second_keep = parts
    first_in, second_in = swap(first_send, "y"), swap(second_send, 2)
    first_out = plus(first_keep[half:], first_in[half:])
    first_own = plus(first_keep[:half], first_in[:half])
    second_out = plus(second_keep[half:], second_in[half:])
    second_own = plus(second_keep[:half], second_in[:half])
    first_in, second_in = swap(first_out, 2), swap(second_out, "y")
    if count == 4:
        total = first_own[0].astype(F32) + first_in[0].astype(F32)
        one = plus(first_own[1], first_in[1])
        two = plus(second_own, second_in)
        total = total + swap(one, 4).astype(F32)
        total = total + swap(two[0], 8).astype(F32)
        return total + swap(two[1], 12).astype(F32)
    column = jnp.concatenate([plus(first_own, first_in), plus(second_own, second_in)], 0)
    return lax.psum_scatter(
        column.astype(F32), "rows", scatter_dimension=0, axis_index_groups=z_groups()
    )


def ordered(flag, own, other, axis):
    return jnp.where(
        flag == 0,
        jnp.concatenate([own, other], axis),
        jnp.concatenate([other, own], axis),
    )


def ends(lengths_ref, count):
    out, total = [], 0
    for s in range(count):
        total = total + lengths_ref[s]
        out.append(total)
    return out


def frames(index, phone, prompt, target, segs):
    pre_end = ends_of([phone[s] + prompt[s] for s in range(segs)])
    tgt_end = ends_of([target[s] for s in range(segs)])
    is_target = index >= ROW
    local = jnp.where(is_target, index - ROW, index)
    seg = jnp.zeros_like(index)
    for s in range(segs):
        edge = jnp.where(is_target, tgt_end[s], pre_end[s])
        seg = seg + jnp.where(local >= edge, 1, 0)
    start = jnp.zeros_like(index)
    phones = jnp.zeros_like(index)
    prompts = jnp.zeros_like(index)
    for s in range(segs):
        pick = seg == s
        pre_start = pre_end[s] - phone[s] - prompt[s]
        tgt_start = tgt_end[s] - target[s]
        start = jnp.where(pick, jnp.where(is_target, tgt_start, pre_start), start)
        phones = jnp.where(pick, phone[s], phones)
        prompts = jnp.where(pick, prompt[s], prompts)
    off = local - start
    is_phone = jnp.where(is_target, 0, jnp.where(off < phones, 1, 0))
    pos = jnp.where(is_target, prompts + off, off - phones)
    return seg, is_phone, pos


def ends_of(lengths):
    out, total = [], 0
    for length in lengths:
        total = total + length
        out.append(total)
    return out


def bias_of(query, key):
    q_seg, q_phone, q_pos = query
    k_seg, k_phone, k_pos = key
    audio = (k_phone == 1) | (k_pos <= q_pos)
    good = (q_seg == k_seg) & (((q_phone == 1) & (k_phone == 1)) | ((q_phone == 0) & audio))
    return jnp.where(good, 0.0, NEG)


def bdot(left, right, dims):
    return lax.dot_general(left, right, (dims, ((), ())), preferred_element_type=F32)


NT = ((1,), (1,))
NN = ((1,), (0,))
TN = ((0,), (0,))


def attention_forward(qkv, phone, prompt, target):
    segs = phone.shape[0]

    def kernel(phone_ref, prompt_ref, target_ref, q_ref, k_ref, v_ref, out_ref, bias_ref):
        @pl.when(pl.program_id(0) == 0)
        def _():
            ph = [phone_ref[s] for s in range(segs)]
            pr = [prompt_ref[s] for s in range(segs)]
            tg = [target_ref[s] for s in range(segs)]
            rows = lax.broadcasted_iota(jnp.int32, (2 * ROW, 1), 0)
            cols = lax.broadcasted_iota(jnp.int32, (1, 2 * ROW), 1)
            bias_ref[...] = bias_of(
                frames(rows, ph, pr, tg, segs), frames(cols, ph, pr, tg, segs)
            )

        lane = lax.broadcasted_iota(jnp.int32, (1, 2 * HEAD), 1)
        for rows, keys in ((0, ROW), (ROW, 2 * ROW)):
            outs = []
            for j in range(2):
                sel = (lane // HEAD) == j
                q = jnp.where(sel, q_ref[rows : rows + ROW, :], jnp.zeros((), BF))
                s = bdot(q, k_ref[:keys, :], NT) * HEAD**-0.5
                s = s + bias_ref[rows : rows + ROW, :keys]
                e = jnp.exp(s - jnp.max(s, 1, keepdims=True))
                p = (e * (1.0 / jnp.sum(e, 1, keepdims=True))).astype(BF)
                outs.append(bdot(p, v_ref[:keys, :], NN))
            out_ref[rows : rows + ROW, :] = jnp.where(lane < HEAD, outs[0], outs[1]).astype(BF)

    pairs = HEADS // 2
    smem = pl.BlockSpec(memory_space=pltpu.SMEM)
    return pl.pallas_call(
        kernel,
        grid=(pairs,),
        out_shape=jax.ShapeDtypeStruct((2 * ROW, D), BF),
        in_specs=[
            smem,
            smem,
            smem,
            pl.BlockSpec((2 * ROW, 2 * HEAD), lambda h: (0, h)),
            pl.BlockSpec((2 * ROW, 2 * HEAD), lambda h: (0, h + pairs)),
            pl.BlockSpec((2 * ROW, 2 * HEAD), lambda h: (0, h + 2 * pairs)),
        ],
        out_specs=pl.BlockSpec((2 * ROW, 2 * HEAD), lambda h: (0, h)),
        scratch_shapes=[pltpu.VMEM((2 * ROW, 2 * ROW), F32)],
        cost_estimate=pl.CostEstimate(
            flops=HEADS * 4 * 196608 * HEAD, bytes_accessed=4 << 20, transcendentals=3 << 20
        ),
        name="attention_forward",
    )(phone, prompt, target, qkv, qkv, qkv)


def attention_backward(qkv, grad_mixed, phone, prompt, target):
    segs = phone.shape[0]

    def kernel(
        phone_ref, prompt_ref, target_ref, q_ref, k_ref, v_ref, g_ref, dq_ref, dk_ref, dv_ref, bias_ref
    ):
        @pl.when(pl.program_id(0) == 0)
        def _():
            ph = [phone_ref[s] for s in range(segs)]
            pr = [prompt_ref[s] for s in range(segs)]
            tg = [target_ref[s] for s in range(segs)]
            rows = lax.broadcasted_iota(jnp.int32, (2 * ROW, 1), 0)
            cols = lax.broadcasted_iota(jnp.int32, (1, 2 * ROW), 1)
            bias_ref[...] = bias_of(
                frames(cols, ph, pr, tg, segs), frames(rows, ph, pr, tg, segs)
            )

        lane = lax.broadcasted_iota(jnp.int32, (1, 2 * HEAD), 1)
        zero = jnp.zeros((), BF)
        dqs = {}
        dks = {}
        dvs = {}
        for rows, keys in ((0, ROW), (ROW, 2 * ROW)):
            for j in range(2):
                sel = (lane // HEAD) == j
                q_all = q_ref[rows : rows + ROW, :]
                g_all = g_ref[rows : rows + ROW, :]
                q = jnp.where(sel, q_all, zero)
                g = jnp.where(sel, g_all, zero)
                k = k_ref[:keys, :]
                v = v_ref[:keys, :]
                s = bdot(k, q, NT) * HEAD**-0.5 + bias_ref[:keys, rows : rows + ROW]
                e = jnp.exp(s - jnp.max(s, 0, keepdims=True))
                p = e * (1.0 / jnp.sum(e, 0, keepdims=True))
                dp = bdot(v, g, NT)
                inner = jnp.sum(dp * p, 0, keepdims=True)
                ds = (p * (dp - inner)).astype(BF)
                dvs[rows, j] = bdot(p.astype(BF), g_all, NN)
                dks[rows, j] = bdot(ds, q_all, NN)
                dqs[rows, j] = bdot(ds, k, TN)
        low = lane < HEAD
        scale = HEAD**-0.5
        for rows in (0, ROW):
            dq_ref[rows : rows + ROW, :] = (
                jnp.where(low, dqs[rows, 0], dqs[rows, 1]) * scale
            ).astype(BF)
        for out, part, factor in ((dk_ref, dks, scale), (dv_ref, dvs, 1.0)):
            early = jnp.where(low, part[0, 0], part[0, 1])
            late = jnp.where(low, part[ROW, 0], part[ROW, 1])
            out[:ROW, :] = ((early + late[:ROW]) * factor).astype(BF)
            out[ROW:, :] = (late[ROW:] * factor).astype(BF)

    pairs = HEADS // 2
    smem = pl.BlockSpec(memory_space=pltpu.SMEM)
    block = (2 * ROW, 2 * HEAD)
    return pl.pallas_call(
        kernel,
        grid=(pairs,),
        out_shape=[jax.ShapeDtypeStruct((2 * ROW, D), BF)] * 3,
        in_specs=[
            smem,
            smem,
            smem,
            pl.BlockSpec(block, lambda h: (0, h)),
            pl.BlockSpec(block, lambda h: (0, h + pairs)),
            pl.BlockSpec(block, lambda h: (0, h + 2 * pairs)),
            pl.BlockSpec(block, lambda h: (0, h)),
        ],
        out_specs=[pl.BlockSpec(block, lambda h: (0, h))] * 3,
        scratch_shapes=[pltpu.VMEM((2 * ROW, 2 * ROW), F32)],
        cost_estimate=pl.CostEstimate(
            flops=HEADS * 10 * 196608 * HEAD, bytes_accessed=7 << 20, transcendentals=3 << 20
        ),
        name="attention_backward",
    )(phone, prompt, target, qkv, qkv, qkv, grad_mixed)


def norm_parts(values):
    center = values - jnp.mean(values, -1, keepdims=True)
    spread = jnp.mean(center * center, -1, keepdims=True)
    inv = lax.rsqrt(spread + 1e-05)
    return center * inv, inv


def norm_back(grad, normal, inv, gain):
    e = grad * gain
    return inv * (
        e - jnp.mean(e, -1, keepdims=True) - normal * jnp.mean(e * normal, -1, keepdims=True)
    )


def gelu_grad(v):
    c = (2.0 / jnp.pi) ** 0.5
    t = jnp.tanh(c * (v + 0.044715 * v * v * v))
    return 0.5 * (1.0 + t) + 0.5 * v * (1.0 - t * t) * c * (1.0 + 3 * 0.044715 * v * v)


def shards(
    inputs,
    cotangent,
    phone_len,
    prompt_len,
    target_len,
    ln1_gain,
    ln1_bias,
    w_qkv,
    w_out,
    ln2_gain,
    ln2_bias,
    w_up,
    up_bias,
    w_down,
):
    y, z, x, c = position()
    count = depth()
    chips = 4 * count
    row_w = w_qkv.shape[0]
    row_f = w_down.shape[0]

    def mine(stack):
        return lax.dynamic_index_in_dim(stack, y, 0, keepdims=False)

    def others(stack):
        return lax.dynamic_index_in_dim(stack, 1 - y, 0, keepdims=False)

    in_blocks = inputs[:, 0, 0]
    ct_blocks = cotangent[:, 0, 0]
    resident = ordered(y, mine(in_blocks), swap(others(in_blocks), "y"), 0)
    grad_result = ordered(y, mine(ct_blocks), swap(others(ct_blocks), "y"), 0)
    lengths = (mine(phone_len)[0], mine(prompt_len)[0], mine(target_len)[0])

    small = jnp.concatenate([ln1_gain, ln1_bias, ln2_gain, ln2_bias, up_bias])
    small = jnp.pad(small.reshape(row_w, -1), ((0, 0), (0, 128 - small.shape[0] // row_w)))
    attn_shard = jnp.concatenate([w_qkv, w_out, small], 1)
    up_split = w_up.reshape(row_w, chips, 2, FF // chips // 2)
    up_own = lax.dynamic_index_in_dim(up_split, c, 2, keepdims=False).reshape(row_w, FF // 2)
    up_other = lax.dynamic_index_in_dim(up_split, 1 - c, 2, keepdims=False).reshape(row_w, FF // 2)
    up_shard = ordered(c, up_own, swap(up_other, 1), 0)

    attn_pieces, attn_done = gather_chips(attn_shard)
    up_pieces, up_done = gather_chips(after(up_shard, *attn_done))
    down_pieces, _ = gather_chips(after(w_down, *up_done))

    attn_core = [(swap(array, 1), rels) for array, rels in attn_pieces]
    qkv_weight, out_weight, smalls = assemble(
        [attn_pieces, attn_core], 2, [(0, 3 * D), (3 * D, D), (4 * D, 128)]
    )
    qkv_weight = qkv_weight.reshape(D, 3 * D)
    out_weight = out_weight.reshape(D, D)
    width = (4 * row_w + row_f) // row_w
    smalls = smalls[..., :width].reshape(2 * chips, row_w * width)
    gain_one, bias_one, gain_two, bias_two = (
        smalls[:, i * row_w : (i + 1) * row_w].reshape(D).astype(F32) for i in range(4)
    )
    shift = smalls[:, 4 * row_w :].reshape(chips, 2, row_f).astype(F32)
    shift = lax.dynamic_index_in_dim(shift, c, 1, keepdims=False).reshape(FF // 2)
    [up_weight] = assemble([up_pieces], 1, [(0, FF // 2)])
    up_weight = up_weight.reshape(D, FF // 2)
    [down_weight] = assemble([down_pieces], 1, [(0, D)])
    down_weight = down_weight.reshape(FF // 2, D)

    resident_f = resident.astype(F32)
    normal_one, inv_one = norm_parts(resident_f)
    normed = (normal_one * gain_one + bias_one).astype(BF)
    qkv = jnp.dot(normed, qkv_weight, preferred_element_type=F32).astype(BF)
    mixed = attention_forward(qkv, *lengths)
    hidden = resident_f + jnp.dot(mixed, out_weight, preferred_element_type=F32)
    normal_two, inv_two = norm_parts(hidden)
    normed_two = (normal_two * gain_two + bias_two).astype(BF)
    normed_both = jnp.concatenate([normed_two, swap(normed_two, 1)], 0)
    pre_act = jnp.dot(normed_both, up_weight, preferred_element_type=F32) + shift
    activ = jax.nn.gelu(pre_act, approximate=True).astype(BF)
    ct_both = jnp.concatenate([grad_result, swap(grad_result, 1)], 0)
    grad_down = bdot(activ, ct_both, TN).astype(BF)
    sum_down = scatter_chips(disassemble(grad_down.reshape(chips, row_f, D)))
    down_out = jnp.dot(activ, down_weight, preferred_element_type=F32)
    result = hidden + down_out[: 2 * ROW] + swap(down_out[2 * ROW :], 1)
    result = result.astype(BF).reshape(2, ROW, D)

    grad_activ = bdot(ct_both, down_weight, NT)
    grad_pre_f = grad_activ * gelu_grad(pre_act)
    grad_pre = grad_pre_f.astype(BF)
    grad_up = bdot(normed_both, grad_pre, TN).astype(BF)
    sum_up = scatter_chips(disassemble(grad_up.reshape(chips, 2 * row_w, FF // 2)))
    grad_shift = jnp.sum(grad_pre.astype(F32), 0)
    grad_two_part = bdot(grad_pre, up_weight, NT)
    grad_two = grad_two_part[: 2 * ROW] + swap(grad_two_part[2 * ROW :], 1)
    grad_gain_two = jnp.sum(grad_two * normal_two, 0)
    grad_bias_two = jnp.sum(grad_two, 0)
    grad_hidden = grad_result.astype(F32) + norm_back(grad_two, normal_two, inv_two, gain_two)
    grad_low = grad_hidden.astype(BF)
    grad_out = bdot(mixed, grad_low, TN).astype(BF)
    grad_mixed = bdot(grad_low, out_weight, NT).astype(BF)
    dq, dk, dv = attention_backward(qkv, grad_mixed, *lengths)
    grad_qkv_rows = jnp.concatenate([dq, dk, dv], 1)
    grad_qkv = bdot(normed, grad_qkv_rows, TN).astype(BF)
    attn_grads = [grad_qkv.reshape(chips, 2, row_w, 3 * D), grad_out.reshape(chips, 2, row_w, D)]
    sum_attn = scatter_chips(core_sum(attn_grads, swap(core_send(attn_grads), 1)))
    grad_one = bdot(grad_qkv_rows, qkv_weight, NT)
    grad_gain_one = jnp.sum(grad_one * normal_one, 0)
    grad_bias_one = jnp.sum(grad_one, 0)
    input_grad = grad_hidden + norm_back(grad_one, normal_one, inv_one, gain_one)

    shift_two = grad_shift.reshape(chips, 1, row_f)
    shift_none = jnp.zeros_like(shift_two)
    shift_two = ordered(c, shift_two, shift_none, 1)
    parts = [
        v.reshape(chips, 2, row_w)
        for v in (grad_gain_one, grad_bias_one, grad_gain_two, grad_bias_two)
    ]
    small_grads = jnp.concatenate([*parts, shift_two], 2)
    small_send = lax.dynamic_index_in_dim(small_grads, 1 - c, 1, keepdims=False)
    small_keep = lax.dynamic_index_in_dim(small_grads, c, 1, keepdims=False)
    small_sum = small_keep + swap(small_send, 1)
    length = small_sum.shape[1]
    lines = -(-length // 1024) * 8
    small_sum = jnp.pad(small_sum, ((0, 0), (0, lines * 128 - length))).reshape(chips, lines, 128)
    small_sum = scatter_chips(disassemble(small_sum)).reshape(-1)

    def home(pair):
        own = lax.dynamic_index_in_dim(pair, y, 0, keepdims=False)
        away = swap(lax.dynamic_index_in_dim(pair, 1 - y, 0, keepdims=False), "y")
        return ordered(y, own[None], away[None], 0).reshape(MICRO, 1, 1, ROW, D)

    out_stack = home(result)
    grad_stack = home(input_grad.reshape(2, ROW, D))

    up_rows = sum_up.reshape(2, row_w, FF // 2)
    up_mine = lax.dynamic_index_in_dim(up_rows, c, 0, keepdims=False)
    up_theirs = swap(lax.dynamic_index_in_dim(up_rows, 1 - c, 0, keepdims=False), 1)
    lines_up = (row_w, chips, 1, FF // chips // 2)
    up_final = ordered(c, up_mine.reshape(lines_up), up_theirs.reshape(lines_up), 2)
    edges = [i * row_w for i in range(5)]
    small_out = [small_sum[a:b] for a, b in zip(edges[:4], edges[1:])]
    return (
        out_stack,
        grad_stack,
        small_out[0],
        small_out[1],
        sum_attn[:, : 3 * D],
        sum_attn[:, 3 * D :],
        small_out[2],
        small_out[3],
        up_final.reshape(row_w, FF),
        small_sum[4 * row_w : 4 * row_w + row_f],
        sum_down,
    )


def solution(mesh):
    rows = P(None, "rows", "pair", None, None)
    line = P(("pair", "rows"))
    flat = P(("pair", "rows"), None)
    lens = P(None, "rows", None)
    return jax.shard_map(
        shards,
        mesh=mesh,
        in_specs=(rows, rows, lens, lens, lens, line, line, flat, flat, line, line, flat, line, flat),
        out_specs=(rows, rows, line, line, flat, flat, line, line, flat, line, flat),
        check_vma=False,
    )
```

```python
import functools

import jax
import jax.numpy as jnp
from jax import lax
from jax.experimental import pallas as pl
from jax.experimental.pallas import tpu as pltpu
from jax.sharding import PartitionSpec as P

D = 1024
HEADS = 16
HEAD = 64
FF = 4096
ROW = 256
MICRO = 2
BF = jnp.bfloat16
F32 = jnp.float32
NEG = -1e30


def position():
    row = lax.axis_index("rows")
    return lax.axis_index("pair"), row // 4, (row // 2) % 2, row % 2


def depth():
    return lax.axis_size("rows") // 4


def swap(block, way):
    if way == "y":
        return lax.ppermute(block, "pair", [(i, i ^ 1) for i in range(2)])
    count = lax.axis_size("rows")
    return lax.ppermute(block, "rows", [(i, i ^ way) for i in range(count)])


def after(block, *others):
    return lax.optimization_barrier((block, *others))[0]


class Chain:
    def __init__(self):
        self.last = None

    def __call__(self, step, *args):
        if self.last is not None:
            args, _ = lax.optimization_barrier((args, self.last))
        out = step(*args)
        self.last = out
        return out


def z_groups():
    count = lax.axis_size("rows")
    return [[z * 4 + low for z in range(count // 4)] for low in range(4)]


def z_gather(block):
    return lax.all_gather(block, "rows", axis_index_groups=z_groups())


def z_scatter(column):
    return lax.psum_scatter(column, "rows", scatter_dimension=0, axis_index_groups=z_groups())


class Gather:
    def __init__(self, chain, by_permutes):
        self.chain = chain
        self.rel_z = by_permutes and depth() == 4

    def over_z(self, block, *first):
        block = after(block, *first)
        if self.rel_z:
            self.column = [block[None]] + [swap(block[None], 4 * k) for k in range(1, 4)]
            return self.column[1:]
        self.column = [z_gather(block)]
        return self.column

    def one(self, *first, extras=()):
        half = depth() // 2

        def halves(column, extras):
            if self.rel_z:
                left, right = jnp.concatenate(column[:2], 0), jnp.concatenate(column[2:], 0)
            else:
                left, right = column[0][:half], column[0][half:]
            return beside((left, right), extras)

        self.halves = self.chain(halves, self.column, extras)
        return self.send(*first)

    def one_halves(self):
        half = depth() // 2
        self.halves = self.chain(lambda v: (v[:half], v[half:]), self.column[0])

    def send(self, *first):
        left, right = lax.optimization_barrier((self.halves, first))[0]
        self.sides = swap(left, 2), swap(right, "y")
        return list(self.sides)

    def two(self, *first, extras=()):
        rows, cols = self.column[0].shape[-2:]
        block = (depth() // 2, rows, cols)

        def planes(halves, sides):
            left, right = halves
            left_x, right_y = sides
            if not extras:
                return jnp.concatenate([left, left_x], 0), jnp.concatenate([right, right_y], 0)
            main = [v[:, :cols].reshape(block) for v in (left, left_x, right, right_y)]
            more = [v[:, cols:].reshape(extras) for v in (left, left_x, right, right_y)]
            return (
                jnp.concatenate(main[:2], 0),
                jnp.concatenate(main[2:], 0),
                jnp.stack(more, 0),
            )

        sides = lax.optimization_barrier((self.sides, first))[0]
        self.planes = self.chain(planes, self.halves, sides)
        left, right = self.planes[:2]
        left_y, right_x = swap(left, "y"), swap(right, 2)
        half = depth() // 2
        low, high = range(half), range(half, 2 * half)
        self.pieces = [
            (left, [(0, i, 0) for i in low] + [(0, i, 1) for i in low]),
            (left_y, [(1, i, 0) for i in low] + [(1, i, 1) for i in low]),
            (right, [(0, i, 0) for i in high] + [(1, i, 0) for i in high]),
            (right_x, [(0, i, 1) for i in high] + [(1, i, 1) for i in high]),
        ]
        return [left_y, right_x]


def beside(blocks, extras):
    if not extras:
        return tuple(blocks)
    out = []
    for block, extra in zip(blocks, extras):
        rows = block.shape[0] * block.shape[1]
        out.append(
            jnp.concatenate([block.reshape(rows, -1), extra.reshape(rows, -1)], 1)
        )
    return tuple(out)


class GatherXZY:
    def __init__(self, chain):
        self.chain = chain

    def over_z(self, lines, *first):
        self.column = z_gather(after(lines, *first))
        return self.column

    def two(self, *first):
        def cut(column):
            shape = (2 * depth(), *column.shape[2:])
            return column[:, :2].reshape(shape), column[:, 2:].reshape(shape)

        upper, lower = self.chain(cut, after(self.column, *first))
        upper_y, lower_x = swap(upper, "y"), swap(lower, 2)
        ids = range(depth())
        self.pieces = [
            (upper, [(0, i, j) for i in ids for j in range(2)]),
            (upper_y, [(1, i, j) for i in ids for j in range(2)]),
            (lower, [(j, i, 0) for i in ids for j in range(2)]),
            (lower_x, [(j, i, 1) for i in ids for j in range(2)]),
        ]
        return [upper_y, lower_x]


def chip_slot(chip, where, rel_z):
    jy, jz, jx = chip
    y, z, x, _ = where
    z_at = (z ^ jz) if rel_z else jz
    return ((y ^ jy) * depth() + z_at) * 2 + (x ^ jx)


def layout_yzx():
    ids = range(depth())
    return [
        [(1, i, j) for i in ids for j in range(2)],
        [(0, i, j) for i in ids for j in range(2)],
        [(j, i, 1) for i in ids for j in range(2)],
        [(j, i, 0) for i in ids for j in range(2)],
    ]


def layout_yxz():
    half = depth() // 2
    low, high = range(half), range(half, 2 * half)
    return [
        [(1, i, j) for j in range(2) for i in low],
        [(0, i, j) for j in range(2) for i in low],
        [(j, i, 1) for j in range(2) for i in high],
        [(j, i, 0) for j in range(2) for i in high],
    ]


def plus(left, right):
    return (left.astype(F32) + right.astype(F32)).astype(left.dtype)


class Scatter:
    def __init__(self, chain, by_permutes):
        self.chain = chain
        self.rel_z = by_permutes and depth() == 4

    def one(self, parts, *first):
        self.parts = parts
        left, _, right, _ = parts
        self.sides = swap(after(left, *first), "y"), swap(after(right, *first), 2)
        return list(self.sides)

    def two(self, *first, extras=()):
        half = depth() // 2

        def add(left, left_in, right, right_in, extras):
            send = (plus(left[half:], left_in[half:]), plus(right[half:], right_in[half:]))
            return (
                *beside(send, extras),
                plus(left[:half], left_in[:half]),
                plus(right[:half], right_in[:half]),
            )

        _, left, _, right = self.parts
        left_in, right_in = lax.optimization_barrier((self.sides, first))[0]
        self.sums = self.chain(add, left, left_in, right, right_in, extras)
        self.ends = swap(self.sums[0], 2), swap(self.sums[1], "y")
        return list(self.ends)

    def over_z(self, *first):
        _, _, left, right = self.sums
        left_in, right_in = self.ends

        def add(left, left_in, right, right_in):
            left_in, right_in = (
                v if v.ndim == 3 else v[:, : left.shape[2]].reshape(left.shape)
                for v in (left_in, right_in)
            )
            if self.rel_z:
                return (
                    plus(left[1], left_in[1]),
                    *plus(right, right_in),
                    left[0].astype(F32) + left_in[0].astype(F32),
                )
            return jnp.concatenate([plus(left, left_in), plus(right, right_in)], 0)

        made = self.chain(add, left, left_in, right, right_in)
        if not self.rel_z:
            return z_scatter(after(made, *first))
        one, two, three, own = made
        return own, swap(one, 4), swap(two, 8), swap(three, 12)

    def total(self, parts):
        if not self.rel_z:
            return parts.astype(F32)
        own, *arrived = parts

        def add(own, *arrived):
            for part in arrived:
                own = own + part.astype(F32)
            return own

        return self.chain(add, own, *arrived)


class ScatterYZX:
    def __init__(self, chain):
        self.chain = chain

    def one(self, parts, *first):
        self.parts = parts
        left, _, right, _ = parts
        self.sides = swap(after(left, *first), "y"), swap(after(right, *first), 2)
        return list(self.sides)

    def over_z(self, *first):
        def add(left, left_in, right, right_in):
            shape = (depth(), 2, *left.shape[1:])
            upper, lower = plus(left, left_in).reshape(shape), plus(right, right_in).reshape(shape)
            return jnp.concatenate([upper, lower], 1)

        _, left, _, right = self.parts
        self.lines = z_scatter(self.chain(add, left, self.sides[0], right, self.sides[1]))
        return self.lines

    def last(self):
        def cut(lines):
            lines = lines.reshape(4, *lines.shape[-2:])
            return lines[1], lines[3], lines[0], lines[2]

        return self.chain(cut, self.lines)


def ordered(flag, own, other, axis):
    return jnp.where(
        flag == 0,
        jnp.concatenate([own, other], axis),
        jnp.concatenate([other, own], axis),
    )


def frames(index, phone, prompt, target, segs):
    pre_end = ends_of([phone[s] + prompt[s] for s in range(segs)])
    tgt_end = ends_of([target[s] for s in range(segs)])
    is_target = index >= ROW
    local = jnp.where(is_target, index - ROW, index)
    seg = jnp.zeros_like(index)
    for s in range(segs):
        edge = jnp.where(is_target, tgt_end[s], pre_end[s])
        seg = seg + jnp.where(local >= edge, 1, 0)
    start = jnp.zeros_like(index)
    phones = jnp.zeros_like(index)
    prompts = jnp.zeros_like(index)
    for s in range(segs):
        pick = seg == s
        pre_start = pre_end[s] - phone[s] - prompt[s]
        tgt_start = tgt_end[s] - target[s]
        start = jnp.where(pick, jnp.where(is_target, tgt_start, pre_start), start)
        phones = jnp.where(pick, phone[s], phones)
        prompts = jnp.where(pick, prompt[s], prompts)
    off = local - start
    is_phone = jnp.where(is_target, 0, jnp.where(off < phones, 1, 0))
    pos = jnp.where(is_target, prompts + off, off - phones)
    return seg, is_phone, pos


def ends_of(lengths):
    out, total = [], 0
    for length in lengths:
        total = total + length
        out.append(total)
    return out


def bias_of(query, key):
    q_seg, q_phone, q_pos = query
    k_seg, k_phone, k_pos = key
    audio = (k_phone == 1) | (k_pos <= q_pos)
    good = (q_seg == k_seg) & (((q_phone == 1) & (k_phone == 1)) | ((q_phone == 0) & audio))
    return jnp.where(good, 0.0, NEG)


def bdot(left, right, dims):
    return lax.dot_general(left, right, (dims, ((), ())), preferred_element_type=F32)


NT = ((1,), (1,))
NN = ((1,), (0,))
TN = ((0,), (0,))


def attention_forward(qkv, phone, prompt, target):
    segs = phone.shape[0]
    group = 2

    def kernel(phone_ref, prompt_ref, target_ref, q_ref, k_ref, v_ref, out_ref, bias_ref):
        @pl.when(pl.program_id(0) == 0)
        def _():
            ph = [phone_ref[s] for s in range(segs)]
            pr = [prompt_ref[s] for s in range(segs)]
            tg = [target_ref[s] for s in range(segs)]
            rows = lax.broadcasted_iota(jnp.int32, (2 * ROW, 1), 0)
            cols = lax.broadcasted_iota(jnp.int32, (1, 2 * ROW), 1)
            bias_ref[...] = bias_of(
                frames(cols, ph, pr, tg, segs), frames(rows, ph, pr, tg, segs)
            )

        lane = lax.broadcasted_iota(jnp.int32, (1, 2 * HEAD), 1)
        zero = jnp.zeros((), BF)
        scale = jnp.asarray(HEAD**-0.5, BF)
        for pair in range(group):
            cols = slice(pair * 2 * HEAD, (pair + 1) * 2 * HEAD)
            for rows, keys in ((0, ROW), (ROW, 2 * ROW)):
                at = slice(rows, rows + ROW)
                outs = []
                for j in range(2):
                    q = jnp.where((lane // HEAD) == j, q_ref[at, cols] * scale, zero)
                    s = bdot(k_ref[:keys, cols], q, NT) + bias_ref[:keys, at]
                    e = jnp.exp(s - jnp.max(s, 0, keepdims=True))
                    p = (e * (1.0 / jnp.sum(e, 0, keepdims=True))).astype(BF)
                    outs.append(bdot(v_ref[:keys, cols], p, TN)[j * HEAD : (j + 1) * HEAD])
                out_ref[at, cols] = jnp.transpose(jnp.concatenate(outs, 0)).astype(BF)

    steps = HEADS // 2 // group
    smem = pl.BlockSpec(memory_space=pltpu.SMEM)
    part = (2 * ROW, 2 * HEAD * group)
    return pl.pallas_call(
        kernel,
        grid=(steps,),
        out_shape=jax.ShapeDtypeStruct((2 * ROW, D), BF),
        in_specs=[
            smem,
            smem,
            smem,
            pl.BlockSpec(part, lambda h: (0, h)),
            pl.BlockSpec(part, lambda h: (0, h + steps)),
            pl.BlockSpec(part, lambda h: (0, h + 2 * steps)),
        ],
        out_specs=pl.BlockSpec(part, lambda h: (0, h)),
        scratch_shapes=[pltpu.VMEM((2 * ROW, 2 * ROW), F32)],
        compiler_params=pltpu.CompilerParams(vmem_limit_bytes=16 << 20),
        cost_estimate=pl.CostEstimate(flops=1 << 20, bytes_accessed=1 << 10, transcendentals=0),
        name="attention_forward",
    )(phone, prompt, target, qkv, qkv, qkv)


def attention_backward(qkv, grad_mixed, phone, prompt, target):
    segs = phone.shape[0]
    group = 2

    def kernel(
        phone_ref, prompt_ref, target_ref, q_ref, k_ref, v_ref, g_ref, out_ref, bias_ref
    ):
        @pl.when(pl.program_id(0) == 0)
        def _():
            ph = [phone_ref[s] for s in range(segs)]
            pr = [prompt_ref[s] for s in range(segs)]
            tg = [target_ref[s] for s in range(segs)]
            rows = lax.broadcasted_iota(jnp.int32, (2 * ROW, 1), 0)
            cols = lax.broadcasted_iota(jnp.int32, (1, 2 * ROW), 1)
            bias_ref[...] = bias_of(
                frames(cols, ph, pr, tg, segs), frames(rows, ph, pr, tg, segs)
            )

        lane = lax.broadcasted_iota(jnp.int32, (1, 2 * HEAD), 1)
        zero = jnp.zeros((), BF)
        scale = HEAD**-0.5
        for pair in range(group):
            cols = slice(pair * 2 * HEAD, (pair + 1) * 2 * HEAD)
            dks, dvs = {}, {}
            for rows, keys in ((0, ROW), (ROW, 2 * ROW)):
                at = slice(rows, rows + ROW)
                dqs = []
                for j in range(2):
                    sel = (lane // HEAD) == j
                    q_all, g_all = q_ref[at, cols], g_ref[at, cols]
                    q = jnp.where(sel, q_all * jnp.asarray(scale, BF), zero)
                    g = jnp.where(sel, g_all, zero)
                    k, v = k_ref[:keys, cols], v_ref[:keys, cols]
                    s = bdot(k, q, NT) + bias_ref[:keys, at]
                    dp = bdot(v, g, NT)
                    e = jnp.exp(s - jnp.max(s, 0, keepdims=True))
                    p = e * (1.0 / jnp.sum(e, 0, keepdims=True))
                    inner = jnp.sum(dp * p, 0, keepdims=True)
                    ds = (p * (dp - inner)).astype(BF)
                    dvs[rows, j] = bdot(p.astype(BF), g_all, NN)
                    dks[rows, j] = bdot(ds, q_all, NN)
                    dqs.append(bdot(k, ds, TN)[j * HEAD : (j + 1) * HEAD])
                dq = jnp.transpose(jnp.concatenate(dqs, 0)) * scale
                out_ref[0, at, cols] = dq.astype(BF)
            low = lane < HEAD
            for place, part, factor in ((1, dks, scale), (2, dvs, 1.0)):
                early = jnp.where(low, part[0, 0], part[0, 1])
                late = jnp.where(low, part[ROW, 0], part[ROW, 1])
                out_ref[place, :ROW, cols] = ((early + late[:ROW]) * factor).astype(BF)
                out_ref[place, ROW:, cols] = (late[ROW:] * factor).astype(BF)

    steps = HEADS // 2 // group
    smem = pl.BlockSpec(memory_space=pltpu.SMEM)
    block = (2 * ROW, 2 * HEAD * group)
    return pl.pallas_call(
        kernel,
        grid=(steps,),
        out_shape=jax.ShapeDtypeStruct((3, 2 * ROW, D), BF),
        in_specs=[
            smem,
            smem,
            smem,
            pl.BlockSpec(block, lambda h: (0, h)),
            pl.BlockSpec(block, lambda h: (0, h + steps)),
            pl.BlockSpec(block, lambda h: (0, h + 2 * steps)),
            pl.BlockSpec(block, lambda h: (0, h)),
        ],
        out_specs=pl.BlockSpec((3, *block), lambda h: (0, 0, h)),
        scratch_shapes=[pltpu.VMEM((2 * ROW, 2 * ROW), F32)],
        compiler_params=pltpu.CompilerParams(vmem_limit_bytes=16 << 20),
        cost_estimate=pl.CostEstimate(flops=1 << 20, bytes_accessed=1 << 10, transcendentals=0),
        name="attention_backward",
    )(phone, prompt, target, qkv, qkv, qkv, grad_mixed)


VMEM = pl.BlockSpec(memory_space=pltpu.VMEM)
SMEM = pl.BlockSpec(memory_space=pltpu.SMEM)
ANY = pl.BlockSpec(memory_space=pl.ANY)


def shape_of(shape, dtype=BF):
    return jax.ShapeDtypeStruct(shape, dtype)


def call(name, kernel, outs, args, specs=None, scratch=(), megabytes=12, long=False):
    return pl.pallas_call(
        kernel,
        out_shape=outs,
        in_specs=[VMEM] * len(args) if specs is None else specs,
        out_specs=[VMEM] * len(outs),
        scratch_shapes=list(scratch),
        compiler_params=pltpu.CompilerParams(vmem_limit_bytes=megabytes << 20),
        cost_estimate=pl.CostEstimate(
            flops=1 << (35 if long else 20), bytes_accessed=1 << 10, transcendentals=0
        ),
        name=name,
    )(*args)


def block(ref, slot, size):
    return ref[:, pl.ds(pl.multiple_of(slot * size, size), size)]


def pack(w_qkv, w_out, vectors):
    rows = w_qkv.shape[0]
    sizes = [v.shape[0] for v in vectors]
    wide = max(sizes)
    table = jnp.stack([jnp.pad(v, (0, wide - v.shape[0])) for v in vectors], 0)

    def kernel(table_ref, qkv_ref, out_ref, to, sems):
        copies = [
            pltpu.make_async_copy(qkv_ref, to.at[:, pl.ds(0, 3 * D)], sems.at[0]),
            pltpu.make_async_copy(out_ref, to.at[:, pl.ds(3 * D, D)], sems.at[1]),
        ]
        for copy in copies:
            copy.start()
        row = lax.broadcasted_iota(jnp.int32, (rows, wide), 0)
        column = lax.broadcasted_iota(jnp.int32, (rows, wide), 1)
        lane = lax.broadcasted_iota(jnp.int32, (rows, 128), 1)
        total, place = jnp.zeros((rows, 128), F32), 0
        for n, size in enumerate(sizes):
            value = table_ref[n : n + 1, :].astype(F32)
            for start in range(0, size, rows):
                picked = jnp.sum(jnp.where(column == row + start, value, 0.0), 1, keepdims=True)
                total = total + jnp.where(lane == place, picked, 0.0)
                place += 1
        to[:, 4 * D :] = total.astype(BF)
        for copy in copies:
            copy.wait()

    return call(
        "pack",
        kernel,
        [shape_of((rows, 4 * D + 128))],
        (table, w_qkv, w_out),
        [VMEM, ANY, ANY],
        [pltpu.SemaphoreType.DMA((2,))],
    )[0]


def unpack(own, other, rel_z, count):
    chips, rows = 4 * depth(), own[0][0].shape[1]
    flat = [(core, p) for core, part in enumerate((own, other)) for p in part]
    arrays = [p[0] for _, p in flat]
    cuts = [(0, 3 * D), (3 * D, D), (4 * D, 128)]

    def kernel(*refs):
        ins = refs[: len(arrays)]
        qkv_ref, out_ref, vec_ref, small_ref, sems = refs[len(arrays) :]
        where = position()
        copies = []
        for n in (2, 0, 1):
            to = (qkv_ref, out_ref, small_ref)[n]
            start, width = cuts[n]
            for ref, (core, (_, names)) in zip(ins, flat):
                at = where[3] ^ core
                for i, name in enumerate(names):
                    copy = pltpu.make_async_copy(
                        ref.at[i, :, pl.ds(start, width)],
                        to.at[chip_slot(name, where, rel_z), at],
                        sems.at[len(copies)],
                    )
                    copy.start()
                    copies.append(copy)
        for copy in copies[: len(copies) // 3]:
            copy.wait()
        small = small_ref[...].reshape(2 * chips * rows, 128).astype(F32)
        vec_ref[...] = jnp.transpose(small)[:count]
        for copy in copies[len(copies) // 3 :]:
            copy.wait()

    shapes = [(chips, 2, rows, w) for _, w in cuts]
    qkv, out, vec = call(
        "unpack",
        kernel,
        [shape_of(shapes[0]), shape_of(shapes[1]), shape_of((count, D), F32)],
        arrays,
        [ANY] * len(arrays),
        [pltpu.VMEM(shapes[2], BF), pltpu.SemaphoreType.DMA((6 * chips,))],
    )
    return qkv.reshape(D, 3 * D), out.reshape(D, D), vec


def normal_of(values):
    center = values - jnp.mean(values, -1, keepdims=True)
    inv = lax.rsqrt(jnp.mean(center * center, -1, keepdims=True) + 1e-05)
    return center * inv, inv


def norm_back(grad, normal, inv, gain):
    e = grad * gain
    return inv * (
        e - jnp.mean(e, -1, keepdims=True) - normal * jnp.mean(e * normal, -1, keepdims=True)
    )


def project(resident, vec, weight):
    def kernel(x_ref, vec_ref, w_ref, normed_ref, qkv_ref):
        for r in range(0, 2 * ROW, ROW):
            normal, _ = normal_of(x_ref[r : r + ROW, :].astype(F32))
            normed_ref[r : r + ROW, :] = (normal * vec_ref[0:1, :] + vec_ref[1:2, :]).astype(BF)
        for n in range(0, 3 * D, 512):
            qkv_ref[:, n : n + 512] = bdot(normed_ref[...], w_ref[:, n : n + 512], NN).astype(BF)

    outs = [shape_of((2 * ROW, D)), shape_of((2 * ROW, 3 * D))]
    return call("project", kernel, outs, (resident, vec, weight))


def attend(mixed, weight, resident, vec):
    def kernel(m_ref, w_ref, x_ref, vec_ref, normed_ref, hidden_ref):
        for r in range(0, 2 * ROW, ROW):
            rows = slice(r, r + ROW)
            hidden = x_ref[rows, :].astype(F32) + bdot(m_ref[rows, :], w_ref[...], NN)
            hidden_ref[rows, :] = hidden
            normal, _ = normal_of(hidden)
            normed_ref[rows, :] = (normal * vec_ref[2:3, :] + vec_ref[3:4, :]).astype(BF)

    outs = [shape_of((2 * ROW, D)), shape_of((2 * ROW, D), F32)]
    return call("attend", kernel, outs, (mixed, weight, resident, vec))


def gelu_both(v):
    c = (2.0 / jnp.pi) ** 0.5
    square = v * v
    t = jnp.tanh(v * (c + (c * 0.044715) * square))
    half = 0.5 + 0.5 * t
    return v * half, half + 0.5 * v * (1.0 - t * t) * (c + (3 * c * 0.044715) * square)


def feed_step(n_ref, w_ref, shift_ref, act_ref, slope_ref, start, size):
    cols = slice(start, start + size)
    pre = bdot(n_ref[...], w_ref[:, cols], NN) + shift_ref[:, cols]
    act, slope = gelu_both(pre)
    act_ref[:, cols] = act.astype(BF)
    slope_ref[:, cols] = slope.astype(BF)


def feed_first(normed, pieces, shift):
    chips, (rows, wide) = 4 * depth(), pieces[0][0].shape[1:]
    arrays = [p[0] for p in pieces]
    size = 512

    def kernel(n_ref, shift_ref, *refs):
        ins = refs[: len(arrays)]
        act_ref, slope_ref, w_ref, sems = refs[len(arrays) :]
        where = position()
        copies = []
        for start in range(0, wide, size):
            for ref, (_, names) in zip(ins, pieces):
                for i, name in enumerate(names):
                    to = pl.multiple_of(chip_slot(name, where, False) * rows, rows)
                    copy = pltpu.make_async_copy(
                        ref.at[i, :, pl.ds(start, size)],
                        w_ref.at[pl.ds(to, rows), pl.ds(start, size)],
                        sems.at[len(copies)],
                    )
                    copy.start()
                    copies.append(copy)
        for n, start in enumerate(range(0, wide, size)):
            for copy in copies[n * chips : (n + 1) * chips]:
                copy.wait()
            feed_step(n_ref, w_ref, shift_ref, act_ref, slope_ref, start, size)

    part = shape_of((2 * ROW, wide))
    return call(
        "feed_first",
        kernel,
        [part, part, shape_of((chips * rows, wide))],
        (normed, shift, *arrays),
        [VMEM, VMEM] + [ANY] * len(arrays),
        [pltpu.SemaphoreType.DMA((chips * (wide // size),))],
        long=True,
    )


def feed_second(normed, weight, shift):
    def kernel(n_ref, w_ref, shift_ref, act_ref, slope_ref):
        for start in range(0, weight.shape[1], 512):
            feed_step(n_ref, w_ref, shift_ref, act_ref, slope_ref, start, 512)

    part = shape_of((2 * ROW, weight.shape[1]))
    return call("feed_second", kernel, [part, part], (normed, weight, shift))


def down_grad(acts, cts):
    lists = layout_yzx()
    chips = 4 * depth()
    size = acts[0].shape[1] // chips
    half = size // 2
    group = 4

    def kernel(a0, a1, c0, c1, *outs):
        where = position()
        for jy in range(2):
            for jx in range(2):
                for z in range(0, depth(), group):
                    names = [(jy, z + i, jx) for i in range(group)]
                    slots = [chip_slot(name, where, False) for name in names]
                    total = 0.0
                    for a, ct in ((a0, c0), (a1, c1)):
                        left = jnp.concatenate([block(a, slot, size) for slot in slots], 1)
                        total = total + bdot(left, ct[...], TN)
                    total = total.astype(BF).reshape(group, size, D)
                    for i, name in enumerate(names):
                        upper, lower = outs[1 - jy], outs[3 - jx]
                        upper[lists[1 - jy].index(name)] = total[i, :half]
                        lower[lists[3 - jx].index(name)] = total[i, half:]

    outs = [shape_of((len(v), half, D)) for v in lists]
    return call("down_grad", kernel, outs, (*acts, *cts))


def back_act(cts, pieces, slopes):
    wide = slopes[0].shape[1]
    chips = 4 * depth()
    size = wide // chips
    arrays = [p[0] for p in pieces]
    half = size // 2
    wave = chips // 2

    def kernel(c0, c1, s0, s1, *refs):
        ins, (g0, g1, sum_ref, w_ref, sems) = refs[: len(arrays)], refs[len(arrays) :]
        where = position()

        def copy_of(n, i):
            name = pieces[n][1][i]
            row = pl.multiple_of(chip_slot(name, where, False) * size + (n // 2) * half, half)
            return pltpu.make_async_copy(
                ins[n].at[i], w_ref.at[pl.ds(row, half), :], sems.at[n * wave + i]
            )

        waves = [[], []]
        for n in range(4):
            for i, (jy, _, _) in enumerate(pieces[n][1]):
                copy = copy_of(n, i)
                copy.start()
                waves[jy].append(copy)
        for jy in range(2):
            for copy in waves[jy]:
                copy.wait()
            for j in range(0, wave * size, 256):
                start = pl.multiple_of((where[0] ^ jy) * (wave * size) + j, 256)
                at = pl.ds(start, 256)
                sums = 0.0
                for ct, slope, out in ((c0, s0, g0), (c1, s1, g1)):
                    grad = bdot(ct[...], w_ref[at, :], NT) * slope[:, at].astype(F32)
                    grad = grad.astype(BF)
                    sums = sums + jnp.sum(grad.astype(F32), 0, keepdims=True)
                    out[:, at] = grad
                sum_ref[:, at] = sums

    part = shape_of((2 * ROW, wide))
    return call(
        "back_act",
        kernel,
        [part, part, shape_of((1, wide), F32), shape_of((wide, D))],
        (*cts, *slopes, *arrays),
        [VMEM] * 4 + [ANY] * 4,
        [pltpu.SemaphoreType.DMA((4 * wave,))],
    )


def back_up(grad, weight, dtype):
    def kernel(g_ref, w_ref, out_ref):
        for n in range(0, D, 256):
            out_ref[:, n : n + 256] = bdot(g_ref[...], w_ref[n : n + 256, :], NT).astype(dtype)

    outs = [shape_of((2 * ROW, D), dtype)]
    return call("back_up", kernel, outs, (grad, weight), long=dtype == F32)[0]


def up_grad(normeds, grads, out_own, out_in):
    lists = layout_yxz()
    half, wide = depth() // 2, grads[0].shape[1]
    rows = D // (4 * depth())
    extra = rows // 4

    def kernel(n0, n1, g0, g1, a_ref, b_ref, *outs_and_scratch):
        outs, part_ref = outs_and_scratch[:4], outs_and_scratch[4]
        where = position()
        for out, names in zip(outs, lists):
            for i, name in enumerate(names):
                slot = chip_slot(name, where, False)
                total = (a_ref[slot].astype(F32) + b_ref[slot].astype(F32)).astype(BF)
                out[i, rows:, :D] = total[:extra]
                out[i, rows:, D:] = total[extra:]
        for side in range(2):
            for jy in range(2):
                base = (where[0] ^ jy) * depth() + side * half
                for n in range(0, wide, 512):
                    total = 0.0
                    for normed, grad in ((n0, g0), (n1, g1)):
                        left = jnp.concatenate(
                            [block(normed, base + i, 2 * rows) for i in range(half)], 1
                        )
                        total = total + bdot(left, grad[:, n : n + 512], TN)
                    part_ref[:, :, :, n : n + 512] = total.astype(BF).reshape(half, 2, rows, 512)
                for jx in range(2):
                    for i in range(half):
                        if side == 0:
                            out, at = outs[1 - jy], jx * half + i
                        else:
                            out, at = outs[3 - jx], jy * half + i
                        out[at, :rows] = part_ref[i, where[2] ^ jx]

    outs = [shape_of((len(v), rows + extra, wide)) for v in lists]
    scratch = [pltpu.VMEM((half, 2, rows, wide), BF)]
    return call("up_grad", kernel, outs, (*normeds, *grads, out_own, out_in), None, scratch)


def out_grad(mixed, low):
    chips = 4 * depth()
    rows = D // (2 * chips)
    group = 256 // (2 * rows)

    def kernel(m_ref, l_ref, send_ref, keep_ref):
        core = position()[3]
        for g in range(D // 256):
            at, cols = slice(g * group, (g + 1) * group), slice(g * 256, (g + 1) * 256)
            total = bdot(m_ref[:, cols], l_ref[...], TN).astype(BF).reshape(group, 2, rows, D)
            first, second = total[:, 0], total[:, 1]
            send_ref[at] = jnp.where(core == 0, second, first)
            keep_ref[at] = jnp.where(core == 0, first, second)

    outs = [shape_of((chips, rows, D))] * 2
    return call("out_grad", kernel, outs, (mixed, low))


def back_norm(own, other, hidden, vec, ct, weight):
    def kernel(a_ref, b_ref, h_ref, vec_ref, ct_ref, w_ref, mixed_ref, low_ref, grad_ref, sum_ref):
        first, second = 0.0, 0.0
        for r in range(0, 2 * ROW, ROW):
            rows = slice(r, r + ROW)
            normal, inv = normal_of(h_ref[rows, :])
            grad = a_ref[rows, :] + b_ref[rows, :].astype(F32)
            first = first + jnp.sum(grad * normal, 0, keepdims=True)
            second = second + jnp.sum(grad, 0, keepdims=True)
            total = ct_ref[rows, :].astype(F32) + norm_back(grad, normal, inv, vec_ref[2:3, :])
            grad_ref[rows, :] = total
            low_ref[rows, :] = total.astype(BF)
            mixed_ref[rows, :] = bdot(low_ref[rows, :], w_ref[...], NT).astype(BF)
        sum_ref[0:1, :] = first
        sum_ref[1:2, :] = second

    part = shape_of((2 * ROW, D))
    outs = [part, part, shape_of((2 * ROW, D), F32), shape_of((2, D), F32)]
    return call("back_norm", kernel, outs, (own, other, hidden, vec, ct, weight))


def attn_grad(normed, grads):
    chips = 4 * depth()
    rows = D // (2 * chips)
    group = 256 // (2 * rows)

    def kernel(n_ref, g_ref, send_ref, keep_ref):
        core = position()[3]
        for g in range(D // 256):
            at, cols = slice(g * group, (g + 1) * group), slice(g * 256, (g + 1) * 256)
            for part in range(3):
                total = bdot(n_ref[:, cols], g_ref[part], TN).astype(BF)
                total = total.reshape(group, 2, rows, D)
                first, second = total[:, 0], total[:, 1]
                to = slice(part * D, (part + 1) * D)
                send_ref[at, :, to] = jnp.where(core == 0, second, first)
                keep_ref[at, :, to] = jnp.where(core == 0, first, second)

    outs = [shape_of((chips, rows, 3 * D))] * 2
    return call("attn_grad", kernel, outs, (normed, grads))


def core_sum(own, arrived, sums, sums_in, rel_z):
    lists = layout_yxz()
    chips, rows, wide = own.shape
    lines = sums.shape[0]

    def kernel(a_ref, b_ref, s_ref, t_ref, *rest):
        outs, pad_ref, small_ref = rest[:4], rest[4], rest[5]
        where = position()
        pad_ref[...] = jnp.zeros_like(pad_ref)
        pad_ref[:lines, :] = s_ref[...] + t_ref[...]
        small_ref[...] = jnp.transpose(pad_ref[...]).astype(BF).reshape(chips, 2, rows, 128)
        for out, names in zip(outs, lists):
            for i, name in enumerate(names):
                slot = chip_slot(name, where, rel_z)
                total = a_ref[slot].astype(F32) + b_ref[slot].astype(F32)
                out[i, :, :wide] = total.astype(BF)
                out[i, :, wide:] = small_ref[slot, where[3]]

    outs = [shape_of((len(v), rows, wide + 128)) for v in lists]
    scratch = [pltpu.VMEM((128, D), F32), pltpu.VMEM((chips, 2, rows, 128), BF)]
    return call("core_sum", kernel, outs, (own, arrived, sums, sums_in), None, scratch)


def back_first(grads, weight, resident, vec, hidden_grad):
    def kernel(g_ref, w_ref, x_ref, vec_ref, h_ref, out_ref, sum_ref):
        first, second = 0.0, 0.0
        for half in range(2):
            rows = slice(half * ROW, (half + 1) * ROW)
            normal, inv = normal_of(x_ref[rows, :].astype(F32))
            grad = 0.0
            for part in range(3):
                grad = grad + bdot(g_ref[part, rows, :], w_ref[:, part * D : (part + 1) * D], NT)
            first = first + jnp.sum(grad * normal, 0, keepdims=True)
            second = second + jnp.sum(grad, 0, keepdims=True)
            total = h_ref[rows, :] + norm_back(grad, normal, inv, vec_ref[0:1, :])
            out_ref[half] = total.astype(BF)
        sum_ref[0:1, :] = first
        sum_ref[1:2, :] = second

    outs = [shape_of((2, ROW, D)), shape_of((2, D), F32)]
    args = (grads, weight, resident, vec, hidden_grad)
    return call("back_first", kernel, outs, args, long=True)


def down_back(act, weight, dtype, hidden=None, late=None):
    extra = tuple(v for v in (hidden, late) if v is not None)

    def kernel(a_ref, w_ref, *refs):
        out_ref = refs[-1]
        for n in range(0, D, 256):
            total = bdot(a_ref[...], w_ref[:, n : n + 256], NN)
            if hidden is not None:
                total = total + refs[0][:, n : n + 256]
            out_ref[:, n : n + 256] = total.astype(dtype)

    return call("down_back", kernel, [shape_of((2 * ROW, D), dtype)], (act, weight, *extra))[0]


def interleave(own, other):
    rows, wide = own.shape
    size = wide // (4 * depth())

    def kernel(a_ref, b_ref, out_ref):
        core = position()[3]
        for n in range(wide // size):
            cols = slice(n * size, (n + 1) * size)
            for ref, at in ((a_ref, core), (b_ref, 1 - core)):
                to = pl.multiple_of((2 * n + at) * size, size)
                out_ref[:, pl.ds(to, size)] = ref[:, cols]

    return call("interleave", kernel, [shape_of((rows, 2 * wide), F32)], (own, other))[0]


def shards(
    inputs,
    cotangent,
    phone_len,
    prompt_len,
    target_len,
    ln1_gain,
    ln1_bias,
    w_qkv,
    w_out,
    ln2_gain,
    ln2_bias,
    w_up,
    up_bias,
    w_down,
):
    y, z, x, c = position()
    count = depth()
    chips = 4 * count
    row_w = w_qkv.shape[0]
    row_f = w_down.shape[0]

    chain = Chain()

    def split_halves(blocks):
        return (
            lax.dynamic_index_in_dim(blocks, 1 - y, 0, keepdims=False),
            lax.dynamic_index_in_dim(blocks, y, 0, keepdims=False),
        )

    attn_g, up_g, down_g = Gather(chain, True), Gather(chain, False), GatherXZY(chain)
    down_s, up_s, attn_s = ScatterYZX(chain), Scatter(chain, False), Scatter(chain, True)

    vectors = (ln1_gain, ln1_bias, ln2_gain, ln2_bias, up_bias)
    attn_z = attn_g.over_z(chain(pack, w_qkv, w_out, vectors))
    def split_both(inputs, cotangent):
        x_send, x_own = split_halves(inputs)
        ct_send, ct_own = split_halves(cotangent)
        return jnp.stack([x_send, ct_send], 0), x_own, ct_own

    both_send, x_own, ct_own = chain(split_both, inputs[:, 0, 0], cotangent[:, 0, 0])
    both_other = swap(both_send, "y")
    lengths = tuple(
        lax.dynamic_index_in_dim(v, y, 0, keepdims=False)[0]
        for v in (phone_len, prompt_len, target_len)
    )

    def split_up(w_up):
        split = w_up.reshape(row_w, chips, 2, FF // chips // 2)
        return tuple(
            lax.dynamic_index_in_dim(split, i, 2, keepdims=False).reshape(row_w, FF // 2)
            for i in (1 - c, c)
        )

    up_send, up_own = chain(split_up, w_up)
    up_other = swap(up_send, 1)
    up_shard = chain(lambda own, other: ordered(c, own, other, 0), up_own, up_other)
    half_f = row_f // 2

    def join_both(x_own, ct_own, other):
        return ordered(y, x_own, other[0], 0), ordered(y, ct_own, other[1], 0)

    resident, grad_result = chain(join_both, x_own, ct_own, both_other)
    attn_one = attn_g.one(extras=(w_down[:half_f], w_down[half_f:]))
    up_z = up_g.over_z(up_shard, *attn_z)


    attn_two = attn_g.two(extras=(half_f, D))
    early = [(swap(array, 1), rels) for array, rels in attn_g.pieces[::2]]
    down_z = down_g.over_z(attn_g.planes[2], *up_z)
    up_g.one_halves()
    late = [(swap(after(array, *up_g.halves), 1), rels) for array, rels in attn_g.pieces[1::2]]
    up_one = up_g.send(*[v[0] for v in early + late])
    lines = 4 + row_f // row_w
    attn_core = early + late
    many = len(attn_core)

    def unpack_pieces(*arrays):
        own = [(a, p[1]) for a, p in zip(arrays[:many], attn_g.pieces)]
        other = [(a, p[1]) for a, p in zip(arrays[many:], attn_core)]
        return unpack(own, other, attn_g.rel_z, lines)

    qkv_weight, out_weight, vec = chain(
        unpack_pieces, *[p[0] for p in attn_g.pieces + attn_core]
    )
    shift = vec[4:].reshape(row_f // row_w, chips, 2, row_w)
    shift = lax.dynamic_index_in_dim(shift, c, 2, keepdims=False)
    shift = shift.transpose(1, 0, 2).reshape(1, FF // 2)

    normed, qkv = chain(project, resident, vec, qkv_weight)
    up_two = up_g.two()
    mixed = chain(lambda v: attention_forward(v, *lengths), qkv)
    normed_two, hidden = chain(attend, mixed, out_weight, resident, vec)
    ct_sent = swap(grad_result, 1)
    normed_sent = swap(normed_two, 1)

    def with_pieces(step, pieces):
        def run(*args):
            arrays, rest = args[: len(pieces)], args[len(pieces) :]
            return step([(a, p[1]) for a, p in zip(arrays, pieces)], *rest)

        return run

    up_arrays = [p[0] for p in up_g.pieces]
    down_two = down_g.two(*up_two)
    act_own, slope_own, up_weight = chain(
        with_pieces(lambda p, n, s: feed_first(n, p, s), up_g.pieces), *up_arrays, normed_two, shift
    )
    act_other, slope_other = chain(feed_second, normed_sent, up_weight, shift)
    down_sone = down_s.one(
        chain(
            lambda a, b, p, q: down_grad((a, b), (p, q)), act_own, act_other, grad_result, ct_sent
        ),
    )

    pre_own, pre_other, grad_shift, down_weight = chain(
        with_pieces(lambda p, a, b, s, t: back_act((a, b), p, (s, t)), down_g.pieces),
        *[p[0] for p in down_g.pieces],
        grad_result,
        ct_sent,
        slope_own,
        slope_other,
    )
    two_other = swap(chain(lambda g, w: back_up(g, w, BF), pre_other, up_weight), 1)
    two_own = chain(lambda g, w: back_up(g, w, F32), pre_own, up_weight)
    grad_mixed, grad_low, grad_hidden, sums_two = chain(
        back_norm, two_own, two_other, hidden, vec, grad_result, out_weight
    )
    out_send, out_keep = chain(out_grad, mixed, grad_low)
    out_in = swap(out_send, 1)
    down_sz = down_s.over_z()
    up_sone = up_s.one(
        chain(
            lambda a, b, p, q, o, i: up_grad((a, b), (p, q), o, i),
            normed_two,
            normed_sent,
            pre_own,
            pre_other,
            out_keep,
            out_in,
        )
    )
    grads = chain(lambda a, b: attention_backward(a, b, *lengths), qkv, grad_mixed)
    up_stwo = up_s.two()
    attn_send, attn_keep = chain(attn_grad, normed, grads)
    attn_in = swap(attn_send, 1)
    grad_rows, sums_one = chain(back_first, grads, qkv_weight, resident, vec, grad_hidden)

    def small_lines(one, two, shift):
        last = shift.reshape(chips, row_f // row_w, row_w).transpose(1, 0, 2)[:, :, None]
        last = ordered(c, last, jnp.zeros_like(last), 2).reshape(-1, D)
        return jnp.concatenate([one, two, last], 0)

    sums = chain(small_lines, sums_one, sums_two, grad_shift)
    sums_in = swap(sums, 1)
    down_x, down_y, down_one_own, down_two_own = down_s.last()
    attn_parts = chain(
        lambda a, b, p, q: core_sum(a, b, p, q, attn_s.rel_z), attn_keep, attn_in, sums, sums_in
    )
    attn_sone = attn_s.one(attn_parts)
    later = swap(attn_parts[0][0, :16, :128], 1)
    down_sent = swap(
        chain(lambda a, w, v: down_back(a, w, BF, None, v), act_other, down_weight, later), 1
    )
    down_own = chain(lambda a, w, h: down_back(a, w, F32, h), act_own, down_weight, hidden)

    up_sz = up_s.over_z()

    def result_of(own, other):
        total = (own + other.astype(F32)).astype(BF).reshape(2, ROW, D)
        return split_halves(total)

    res_send, res_own = chain(result_of, down_own, down_sent)
    gx_send, gx_own = chain(split_halves, grad_rows)
    attn_stwo = attn_s.two(extras=(down_x, down_y))
    sum_up = chain(up_s.total, up_sz)
    sum_up = sum_up.reshape(-1, FF // 2)
    out_rows = sum_up[2 * row_w :]
    sum_out = jnp.concatenate([out_rows[:, :D], out_rows[:, D:]], 0)
    up_rows = sum_up[: 2 * row_w].reshape(2, row_w, FF // 2)
    up_mine = lax.dynamic_index_in_dim(up_rows, c, 0, keepdims=False)
    up_theirs = swap(lax.dynamic_index_in_dim(up_rows, 1 - c, 0, keepdims=False), 1)
    gx_other = swap(after(gx_send, *attn_stwo), "y")
    out_other = swap(after(res_send, *attn_stwo), "y")
    attn_sz = attn_s.over_z()

    def sum_of_down(upper, from_x, lower, from_y):
        from_x, from_y = (v[:, 3 * D + 128 :].reshape(half_f, D) for v in (from_x, from_y))
        return jnp.concatenate([plus(upper.astype(F32), from_x), plus(lower.astype(F32), from_y)], 0)

    sum_down = chain(sum_of_down, down_one_own, attn_stwo[0], down_two_own, attn_stwo[1])

    def home(own, other):
        return ordered(y, own[None], other[None], 0).reshape(MICRO, 1, 1, ROW, D)

    up_final = chain(interleave, up_mine, up_theirs)
    out_stack = chain(home, res_own, out_other)
    grad_stack = chain(lambda own, other: home(own, other).astype(F32), gx_own, gx_other)
    sum_attn = attn_s.total(attn_sz)
    small_sum = sum_attn[:, 3 * D : 3 * D + lines].T.reshape(-1)
    edges = [i * row_w for i in range(5)]
    small_out = [small_sum[a:b] for a, b in zip(edges[:4], edges[1:])]
    return (
        out_stack,
        grad_stack,
        small_out[0],
        small_out[1],
        sum_attn[:, : 3 * D],
        sum_out,
        small_out[2],
        small_out[3],
        up_final.reshape(row_w, FF),
        small_sum[4 * row_w : 4 * row_w + row_f],
        sum_down,
    )


def plain_passed_along(block, axis, distance):
    devices = range(lax.axis_size(axis))
    route = [(i - distance, i) for i in devices if i - distance in devices]
    return lax.ppermute(block, axis, route)


def plain_times_transposed(left, right):
    return lax.dot_general(
        left, right, (((1,), (1,)), ((), ())), preferred_element_type=jnp.float32
    )


def plain_transposed_times(left, right):
    return lax.dot_general(
        left, right, (((0,), (0,)), ((), ())), preferred_element_type=jnp.float32
    )


def plain_layer_norm(values, gain, bias):
    center = values - jnp.mean(values, -1, keepdims=True)
    spread = jnp.mean(center * center, -1, keepdims=True)
    return center * lax.rsqrt(spread + 1e-05) * gain + bias


def plain_locate(lengths, slot_ids):
    count = jnp.arange(lengths.shape[0])
    seg_ends = jnp.sum(jnp.where(count[None, :] <= count[:, None], lengths[None, :], 0), 1, dtype=jnp.int32)
    seg_ids = jnp.sum(
        (slot_ids[:, None] >= seg_ends[None, :]).astype(jnp.int32), 1, dtype=jnp.int32
    )
    one_hot = (seg_ids[:, None] == jnp.arange(lengths.shape[0], dtype=jnp.int32)[None, :]).astype(
        jnp.int32
    )
    seg_start = jnp.sum(one_hot * (seg_ends - lengths)[None, :], 1, dtype=jnp.int32)
    return (seg_ids, one_hot, slot_ids - seg_start)


def plain_frame_meta(phone_lens, prompt_lens, target_lens, slot_count):
    slot_ids = jnp.arange(slot_count, dtype=jnp.int32)
    pre_seg, pre_hot, pre_off = plain_locate(phone_lens + prompt_lens, slot_ids)
    pre_phone = jnp.sum(pre_hot * phone_lens[None, :], 1, dtype=jnp.int32)
    prefix = (pre_seg, pre_off < pre_phone, pre_off - pre_phone)
    tgt_seg, tgt_hot, tgt_off = plain_locate(target_lens, slot_ids)
    tgt_pos = jnp.sum(tgt_hot * prompt_lens[None, :], 1, dtype=jnp.int32) + tgt_off
    targets = (tgt_seg, tgt_off < 0, tgt_pos)
    return (prefix, targets)


def plain_allowed(query_meta, key_meta):
    same_seg = query_meta[0][:, None] == key_meta[0][None, :]
    audio_ok = key_meta[1][None, :] | (key_meta[2][None, :] <= query_meta[2][:, None])
    return same_seg & jnp.where(query_meta[1][:, None], key_meta[1][None, :], audio_ok)


def plain_masked_scores(queries, key_rows, allowed_mask, score_scale):
    scores = (
        jnp.einsum("qhd,khd->hqk", queries, key_rows, preferred_element_type=jnp.float32)
        * score_scale
    )
    return jnp.where(allowed_mask[None], scores, -1e30)


def plain_attention_forward(queries, key_rows, value_rows, allowed_mask, score_scale):
    scores = plain_masked_scores(queries, key_rows, allowed_mask, score_scale)
    peak = jnp.max(scores, -1, keepdims=True)
    exp_scores = jnp.exp(scores - peak)
    row_total = jnp.sum(exp_scores, -1, keepdims=True)
    probs = (exp_scores / row_total).astype(jnp.bfloat16)
    mixed = jnp.einsum("hqk,khd->qhd", probs, value_rows, preferred_element_type=jnp.float32)
    return (mixed.astype(jnp.bfloat16), peak + jnp.log(row_total))


def plain_attention_backward(
    queries, key_rows, value_rows, allowed_mask, log_total, grad_mixed, score_scale
):
    scores = plain_masked_scores(queries, key_rows, allowed_mask, score_scale)
    probs = jnp.where(allowed_mask[None], jnp.exp(scores - log_total), 0.0)
    grad_probs = jnp.einsum(
        "qhd,khd->hqk", grad_mixed, value_rows, preferred_element_type=jnp.float32
    )
    grad_values = jnp.einsum(
        "hqk,qhd->khd", probs.astype(jnp.bfloat16), grad_mixed, preferred_element_type=jnp.float32
    )
    inner = jnp.sum(grad_probs * probs, -1, keepdims=True)
    grad_scores = (probs * (grad_probs - inner)).astype(jnp.bfloat16)
    grad_queries = (
        jnp.einsum("hqk,khd->qhd", grad_scores, key_rows, preferred_element_type=jnp.float32)
        * score_scale
    )
    grad_keys = (
        jnp.einsum("hqk,qhd->khd", grad_scores, queries, preferred_element_type=jnp.float32)
        * score_scale
    )
    return (grad_queries, grad_keys, grad_values)


def plain_add_up(summed, fresh):
    if summed is None:
        return fresh
    return jax.tree.map(lambda summed_part, fresh_part: summed_part + fresh_part, summed, fresh)


def plain_fetch_forward(params):
    return (
        lax.all_gather(params[0], ("pair", "rows"), axis=0, tiled=True),
        lax.all_gather(params[1], ("pair", "rows"), axis=0, tiled=True),
        lax.all_gather(params[2], ("pair", "rows"), axis=0, tiled=True),
        lax.all_gather(params[3], ("pair", "rows"), axis=0, tiled=True),
        lax.all_gather(params[4], ("pair", "rows"), axis=0, tiled=True),
        lax.all_gather(params[5], ("pair", "rows"), axis=0, tiled=True),
        lax.all_gather(params[6], ("pair", "rows"), axis=0, tiled=True),
        lax.all_gather(params[7], ("pair", "rows"), axis=0, tiled=True),
        lax.all_gather(params[8], ("pair", "rows"), axis=0, tiled=True),
    )


def plain_shards(
    inputs,
    cotangent,
    phone_len,
    prompt_len,
    target_len,
    ln1_gain,
    ln1_bias,
    w_qkv,
    w_out,
    ln2_gain,
    ln2_bias,
    w_up,
    up_bias,
    w_down,
):
    half_index = lax.axis_index("pair")
    score_scale = HEAD ** (-0.5)
    params = (ln1_gain, ln1_bias, w_qkv, w_out, ln2_gain, ln2_bias, w_up, up_bias, w_down)
    out_blocks = []
    grad_blocks = []
    summed = None
    for batch_index in range(MICRO):
        gathered = plain_fetch_forward(params)
        (
            gain_one,
            bias_one,
            qkv_weight,
            out_weight,
            gain_two,
            bias_two,
            up_weight,
            up_shift,
            down_weight,
        ) = gathered
        gain_one_f = gain_one.astype(jnp.float32)
        bias_one_f = bias_one.astype(jnp.float32)
        gain_two_f = gain_two.astype(jnp.float32)
        bias_two_f = bias_two.astype(jnp.float32)
        prefix, targets = plain_frame_meta(
            phone_len[batch_index, 0], prompt_len[batch_index, 0], target_len[batch_index, 0], ROW
        )
        query_meta = tuple(
            (
                jnp.where(half_index == 0, pre_field, tgt_field)
                for pre_field, tgt_field in zip(prefix, targets)
            )
        )
        remote_mask = plain_allowed(query_meta, prefix) & (half_index == 1)
        allowed_mask = jnp.concatenate([remote_mask, plain_allowed(query_meta, query_meta)], 1)
        resident = inputs[batch_index, 0, 0].astype(jnp.float32)
        normed = plain_layer_norm(resident, gain_one_f, bias_one_f).astype(jnp.bfloat16)
        qkv_rows = jnp.dot(normed, qkv_weight, preferred_element_type=jnp.float32).astype(
            jnp.bfloat16
        )
        own_kv = qkv_rows[:, D:]
        remote_kv = plain_passed_along(own_kv, "pair", 1)
        queries = qkv_rows[:, :D].reshape(ROW, HEADS, HEAD)
        key_rows = jnp.concatenate([remote_kv[:, :D], own_kv[:, :D]], 0).reshape(
            2 * ROW, HEADS, HEAD
        )
        value_rows = jnp.concatenate([remote_kv[:, D:], own_kv[:, D:]], 0).reshape(
            2 * ROW, HEADS, HEAD
        )
        mixed, log_total = plain_attention_forward(
            queries, key_rows, value_rows, allowed_mask, score_scale
        )
        mixed_flat = mixed.reshape(ROW, D)
        hidden_res = resident + jnp.dot(mixed_flat, out_weight, preferred_element_type=jnp.float32)
        normed_two = plain_layer_norm(hidden_res, gain_two_f, bias_two_f).astype(jnp.bfloat16)
        pre_act = jnp.dot(
            normed_two, up_weight, preferred_element_type=jnp.float32
        ) + up_shift.astype(jnp.float32)
        activ = jax.nn.gelu(pre_act, approximate=True).astype(jnp.bfloat16)
        result = hidden_res + jnp.dot(activ, down_weight, preferred_element_type=jnp.float32)
        out_blocks.append(result.astype(jnp.bfloat16))
        gathered = (
            lax.all_gather(params[0], ("pair", "rows"), axis=0, tiled=True),
            lax.all_gather(params[1], ("pair", "rows"), axis=0, tiled=True),
            lax.all_gather(params[2], ("pair", "rows"), axis=0, tiled=True),
            lax.all_gather(params[3], ("pair", "rows"), axis=0, tiled=True),
            lax.all_gather(params[4], ("pair", "rows"), axis=0, tiled=True),
            lax.all_gather(params[5], ("pair", "rows"), axis=0, tiled=True),
            lax.all_gather(params[6], ("pair", "rows"), axis=0, tiled=True),
            lax.all_gather(params[7], ("pair", "rows"), axis=0, tiled=True),
            lax.all_gather(params[8], ("pair", "rows"), axis=0, tiled=True),
        )
        (
            gain_one,
            bias_one,
            qkv_weight,
            out_weight,
            gain_two,
            bias_two,
            up_weight,
            up_shift,
            down_weight,
        ) = gathered
        gain_one_f = gain_one.astype(jnp.float32)
        bias_one_f = bias_one.astype(jnp.float32)
        gain_two_f = gain_two.astype(jnp.float32)
        bias_two_f = bias_two.astype(jnp.float32)
        grad_result = cotangent[batch_index, 0, 0]
        grad_down = plain_transposed_times(activ, grad_result)
        grad_activ = plain_times_transposed(grad_result, down_weight)
        _, gelu_back = jax.vjp(lambda pre_value: jax.nn.gelu(pre_value, approximate=True), pre_act)
        grad_pre = gelu_back(grad_activ)[0].astype(jnp.bfloat16)
        grad_up = plain_transposed_times(normed_two, grad_pre)
        grad_up_bias = jnp.sum(grad_pre.astype(jnp.float32), 0)
        grad_normed_two = plain_times_transposed(grad_pre, up_weight)
        _, norm_back_two = jax.vjp(plain_layer_norm, hidden_res, gain_two_f, bias_two_f)
        grad_hidden_ln, grad_gain_two, grad_bias_two = norm_back_two(grad_normed_two)
        grad_hidden = grad_result.astype(jnp.float32) + grad_hidden_ln
        grad_hidden_low = grad_hidden.astype(jnp.bfloat16)
        grad_out_w = plain_transposed_times(mixed_flat, grad_hidden_low)
        grad_mixed = (
            plain_times_transposed(grad_hidden_low, out_weight)
            .astype(jnp.bfloat16)
            .reshape(ROW, HEADS, HEAD)
        )
        grad_queries, grad_keys, grad_values = plain_attention_backward(
            queries, key_rows, value_rows, allowed_mask, log_total, grad_mixed, score_scale
        )
        remote_grads = jnp.concatenate(
            [grad_keys[:ROW].reshape(ROW, D), grad_values[:ROW].reshape(ROW, D)], 1
        )
        returned = plain_passed_along(remote_grads.astype(jnp.bfloat16), "pair", -1).astype(
            remote_grads.dtype
        )
        grad_qkv_rows = jnp.concatenate(
            [
                grad_queries.reshape(ROW, D),
                grad_keys[ROW:].reshape(ROW, D) + returned[:, :D],
                grad_values[ROW:].reshape(ROW, D) + returned[:, D:],
            ],
            1,
        ).astype(jnp.bfloat16)
        grad_qkv_w = plain_transposed_times(normed, grad_qkv_rows)
        grad_normed = plain_times_transposed(grad_qkv_rows, qkv_weight)
        _, norm_back_one = jax.vjp(plain_layer_norm, resident, gain_one_f, bias_one_f)
        grad_resident_ln, grad_gain_one, grad_bias_one = norm_back_one(grad_normed)
        grad_blocks.append(grad_hidden + grad_resident_ln)
        local_grads = (
            grad_gain_one,
            grad_bias_one,
            grad_qkv_w,
            grad_out_w,
            grad_gain_two,
            grad_bias_two,
            grad_up,
            grad_up_bias,
            grad_down,
        )
        shard_part = (
            lax.psum_scatter(local_grads[0], ("pair", "rows"), scatter_dimension=0, tiled=True),
            lax.psum_scatter(local_grads[1], ("pair", "rows"), scatter_dimension=0, tiled=True),
            lax.psum_scatter(local_grads[2], ("pair", "rows"), scatter_dimension=0, tiled=True),
            lax.psum_scatter(local_grads[3], ("pair", "rows"), scatter_dimension=0, tiled=True),
            lax.psum_scatter(local_grads[4], ("pair", "rows"), scatter_dimension=0, tiled=True),
            lax.psum_scatter(local_grads[5], ("pair", "rows"), scatter_dimension=0, tiled=True),
            lax.psum_scatter(local_grads[6], ("pair", "rows"), scatter_dimension=0, tiled=True),
            lax.psum_scatter(local_grads[7], ("pair", "rows"), scatter_dimension=0, tiled=True),
            lax.psum_scatter(local_grads[8], ("pair", "rows"), scatter_dimension=0, tiled=True),
        )
        summed = plain_add_up(summed, shard_part)
    block_shape = (MICRO, 1, 1, ROW, D)
    out_stack = jnp.stack(out_blocks, 0).reshape(block_shape)
    grad_stack = jnp.stack(grad_blocks, 0).reshape(block_shape)
    return (
        out_stack,
        grad_stack,
        summed[0],
        summed[1],
        summed[2],
        summed[3],
        summed[4],
        summed[5],
        summed[6],
        summed[7],
        summed[8],
    )


def solution(mesh):
    rows = P(None, "rows", "pair", None, None)
    line = P(("pair", "rows"))
    flat = P(("pair", "rows"), None)
    lens = P(None, "rows", None)
    return jax.shard_map(
        shards if mesh.shape["rows"] == 16 else plain_shards,
        mesh=mesh,
        in_specs=(rows, rows, lens, lens, lens, line, line, flat, flat, line, line, flat, line, flat),
        out_specs=(rows, rows, line, line, flat, flat, line, line, flat, line, flat),
        check_vma=False,
    )
```

```python
import functools

import jax
import jax.numpy as jnp
from jax import lax
from jax.experimental import pallas as pl
from jax.experimental.pallas import tpu as pltpu
from jax.sharding import PartitionSpec as P

D = 1024
HEADS = 16
HEAD = 64
FF = 4096
ROW = 256
MICRO = 2
BF = jnp.bfloat16
F32 = jnp.float32
NEG = -1e30


def position():
    row = lax.axis_index("rows")
    return lax.axis_index("pair"), row // 4, (row // 2) % 2, row % 2


def depth():
    return lax.axis_size("rows") // 4


def swap(block, way):
    if way == "y":
        return lax.ppermute(block, "pair", [(i, i ^ 1) for i in range(2)])
    count = lax.axis_size("rows")
    return lax.ppermute(block, "rows", [(i, i ^ way) for i in range(count)])


def after(block, *others):
    return lax.optimization_barrier((block, *others))[0]


class Chain:
    def __init__(self):
        self.last = None

    def __call__(self, step, *args):
        if self.last is not None:
            args, _ = lax.optimization_barrier((args, self.last))
        out = step(*args)
        self.last = out
        return out


def z_groups():
    count = lax.axis_size("rows")
    return [[z * 4 + low for z in range(count // 4)] for low in range(4)]


def z_gather(block):
    return lax.all_gather(block, "rows", axis_index_groups=z_groups())


def z_scatter(column):
    return lax.psum_scatter(column, "rows", scatter_dimension=0, axis_index_groups=z_groups())


class Gather:
    def __init__(self, chain, by_permutes):
        self.chain = chain
        self.rel_z = by_permutes and depth() == 4

    def over_z(self, block, *first):
        block = after(block, *first)
        if self.rel_z:
            self.column = [block[None]] + [swap(block[None], 4 * k) for k in range(1, 4)]
            return self.column[1:]
        self.column = [z_gather(block)]
        return self.column

    def one(self, *first, extras=()):
        half = depth() // 2

        def halves(column, extras):
            if self.rel_z:
                left, right = jnp.concatenate(column[:2], 0), jnp.concatenate(column[2:], 0)
            else:
                left, right = column[0][:half], column[0][half:]
            return beside((left, right), extras)

        self.halves = self.chain(halves, self.column, extras)
        return self.send(*first)

    def one_halves(self):
        half = depth() // 2
        self.halves = self.chain(lambda v: (v[:half], v[half:]), self.column[0])

    def send(self, *first):
        left, right = lax.optimization_barrier((self.halves, first))[0]
        self.sides = swap(left, 2), swap(right, "y")
        return list(self.sides)

    def two(self, *first, extras=()):
        rows, cols = self.column[0].shape[-2:]
        block = (depth() // 2, rows, cols)

        def planes(halves, sides):
            left, right = halves
            left_x, right_y = sides
            if not extras:
                return jnp.concatenate([left, left_x], 0), jnp.concatenate([right, right_y], 0)
            main = [v[:, :cols].reshape(block) for v in (left, left_x, right, right_y)]
            more = [v[:, cols:].reshape(extras) for v in (left, left_x, right, right_y)]
            return (
                jnp.concatenate(main[:2], 0),
                jnp.concatenate(main[2:], 0),
                jnp.stack(more, 0),
            )

        sides = lax.optimization_barrier((self.sides, first))[0]
        self.planes = self.chain(planes, self.halves, sides)
        left, right = self.planes[:2]
        left_y, right_x = swap(left, "y"), swap(right, 2)
        half = depth() // 2
        low, high = range(half), range(half, 2 * half)
        self.pieces = [
            (left, [(0, i, 0) for i in low] + [(0, i, 1) for i in low]),
            (left_y, [(1, i, 0) for i in low] + [(1, i, 1) for i in low]),
            (right, [(0, i, 0) for i in high] + [(1, i, 0) for i in high]),
            (right_x, [(0, i, 1) for i in high] + [(1, i, 1) for i in high]),
        ]
        return [left_y, right_x]


def beside(blocks, extras):
    if not extras:
        return tuple(blocks)
    out = []
    for block, extra in zip(blocks, extras):
        rows = block.shape[0] * block.shape[1]
        out.append(
            jnp.concatenate([block.reshape(rows, -1), extra.reshape(rows, -1)], 1)
        )
    return tuple(out)


class GatherXZY:
    def __init__(self, chain):
        self.chain = chain

    def over_z(self, lines, *first):
        self.column = z_gather(after(lines, *first))
        return self.column

    def two(self, *first):
        def cut(column):
            shape = (2 * depth(), *column.shape[2:])
            return column[:, :2].reshape(shape), column[:, 2:].reshape(shape)

        upper, lower = self.chain(cut, after(self.column, *first))
        upper_y, lower_x = swap(upper, "y"), swap(lower, 2)
        ids = range(depth())
        self.pieces = [
            (upper, [(0, i, j) for i in ids for j in range(2)]),
            (upper_y, [(1, i, j) for i in ids for j in range(2)]),
            (lower, [(j, i, 0) for i in ids for j in range(2)]),
            (lower_x, [(j, i, 1) for i in ids for j in range(2)]),
        ]
        return [upper_y, lower_x]


def chip_slot(chip, where, rel_z):
    jy, jz, jx = chip
    y, z, x, _ = where
    z_at = (z ^ jz) if rel_z else jz
    return ((y ^ jy) * depth() + z_at) * 2 + (x ^ jx)


def layout_yzx():
    ids = range(depth())
    return [
        [(1, i, j) for i in ids for j in range(2)],
        [(0, i, j) for i in ids for j in range(2)],
        [(j, i, 1) for i in ids for j in range(2)],
        [(j, i, 0) for i in ids for j in range(2)],
    ]


def layout_yxz():
    half = depth() // 2
    low, high = range(half), range(half, 2 * half)
    return [
        [(1, i, j) for j in range(2) for i in low],
        [(0, i, j) for j in range(2) for i in low],
        [(j, i, 1) for j in range(2) for i in high],
        [(j, i, 0) for j in range(2) for i in high],
    ]


def plus(left, right):
    return (left.astype(F32) + right.astype(F32)).astype(left.dtype)


def add_halves(left, left_in, right, right_in, extras):
    count, rows, cols = left.shape
    half = count // 2
    more = extras[0].shape[2] if extras else 0
    extras = list(extras) * 2

    def kernel(*refs):
        ins, outs = refs[: 8 + len(extras)], refs[8 + len(extras) :]
        for side in range(2):
            a, b, c, d = ins[4 * side : 4 * side + 4]
            own, send = outs[2 + side], outs[side]
            own[...] = (a[...].astype(F32) + b[...].astype(F32)).astype(BF)
            total = (c[0].astype(F32) + d[0].astype(F32)).astype(BF)
            if extras:
                send[:, :cols] = total
                send[:, cols:] = ins[8 + side][0]
            else:
                send[0] = total

    low = pl.BlockSpec((1, rows, cols), lambda i: (i, 0, 0))
    high = pl.BlockSpec((1, rows, cols), lambda i: (i + half, 0, 0))
    wide = pl.BlockSpec((rows, cols + more), lambda i: (i, 0))
    send = jax.ShapeDtypeStruct((half * rows, cols + more) if extras else (half, rows, cols), BF)
    own = jax.ShapeDtypeStruct((half, rows, cols), BF)
    return pl.pallas_call(
        kernel,
        grid=(half,),
        out_shape=[send, send, own, own],
        in_specs=[low, low, high, high] * 2
        + [pl.BlockSpec((1, rows, more), lambda i, n=n: (n, i, 0)) for n in (1, 3)[: len(extras)]],
        out_specs=[wide if extras else low] * 2 + [low] * 2,
        compiler_params=pltpu.CompilerParams(vmem_limit_bytes=16 << 20),
        cost_estimate=pl.CostEstimate(flops=1 << 35, bytes_accessed=1 << 10, transcendentals=0),
        name="add_halves",
    )(left, left_in, left, left_in, right, right_in, right, right_in, *extras)


def add_column(left, left_in, right, right_in):
    half, rows, cols = left.shape

    def kernel(a_ref, b_ref, c_ref, d_ref, out_ref):
        out_ref[0] = (a_ref[0].astype(F32) + b_ref[0].astype(F32)).astype(BF)
        out_ref[1] = (c_ref[0].astype(F32) + d_ref[0].astype(F32)).astype(BF)

    part = pl.BlockSpec((1, rows, cols), lambda i: (i, 0, 0))
    return pl.pallas_call(
        kernel,
        grid=(half,),
        out_shape=jax.ShapeDtypeStruct((2, half, rows, cols), BF),
        in_specs=[part] * 4,
        out_specs=pl.BlockSpec((2, None, rows, cols), lambda i: (0, i, 0, 0)),
        compiler_params=pltpu.CompilerParams(vmem_limit_bytes=16 << 20),
        cost_estimate=pl.CostEstimate(flops=1 << 20, bytes_accessed=1 << 10, transcendentals=0),
        name="add_column",
    )(left, left_in, right, right_in).reshape(2 * half, rows, cols)


class Scatter:
    def __init__(self, chain, by_permutes):
        self.chain = chain
        self.rel_z = by_permutes and depth() == 4

    def one(self, parts, *first):
        self.parts = parts
        left, _, right, _ = parts
        self.sides = swap(after(left, *first), "y"), swap(after(right, *first), 2)
        return list(self.sides)

    def two(self, *first, extras=()):
        _, left, _, right = self.parts
        left_in, right_in = lax.optimization_barrier((self.sides, first))[0]
        self.sums = self.chain(add_halves, left, left_in, right, right_in, extras)
        self.ends = swap(self.sums[0], 2), swap(self.sums[1], "y")
        return list(self.ends)

    def over_z(self, *first):
        _, _, left, right = self.sums
        left_in, right_in = self.ends

        def add(left, left_in, right, right_in):
            left_in, right_in = (
                v if v.ndim == 3 else v[:, : left.shape[2]].reshape(left.shape)
                for v in (left_in, right_in)
            )
            if self.rel_z:
                return (
                    plus(left[1], left_in[1]),
                    *plus(right, right_in),
                    left[0].astype(F32) + left_in[0].astype(F32),
                )
            return add_column(left, left_in, right, right_in)

        made = self.chain(add, left, left_in, right, right_in)
        if not self.rel_z:
            return z_scatter(after(made, *first))
        one, two, three, own = made
        return own, swap(one, 4), swap(two, 8), swap(three, 12)

    def total(self, parts):
        if not self.rel_z:
            return parts.astype(F32)
        own, *arrived = parts

        def add(own, *arrived):
            for part in arrived:
                own = own + part.astype(F32)
            return own

        return self.chain(add, own, *arrived)


class ScatterYZX:
    def __init__(self, chain):
        self.chain = chain

    def one(self, parts, *first):
        self.parts = parts
        left, _, right, _ = parts
        self.sides = swap(after(left, *first), "y"), swap(after(right, *first), 2)
        return list(self.sides)

    def over_z(self, *first):
        def add(left, left_in, right, right_in):
            shape = (depth(), 2, *left.shape[1:])
            upper, lower = plus(left, left_in).reshape(shape), plus(right, right_in).reshape(shape)
            return jnp.concatenate([upper, lower], 1)

        _, left, _, right = self.parts
        self.lines = z_scatter(self.chain(add, left, self.sides[0], right, self.sides[1]))
        return self.lines


def ordered(flag, own, other, axis):
    return jnp.where(
        flag == 0,
        jnp.concatenate([own, other], axis),
        jnp.concatenate([other, own], axis),
    )


def frames(index, phone, prompt, target, segs):
    pre_end = ends_of([phone[s] + prompt[s] for s in range(segs)])
    tgt_end = ends_of([target[s] for s in range(segs)])
    is_target = index >= ROW
    local = jnp.where(is_target, index - ROW, index)
    seg = jnp.zeros_like(index)
    for s in range(segs):
        edge = jnp.where(is_target, tgt_end[s], pre_end[s])
        seg = seg + jnp.where(local >= edge, 1, 0)
    start = jnp.zeros_like(index)
    phones = jnp.zeros_like(index)
    prompts = jnp.zeros_like(index)
    for s in range(segs):
        pick = seg == s
        pre_start = pre_end[s] - phone[s] - prompt[s]
        tgt_start = tgt_end[s] - target[s]
        start = jnp.where(pick, jnp.where(is_target, tgt_start, pre_start), start)
        phones = jnp.where(pick, phone[s], phones)
        prompts = jnp.where(pick, prompt[s], prompts)
    off = local - start
    is_phone = jnp.where(is_target, 0, jnp.where(off < phones, 1, 0))
    pos = jnp.where(is_target, prompts + off, off - phones)
    return seg, is_phone, pos


def ends_of(lengths):
    out, total = [], 0
    for length in lengths:
        total = total + length
        out.append(total)
    return out


def bias_of(query, key):
    q_seg, q_phone, q_pos = query
    k_seg, k_phone, k_pos = key
    audio = (k_phone == 1) | (k_pos <= q_pos)
    good = (q_seg == k_seg) & (((q_phone == 1) & (k_phone == 1)) | ((q_phone == 0) & audio))
    return jnp.where(good, 0.0, NEG)


def bdot(left, right, dims):
    return lax.dot_general(left, right, (dims, ((), ())), preferred_element_type=F32)


NT = ((1,), (1,))
NN = ((1,), (0,))
TN = ((0,), (0,))


def attention_forward(qkv, phone, prompt, target):
    segs = phone.shape[0]
    group = 2

    def kernel(
        phone_ref, prompt_ref, target_ref, q_ref, k_ref, v_ref, out_ref, log_ref, bias_ref
    ):
        @pl.when(pl.program_id(0) == 0)
        def _():
            ph = [phone_ref[s] for s in range(segs)]
            pr = [prompt_ref[s] for s in range(segs)]
            tg = [target_ref[s] for s in range(segs)]
            rows = lax.broadcasted_iota(jnp.int32, (2 * ROW, 1), 0)
            cols = lax.broadcasted_iota(jnp.int32, (1, 2 * ROW), 1)
            bias_ref[...] = bias_of(
                frames(cols, ph, pr, tg, segs), frames(rows, ph, pr, tg, segs)
            )

        lane = lax.broadcasted_iota(jnp.int32, (1, 2 * HEAD), 1)
        zero = jnp.zeros((), BF)
        scale = jnp.asarray(HEAD**-0.5, BF)
        for pair in range(group):
            cols = slice(pair * 2 * HEAD, (pair + 1) * 2 * HEAD)
            for rows, keys in ((0, ROW), (ROW, 2 * ROW)):
                at = slice(rows, rows + ROW)
                outs = []
                for j in range(2):
                    q = jnp.where((lane // HEAD) == j, q_ref[at, cols] * scale, zero)
                    s = bdot(k_ref[:keys, cols], q, NT) + bias_ref[:keys, at]
                    peak = jnp.max(s, 0, keepdims=True)
                    e = jnp.exp(s - peak)
                    total = jnp.sum(e, 0, keepdims=True)
                    log_ref[0, 2 * pair + j : 2 * pair + j + 1, at] = peak + jnp.log(total)
                    p = (e * (1.0 / total)).astype(BF)
                    outs.append(bdot(v_ref[:keys, cols], p, TN)[j * HEAD : (j + 1) * HEAD])
                out_ref[at, cols] = jnp.transpose(jnp.concatenate(outs, 0)).astype(BF)

    steps = HEADS // 2 // group
    smem = pl.BlockSpec(memory_space=pltpu.SMEM)
    part = (2 * ROW, 2 * HEAD * group)
    return pl.pallas_call(
        kernel,
        grid=(steps,),
        out_shape=[
            jax.ShapeDtypeStruct((2 * ROW, D), BF),
            jax.ShapeDtypeStruct((steps, 2 * group, 2 * ROW), F32),
        ],
        in_specs=[
            smem,
            smem,
            smem,
            pl.BlockSpec(part, lambda h: (0, h)),
            pl.BlockSpec(part, lambda h: (0, h + steps)),
            pl.BlockSpec(part, lambda h: (0, h + 2 * steps)),
        ],
        out_specs=[
            pl.BlockSpec(part, lambda h: (0, h)),
            pl.BlockSpec((1, 2 * group, 2 * ROW), lambda h: (h, 0, 0)),
        ],
        scratch_shapes=[pltpu.VMEM((2 * ROW, 2 * ROW), F32)],
        compiler_params=pltpu.CompilerParams(vmem_limit_bytes=16 << 20),
        cost_estimate=pl.CostEstimate(flops=1 << 20, bytes_accessed=1 << 10, transcendentals=0),
        name="attention_forward",
    )(phone, prompt, target, qkv, qkv, qkv)


def attention_backward(qkv, grad_mixed, logs, phone, prompt, target):
    segs = phone.shape[0]
    group = 2

    def kernel(
        phone_ref, prompt_ref, target_ref, q_ref, k_ref, v_ref, g_ref, log_ref, out_ref, bias_ref
    ):
        @pl.when(pl.program_id(0) == 0)
        def _():
            ph = [phone_ref[s] for s in range(segs)]
            pr = [prompt_ref[s] for s in range(segs)]
            tg = [target_ref[s] for s in range(segs)]
            rows = lax.broadcasted_iota(jnp.int32, (2 * ROW, 1), 0)
            cols = lax.broadcasted_iota(jnp.int32, (1, 2 * ROW), 1)
            bias_ref[...] = bias_of(
                frames(cols, ph, pr, tg, segs), frames(rows, ph, pr, tg, segs)
            )

        lane = lax.broadcasted_iota(jnp.int32, (1, 2 * HEAD), 1)
        zero = jnp.zeros((), BF)
        scale = HEAD**-0.5
        for pair in range(group):
            cols = slice(pair * 2 * HEAD, (pair + 1) * 2 * HEAD)
            dks, dvs = {}, {}
            for rows, keys in ((0, ROW), (ROW, 2 * ROW)):
                at = slice(rows, rows + ROW)
                dqs = []
                for j in range(2):
                    sel = (lane // HEAD) == j
                    q_all, g_all = q_ref[at, cols], g_ref[at, cols]
                    q = jnp.where(sel, q_all * jnp.asarray(scale, BF), zero)
                    g = jnp.where(sel, g_all, zero)
                    k, v = k_ref[:keys, cols], v_ref[:keys, cols]
                    s = bdot(k, q, NT) + bias_ref[:keys, at]
                    dp = bdot(v, g, NT)
                    p = jnp.exp(s - log_ref[0, 2 * pair + j : 2 * pair + j + 1, at])
                    inner = jnp.sum(dp * p, 0, keepdims=True)
                    ds = (p * (dp - inner)).astype(BF)
                    dvs[rows, j] = bdot(p.astype(BF), g_all, NN)
                    dks[rows, j] = bdot(ds, q_all, NN)
                    dqs.append(bdot(k, ds, TN)[j * HEAD : (j + 1) * HEAD])
                dq = jnp.transpose(jnp.concatenate(dqs, 0)) * scale
                out_ref[0, at, cols] = dq.astype(BF)
            low = lane < HEAD
            for place, part, factor in ((1, dks, scale), (2, dvs, 1.0)):
                early = jnp.where(low, part[0, 0], part[0, 1])
                late = jnp.where(low, part[ROW, 0], part[ROW, 1])
                out_ref[place, :ROW, cols] = ((early + late[:ROW]) * factor).astype(BF)
                out_ref[place, ROW:, cols] = (late[ROW:] * factor).astype(BF)

    steps = HEADS // 2 // group
    smem = pl.BlockSpec(memory_space=pltpu.SMEM)
    block = (2 * ROW, 2 * HEAD * group)
    return pl.pallas_call(
        kernel,
        grid=(steps,),
        out_shape=jax.ShapeDtypeStruct((3, 2 * ROW, D), BF),
        in_specs=[
            smem,
            smem,
            smem,
            pl.BlockSpec(block, lambda h: (0, h)),
            pl.BlockSpec(block, lambda h: (0, h + steps)),
            pl.BlockSpec(block, lambda h: (0, h + 2 * steps)),
            pl.BlockSpec(block, lambda h: (0, h)),
            pl.BlockSpec((1, 2 * group, 2 * ROW), lambda h: (h, 0, 0)),
        ],
        out_specs=pl.BlockSpec((3, *block), lambda h: (0, 0, h)),
        scratch_shapes=[pltpu.VMEM((2 * ROW, 2 * ROW), F32)],
        compiler_params=pltpu.CompilerParams(vmem_limit_bytes=16 << 20),
        cost_estimate=pl.CostEstimate(flops=1 << 20, bytes_accessed=1 << 10, transcendentals=0),
        name="attention_backward",
    )(phone, prompt, target, qkv, qkv, qkv, grad_mixed, logs)


VMEM = pl.BlockSpec(memory_space=pltpu.VMEM)
SMEM = pl.BlockSpec(memory_space=pltpu.SMEM)
ANY = pl.BlockSpec(memory_space=pl.ANY)


def shape_of(shape, dtype=BF):
    return jax.ShapeDtypeStruct(shape, dtype)


def call(name, kernel, outs, args, specs=None, scratch=(), megabytes=12, long=False):
    return pl.pallas_call(
        kernel,
        out_shape=outs,
        in_specs=[VMEM] * len(args) if specs is None else specs,
        out_specs=[VMEM] * len(outs),
        scratch_shapes=list(scratch),
        compiler_params=pltpu.CompilerParams(vmem_limit_bytes=megabytes << 20),
        cost_estimate=pl.CostEstimate(
            flops=1 << (35 if long else 20), bytes_accessed=1 << 10, transcendentals=0
        ),
        name=name,
    )(*args)


def block(ref, slot, size):
    return ref[:, pl.ds(pl.multiple_of(slot * size, size), size)]


def pack(w_qkv, w_out, vectors):
    rows = w_qkv.shape[0]
    sizes = [v.shape[0] for v in vectors]
    wide = max(sizes)
    table = jnp.stack([jnp.pad(v, (0, wide - v.shape[0])) for v in vectors], 0)

    def kernel(table_ref, qkv_ref, out_ref, to, sems):
        copies = [
            pltpu.make_async_copy(qkv_ref, to.at[:, pl.ds(0, 3 * D)], sems.at[0]),
            pltpu.make_async_copy(out_ref, to.at[:, pl.ds(3 * D, D)], sems.at[1]),
        ]
        for copy in copies:
            copy.start()
        row = lax.broadcasted_iota(jnp.int32, (rows, wide), 0)
        column = lax.broadcasted_iota(jnp.int32, (rows, wide), 1)
        lane = lax.broadcasted_iota(jnp.int32, (rows, 128), 1)
        total, place = jnp.zeros((rows, 128), F32), 0
        for n, size in enumerate(sizes):
            value = table_ref[n : n + 1, :].astype(F32)
            for start in range(0, size, rows):
                picked = jnp.sum(jnp.where(column == row + start, value, 0.0), 1, keepdims=True)
                total = total + jnp.where(lane == place, picked, 0.0)
                place += 1
        to[:, 4 * D :] = total.astype(BF)
        for copy in copies:
            copy.wait()

    return call(
        "pack",
        kernel,
        [shape_of((rows, 4 * D + 128))],
        (table, w_qkv, w_out),
        [VMEM, ANY, ANY],
        [pltpu.SemaphoreType.DMA((2,))],
    )[0]


def unpack(own, other, rel_z, count):
    chips, rows = 4 * depth(), own[0][0].shape[1]
    flat = [(core, p) for core, part in enumerate((own, other)) for p in part]
    arrays = [p[0] for _, p in flat]
    cuts = [(0, 3 * D), (3 * D, D), (4 * D, 128)]

    def kernel(*refs):
        ins = refs[: len(arrays)]
        qkv_ref, out_ref, vec_ref, small_ref, sems = refs[len(arrays) :]
        where = position()
        copies = []
        for n in (2, 0, 1):
            to = (qkv_ref, out_ref, small_ref)[n]
            start, width = cuts[n]
            for ref, (core, (_, names)) in zip(ins, flat):
                at = where[3] ^ core
                for i, name in enumerate(names):
                    copy = pltpu.make_async_copy(
                        ref.at[i, :, pl.ds(start, width)],
                        to.at[chip_slot(name, where, rel_z), at],
                        sems.at[len(copies)],
                    )
                    copy.start()
                    copies.append(copy)
        for copy in copies[: len(copies) // 3]:
            copy.wait()
        small = small_ref[...].reshape(2 * chips * rows, 128).astype(F32)
        vec_ref[...] = jnp.transpose(small)[:count]
        for copy in copies[len(copies) // 3 :]:
            copy.wait()

    shapes = [(chips, 2, rows, w) for _, w in cuts]
    qkv, out, vec = call(
        "unpack",
        kernel,
        [shape_of(shapes[0]), shape_of(shapes[1]), shape_of((count, D), F32)],
        arrays,
        [ANY] * len(arrays),
        [pltpu.VMEM(shapes[2], BF), pltpu.SemaphoreType.DMA((6 * chips,))],
    )
    return qkv.reshape(D, 3 * D), out.reshape(D, D), vec


def normal_of(values):
    center = values - jnp.mean(values, -1, keepdims=True)
    inv = lax.rsqrt(jnp.mean(center * center, -1, keepdims=True) + 1e-05)
    return center * inv, inv


def norm_back(grad, normal, inv, gain):
    e = grad * gain
    return inv * (
        e - jnp.mean(e, -1, keepdims=True) - normal * jnp.mean(e * normal, -1, keepdims=True)
    )


def project(resident, vec, weight):
    def kernel(x_ref, vec_ref, w_ref, normed_ref, qkv_ref):
        for r in range(0, 2 * ROW, ROW):
            normal, _ = normal_of(x_ref[r : r + ROW, :].astype(F32))
            normed_ref[r : r + ROW, :] = (normal * vec_ref[0:1, :] + vec_ref[1:2, :]).astype(BF)
        for n in range(0, 3 * D, 512):
            qkv_ref[:, n : n + 512] = bdot(normed_ref[...], w_ref[:, n : n + 512], NN).astype(BF)

    outs = [shape_of((2 * ROW, D)), shape_of((2 * ROW, 3 * D))]
    return call("project", kernel, outs, (resident, vec, weight))


def attend(mixed, weight, resident, vec):
    def kernel(m_ref, w_ref, x_ref, vec_ref, normed_ref, hidden_ref):
        for r in range(0, 2 * ROW, ROW):
            rows = slice(r, r + ROW)
            hidden = x_ref[rows, :].astype(F32) + bdot(m_ref[rows, :], w_ref[...], NN)
            hidden_ref[rows, :] = hidden
            normal, _ = normal_of(hidden)
            normed_ref[rows, :] = (normal * vec_ref[2:3, :] + vec_ref[3:4, :]).astype(BF)

    outs = [shape_of((2 * ROW, D)), shape_of((2 * ROW, D), F32)]
    return call("attend", kernel, outs, (mixed, weight, resident, vec))


def gelu_both(v):
    c = (2.0 / jnp.pi) ** 0.5
    square = v * v
    t = jnp.tanh(v * (c + (c * 0.044715) * square))
    half = 0.5 + 0.5 * t
    return v * half, half + 0.5 * v * (1.0 - t * t) * (c + (3 * c * 0.044715) * square)


def feed_step(n_ref, w_ref, shift_ref, act_ref, slope_ref, start, size):
    cols = slice(start, start + size)
    pre = bdot(n_ref[...], w_ref[:, cols], NN) + shift_ref[:, cols]
    act, slope = gelu_both(pre)
    act_ref[:, cols] = act.astype(BF)
    slope_ref[:, cols] = slope.astype(BF)


def feed_first(normed, pieces, shift):
    chips, (rows, wide) = 4 * depth(), pieces[0][0].shape[1:]
    arrays = [p[0] for p in pieces]
    size = 512

    def kernel(n_ref, shift_ref, *refs):
        ins = refs[: len(arrays)]
        act_ref, slope_ref, w_ref, sems = refs[len(arrays) :]
        where = position()
        copies = []
        for start in range(0, wide, size):
            for ref, (_, names) in zip(ins, pieces):
                for i, name in enumerate(names):
                    to = pl.multiple_of(chip_slot(name, where, False) * rows, rows)
                    copy = pltpu.make_async_copy(
                        ref.at[i, :, pl.ds(start, size)],
                        w_ref.at[pl.ds(to, rows), pl.ds(start, size)],
                        sems.at[len(copies)],
                    )
                    copy.start()
                    copies.append(copy)
        for n, start in enumerate(range(0, wide, size)):
            for copy in copies[n * chips : (n + 1) * chips]:
                copy.wait()
            feed_step(n_ref, w_ref, shift_ref, act_ref, slope_ref, start, size)

    part = shape_of((2 * ROW, wide))
    return call(
        "feed_first",
        kernel,
        [part, part, shape_of((chips * rows, wide))],
        (normed, shift, *arrays),
        [VMEM, VMEM] + [ANY] * len(arrays),
        [pltpu.SemaphoreType.DMA((chips * (wide // size),))],
        long=True,
    )


def feed_second(normed, weight, shift):
    def kernel(n_ref, w_ref, shift_ref, act_ref, slope_ref):
        for start in range(0, weight.shape[1], 512):
            feed_step(n_ref, w_ref, shift_ref, act_ref, slope_ref, start, 512)

    part = shape_of((2 * ROW, weight.shape[1]))
    return call("feed_second", kernel, [part, part], (normed, weight, shift))


def down_grad(acts, cts):
    lists = layout_yzx()
    chips = 4 * depth()
    size = acts[0].shape[1] // chips
    half = size // 2
    group = 4

    def kernel(a0, a1, c0, c1, *outs):
        where = position()
        for jy in range(2):
            for jx in range(2):
                for z in range(0, depth(), group):
                    names = [(jy, z + i, jx) for i in range(group)]
                    slots = [chip_slot(name, where, False) for name in names]
                    total = 0.0
                    for a, ct in ((a0, c0), (a1, c1)):
                        left = jnp.concatenate([block(a, slot, size) for slot in slots], 1)
                        total = total + bdot(left, ct[...], TN)
                    total = total.astype(BF).reshape(group, size, D)
                    for i, name in enumerate(names):
                        upper, lower = outs[1 - jy], outs[3 - jx]
                        upper[lists[1 - jy].index(name)] = total[i, :half]
                        lower[lists[3 - jx].index(name)] = total[i, half:]

    outs = [shape_of((len(v), half, D)) for v in lists]
    return call("down_grad", kernel, outs, (*acts, *cts))


def back_act(cts, pieces, slopes):
    wide = slopes[0].shape[1]
    chips = 4 * depth()
    size = wide // chips
    arrays = [p[0] for p in pieces]
    half = size // 2
    wave = chips // 2

    def kernel(c0, c1, s0, s1, *refs):
        ins, (g0, g1, sum_ref, w_ref, sems) = refs[: len(arrays)], refs[len(arrays) :]
        where = position()

        def copy_of(n, i):
            name = pieces[n][1][i]
            row = pl.multiple_of(chip_slot(name, where, False) * size + (n // 2) * half, half)
            return pltpu.make_async_copy(
                ins[n].at[i], w_ref.at[pl.ds(row, half), :], sems.at[n * wave + i]
            )

        waves = [[], []]
        for n in range(4):
            for i, (jy, _, _) in enumerate(pieces[n][1]):
                waves[jy].append(copy_of(n, i))
        for copy in waves[0] + waves[1]:
            copy.start()
        for jy in range(2):
            for copy in waves[jy]:
                copy.wait()
            for j in range(0, wave * size, 256):
                start = pl.multiple_of((where[0] ^ jy) * (wave * size) + j, 256)
                at = pl.ds(start, 256)
                sums = 0.0
                for ct, slope, out in ((c0, s0, g0), (c1, s1, g1)):
                    grad = bdot(ct[...], w_ref[at, :], NT) * slope[:, at].astype(F32)
                    grad = grad.astype(BF)
                    sums = sums + jnp.sum(grad.astype(F32), 0, keepdims=True)
                    out[:, at] = grad
                sum_ref[:, at] = sums

    part = shape_of((2 * ROW, wide))
    return call(
        "back_act",
        kernel,
        [part, part, shape_of((1, wide), F32), shape_of((wide, D))],
        (*cts, *slopes, *arrays),
        [VMEM] * 4 + [ANY] * 4,
        [pltpu.SemaphoreType.DMA((4 * wave,))],
    )


def back_up(grad, weight, dtype):
    def kernel(g_ref, w_ref, out_ref):
        for n in range(0, D, 256):
            out_ref[:, n : n + 256] = bdot(g_ref[...], w_ref[n : n + 256, :], NT).astype(dtype)

    outs = [shape_of((2 * ROW, D), dtype)]
    return call("back_up", kernel, outs, (grad, weight), long=dtype == F32)[0]


def up_grad(normeds, grads, out_own, out_in):
    lists = layout_yxz()
    half, wide = depth() // 2, grads[0].shape[1]
    rows = D // (4 * depth())
    extra = rows // 4

    def kernel(n0, n1, g0, g1, a_ref, b_ref, *outs_and_scratch):
        outs, part_ref = outs_and_scratch[:4], outs_and_scratch[4]
        where = position()
        for out, names in zip(outs, lists):
            for i, name in enumerate(names):
                slot = chip_slot(name, where, False)
                total = (a_ref[slot].astype(F32) + b_ref[slot].astype(F32)).astype(BF)
                out[i, rows:, :D] = total[:extra]
                out[i, rows:, D:] = total[extra:]
        for side in range(2):
            for jy in range(2):
                base = (where[0] ^ jy) * depth() + side * half
                for n in range(0, wide, 512):
                    total = 0.0
                    for normed, grad in ((n0, g0), (n1, g1)):
                        left = jnp.concatenate(
                            [block(normed, base + i, 2 * rows) for i in range(half)], 1
                        )
                        total = total + bdot(left, grad[:, n : n + 512], TN)
                    part_ref[:, :, :, n : n + 512] = total.astype(BF).reshape(half, 2, rows, 512)
                for jx in range(2):
                    for i in range(half):
                        if side == 0:
                            out, at = outs[1 - jy], jx * half + i
                        else:
                            out, at = outs[3 - jx], jy * half + i
                        out[at, :rows] = part_ref[i, where[2] ^ jx]

    outs = [shape_of((len(v), rows + extra, wide)) for v in lists]
    scratch = [pltpu.VMEM((half, 2, rows, wide), BF)]
    return call("up_grad", kernel, outs, (*normeds, *grads, out_own, out_in), None, scratch)


def out_grad(mixed, low):
    chips = 4 * depth()
    rows = D // (2 * chips)
    group = 256 // (2 * rows)

    def kernel(m_ref, l_ref, send_ref, keep_ref):
        core = position()[3]
        for g in range(D // 256):
            at, cols = slice(g * group, (g + 1) * group), slice(g * 256, (g + 1) * 256)
            total = bdot(m_ref[:, cols], l_ref[...], TN).astype(BF).reshape(group, 2, rows, D)
            first, second = total[:, 0], total[:, 1]
            send_ref[at] = jnp.where(core == 0, second, first)
            keep_ref[at] = jnp.where(core == 0, first, second)

    outs = [shape_of((chips, rows, D))] * 2
    return call("out_grad", kernel, outs, (mixed, low))


def back_norm(own, other, hidden, vec, ct, weight):
    def kernel(a_ref, b_ref, h_ref, vec_ref, ct_ref, w_ref, mixed_ref, low_ref, grad_ref, sum_ref):
        first, second = 0.0, 0.0
        for r in range(0, 2 * ROW, ROW):
            rows = slice(r, r + ROW)
            normal, inv = normal_of(h_ref[rows, :])
            grad = a_ref[rows, :] + b_ref[rows, :].astype(F32)
            first = first + jnp.sum(grad * normal, 0, keepdims=True)
            second = second + jnp.sum(grad, 0, keepdims=True)
            total = ct_ref[rows, :].astype(F32) + norm_back(grad, normal, inv, vec_ref[2:3, :])
            grad_ref[rows, :] = total
            low_ref[rows, :] = total.astype(BF)
            mixed_ref[rows, :] = bdot(low_ref[rows, :], w_ref[...], NT).astype(BF)
        sum_ref[0:1, :] = first
        sum_ref[1:2, :] = second

    part = shape_of((2 * ROW, D))
    outs = [part, part, shape_of((2 * ROW, D), F32), shape_of((2, D), F32)]
    return call("back_norm", kernel, outs, (own, other, hidden, vec, ct, weight))


def attn_grad(normed, grads):
    chips = 4 * depth()
    rows = D // (2 * chips)
    group = 256 // (2 * rows)

    def kernel(n_ref, g_ref, send_ref, keep_ref):
        core = position()[3]
        for g in range(D // 256):
            at, cols = slice(g * group, (g + 1) * group), slice(g * 256, (g + 1) * 256)
            for part in range(3):
                total = bdot(n_ref[:, cols], g_ref[part], TN).astype(BF)
                total = total.reshape(group, 2, rows, D)
                first, second = total[:, 0], total[:, 1]
                to = slice(part * D, (part + 1) * D)
                send_ref[at, :, to] = jnp.where(core == 0, second, first)
                keep_ref[at, :, to] = jnp.where(core == 0, first, second)

    outs = [shape_of((chips, rows, 3 * D))] * 2
    return call("attn_grad", kernel, outs, (normed, grads))


def core_sum(own, arrived, sums, sums_in, rel_z):
    lists = layout_yxz()
    chips, rows, wide = own.shape
    lines = sums.shape[0]

    def kernel(a_ref, b_ref, s_ref, t_ref, *rest):
        outs, pad_ref, small_ref = rest[:4], rest[4], rest[5]
        where = position()
        pad_ref[...] = jnp.zeros_like(pad_ref)
        pad_ref[:lines, :] = s_ref[...] + t_ref[...]
        small_ref[...] = jnp.transpose(pad_ref[...]).astype(BF).reshape(chips, 2, rows, 128)
        for out, names in zip(outs, lists):
            for i, name in enumerate(names):
                slot = chip_slot(name, where, rel_z)
                total = a_ref[slot].astype(F32) + b_ref[slot].astype(F32)
                out[i, :, :wide] = total.astype(BF)
                out[i, :, wide:] = small_ref[slot, where[3]]

    outs = [shape_of((len(v), rows, wide + 128)) for v in lists]
    scratch = [pltpu.VMEM((128, D), F32), pltpu.VMEM((chips, 2, rows, 128), BF)]
    return call("core_sum", kernel, outs, (own, arrived, sums, sums_in), None, scratch)


def back_first(grads, weight, resident, vec, hidden_grad):
    def kernel(g_ref, w_ref, x_ref, vec_ref, h_ref, own_ref, send_ref, sum_ref):
        first, second = 0.0, 0.0
        y = position()[0]
        for half, out_ref in ((y, own_ref), (1 - y, send_ref)):
            rows = pl.ds(pl.multiple_of(half * ROW, ROW), ROW)
            normal, inv = normal_of(x_ref[rows, :].astype(F32))
            grad = 0.0
            for part in range(3):
                grad = grad + bdot(g_ref[part, rows, :], w_ref[:, part * D : (part + 1) * D], NT)
            first = first + jnp.sum(grad * normal, 0, keepdims=True)
            second = second + jnp.sum(grad, 0, keepdims=True)
            total = h_ref[rows, :] + norm_back(grad, normal, inv, vec_ref[0:1, :])
            out_ref[...] = total.astype(BF)
        sum_ref[0:1, :] = first
        sum_ref[1:2, :] = second

    outs = [shape_of((ROW, D)), shape_of((ROW, D)), shape_of((2, D), F32)]
    args = (grads, weight, resident, vec, hidden_grad)
    return call("back_first", kernel, outs, args)


def down_back(act, weight, dtype, hidden=None):
    extra = () if hidden is None else (hidden,)

    def kernel(a_ref, w_ref, *refs):
        out_ref = refs[-1]
        for n in range(0, D, 256):
            total = bdot(a_ref[...], w_ref[:, n : n + 256], NN)
            if hidden is not None:
                total = total + refs[0][:, n : n + 256]
            out_ref[:, n : n + 256] = total.astype(dtype)

    outs = [shape_of((2 * ROW, D), dtype)]
    return call("down_back", kernel, outs, (act, weight, *extra))[0]


def result_of(own, other):
    def kernel(a_ref, b_ref, own_ref, send_ref):
        y = position()[0]
        for half, out_ref in ((y, own_ref), (1 - y, send_ref)):
            rows = pl.ds(pl.multiple_of(half * ROW, ROW), ROW)
            out_ref[...] = (a_ref[rows, :] + b_ref[rows, :].astype(F32)).astype(BF)

    return call("result_of", kernel, [shape_of((ROW, D))] * 2, (own, other))


def interleave(own, other):
    rows, wide = own.shape
    size = wide // (4 * depth())

    def kernel(a_ref, b_ref, out_ref):
        core = position()[3]
        for n in range(wide // size):
            cols = slice(n * size, (n + 1) * size)
            for ref, at in ((a_ref, core), (b_ref, 1 - core)):
                to = pl.multiple_of((2 * n + at) * size, size)
                out_ref[:, pl.ds(to, size)] = ref[:, cols]

    return call("interleave", kernel, [shape_of((rows, 2 * wide), F32)], (own, other))[0]


def shards(
    inputs,
    cotangent,
    phone_len,
    prompt_len,
    target_len,
    ln1_gain,
    ln1_bias,
    w_qkv,
    w_out,
    ln2_gain,
    ln2_bias,
    w_up,
    up_bias,
    w_down,
):
    y, z, x, c = position()
    count = depth()
    chips = 4 * count
    row_w = w_qkv.shape[0]
    row_f = w_down.shape[0]

    chain = Chain()

    def split_halves(blocks):
        return (
            lax.dynamic_index_in_dim(blocks, 1 - y, 0, keepdims=False),
            lax.dynamic_index_in_dim(blocks, y, 0, keepdims=False),
        )

    attn_g, up_g, down_g = Gather(chain, True), Gather(chain, False), GatherXZY(chain)
    down_s, up_s, attn_s = ScatterYZX(chain), Scatter(chain, False), Scatter(chain, True)

    vectors = (ln1_gain, ln1_bias, ln2_gain, ln2_bias, up_bias)
    attn_z = attn_g.over_z(chain(pack, w_qkv, w_out, vectors))
    def split_both(inputs, cotangent):
        x_send, x_own = split_halves(inputs)
        ct_send, ct_own = split_halves(cotangent)
        return jnp.stack([x_send, ct_send], 0), x_own, ct_own

    both_send, x_own, ct_own = chain(split_both, inputs[:, 0, 0], cotangent[:, 0, 0])
    both_other = swap(both_send, "y")
    lengths = tuple(
        lax.dynamic_index_in_dim(v, y, 0, keepdims=False)[0]
        for v in (phone_len, prompt_len, target_len)
    )

    def split_up(w_up):
        split = w_up.reshape(row_w, chips, 2, FF // chips // 2)
        return tuple(
            lax.dynamic_index_in_dim(split, i, 2, keepdims=False).reshape(row_w, FF // 2)
            for i in (1 - c, c)
        )

    up_send, up_own = chain(split_up, w_up)
    up_other = swap(up_send, 1)
    up_shard = chain(lambda own, other: ordered(c, own, other, 0), up_own, up_other)
    half_f = row_f // 2

    def join_both(x_own, ct_own, other):
        return ordered(y, x_own, other[0], 0), ordered(y, ct_own, other[1], 0)

    resident, grad_result = chain(join_both, x_own, ct_own, both_other)
    attn_one = attn_g.one(extras=(w_down[:half_f], w_down[half_f:]))
    up_z = up_g.over_z(up_shard, *attn_z)


    attn_two = attn_g.two(extras=(half_f, D))
    early = [(swap(array, 1), rels) for array, rels in attn_g.pieces[::2]]
    down_z = down_g.over_z(attn_g.planes[2], *up_z)
    up_g.one_halves()
    late = [(swap(after(array, *up_g.halves), 1), rels) for array, rels in attn_g.pieces[1::2]]
    up_one = up_g.send(*[v[0] for v in early + late])
    lines = 4 + row_f // row_w
    attn_core = early + late
    many = len(attn_core)

    def unpack_pieces(*arrays):
        own = [(a, p[1]) for a, p in zip(arrays[:many], attn_g.pieces)]
        other = [(a, p[1]) for a, p in zip(arrays[many:], attn_core)]
        return unpack(own, other, attn_g.rel_z, lines)

    qkv_weight, out_weight, vec = chain(
        unpack_pieces, *[p[0] for p in attn_g.pieces + attn_core]
    )
    shift = vec[4:].reshape(row_f // row_w, chips, 2, row_w)
    shift = lax.dynamic_index_in_dim(shift, c, 2, keepdims=False)
    shift = shift.transpose(1, 0, 2).reshape(1, FF // 2)

    normed, qkv = chain(project, resident, vec, qkv_weight)
    up_two = up_g.two()
    mixed, logs = chain(lambda v: attention_forward(v, *lengths), qkv)
    normed_two, hidden = chain(attend, mixed, out_weight, resident, vec)
    ct_sent = swap(grad_result, 1)
    normed_sent = swap(normed_two, 1)

    def with_pieces(step, pieces):
        def run(*args):
            arrays, rest = args[: len(pieces)], args[len(pieces) :]
            return step([(a, p[1]) for a, p in zip(arrays, pieces)], *rest)

        return run

    up_arrays = [p[0] for p in up_g.pieces]
    down_two = down_g.two(*up_two)
    act_own, slope_own, up_weight = chain(
        with_pieces(lambda p, n, s: feed_first(n, p, s), up_g.pieces), *up_arrays, normed_two, shift
    )
    act_other, slope_other = chain(feed_second, normed_sent, up_weight, shift)
    down_sone = down_s.one(
        chain(
            lambda a, b, p, q: down_grad((a, b), (p, q)), act_own, act_other, grad_result, ct_sent
        ),
    )

    pre_own, pre_other, grad_shift, down_weight = chain(
        with_pieces(lambda p, a, b, s, t: back_act((a, b), p, (s, t)), down_g.pieces),
        *[p[0] for p in down_g.pieces],
        grad_result,
        ct_sent,
        slope_own,
        slope_other,
    )
    two_other = swap(chain(lambda g, w: back_up(g, w, BF), pre_other, up_weight), 1)
    two_own = chain(lambda g, w: back_up(g, w, F32), pre_own, up_weight)
    grad_mixed, grad_low, grad_hidden, sums_two = chain(
        back_norm, two_own, two_other, hidden, vec, grad_result, out_weight
    )
    out_send, out_keep = chain(out_grad, mixed, grad_low)
    out_in = swap(out_send, 1)
    down_sz = down_s.over_z()
    up_sone = up_s.one(
        chain(
            lambda a, b, p, q, o, i: up_grad((a, b), (p, q), o, i),
            normed_two,
            normed_sent,
            pre_own,
            pre_other,
            out_keep,
            out_in,
        )
    )
    grads = chain(lambda a, b, v: attention_backward(a, b, v, *lengths), qkv, grad_mixed, logs)
    attn_send, attn_keep = chain(attn_grad, normed, grads)
    attn_in = swap(attn_send, 1)
    gx_own, gx_send, sums_one = chain(back_first, grads, qkv_weight, resident, vec, grad_hidden)

    def small_lines(one, two, shift):
        last = shift.reshape(chips, row_f // row_w, row_w).transpose(1, 0, 2)[:, :, None]
        last = ordered(c, last, jnp.zeros_like(last), 2).reshape(-1, D)
        return jnp.concatenate([one, two, last], 0)

    sums = chain(small_lines, sums_one, sums_two, grad_shift)
    sums_in = swap(sums, 1)
    up_stwo = up_s.two()
    attn_parts = chain(
        lambda a, b, p, q: core_sum(a, b, p, q, attn_s.rel_z), attn_keep, attn_in, sums, sums_in
    )
    attn_sone = attn_s.one(attn_parts, *up_stwo)
    down_sent = swap(chain(lambda a, w: down_back(a, w, BF), act_other, down_weight), 1)
    down_own = chain(lambda a, w, h: down_back(a, w, F32, h), act_own, down_weight, hidden)
    up_sz = up_s.over_z()

    down_sz = down_sz.reshape(4, half_f, D)
    attn_stwo = attn_s.two(extras=(down_sz,))
    res_own, res_send = chain(result_of, down_own, down_sent)
    sum_up = chain(up_s.total, up_sz)
    sum_up = sum_up.reshape(-1, FF // 2)
    out_rows = sum_up[2 * row_w :]
    sum_out = jnp.concatenate([out_rows[:, :D], out_rows[:, D:]], 0)
    up_rows = sum_up[: 2 * row_w].reshape(2, row_w, FF // 2)
    up_mine = lax.dynamic_index_in_dim(up_rows, c, 0, keepdims=False)
    up_theirs = swap(lax.dynamic_index_in_dim(up_rows, 1 - c, 0, keepdims=False), 1)
    attn_sz = attn_s.over_z()
    gx_other = swap(after(gx_send, *attn_stwo), "y")
    out_other = swap(after(res_send, *attn_stwo), "y")

    def sum_of_down(lines, from_x, from_y):
        upper, lower = lines[0], lines[2]
        from_x, from_y = (v[:, 3 * D + 128 :].reshape(half_f, D) for v in (from_x, from_y))
        return jnp.concatenate([plus(upper.astype(F32), from_x), plus(lower.astype(F32), from_y)], 0)

    sum_down = chain(sum_of_down, down_sz, *attn_stwo)

    def home(own, other):
        return ordered(y, own[None], other[None], 0).reshape(MICRO, 1, 1, ROW, D)

    up_final = chain(interleave, up_mine, up_theirs)
    out_stack = chain(home, res_own, out_other)
    grad_stack = chain(lambda own, other: home(own, other).astype(F32), gx_own, gx_other)
    sum_attn = attn_s.total(attn_sz)
    small_sum = sum_attn[:, 3 * D : 3 * D + lines].T.reshape(-1)
    edges = [i * row_w for i in range(5)]
    small_out = [small_sum[a:b] for a, b in zip(edges[:4], edges[1:])]
    return (
        out_stack,
        grad_stack,
        small_out[0],
        small_out[1],
        sum_attn[:, : 3 * D],
        sum_out,
        small_out[2],
        small_out[3],
        up_final.reshape(row_w, FF),
        small_sum[4 * row_w : 4 * row_w + row_f],
        sum_down,
    )


def plain_passed_along(block, axis, distance):
    devices = range(lax.axis_size(axis))
    route = [(i - distance, i) for i in devices if i - distance in devices]
    return lax.ppermute(block, axis, route)


def plain_times_transposed(left, right):
    return lax.dot_general(
        left, right, (((1,), (1,)), ((), ())), preferred_element_type=jnp.float32
    )


def plain_transposed_times(left, right):
    return lax.dot_general(
        left, right, (((0,), (0,)), ((), ())), preferred_element_type=jnp.float32
    )


def plain_layer_norm(values, gain, bias):
    center = values - jnp.mean(values, -1, keepdims=True)
    spread = jnp.mean(center * center, -1, keepdims=True)
    return center * lax.rsqrt(spread + 1e-05) * gain + bias


def plain_locate(lengths, slot_ids):
    count = jnp.arange(lengths.shape[0])
    seg_ends = jnp.sum(jnp.where(count[None, :] <= count[:, None], lengths[None, :], 0), 1, dtype=jnp.int32)
    seg_ids = jnp.sum(
        (slot_ids[:, None] >= seg_ends[None, :]).astype(jnp.int32), 1, dtype=jnp.int32
    )
    one_hot = (seg_ids[:, None] == jnp.arange(lengths.shape[0], dtype=jnp.int32)[None, :]).astype(
        jnp.int32
    )
    seg_start = jnp.sum(one_hot * (seg_ends - lengths)[None, :], 1, dtype=jnp.int32)
    return (seg_ids, one_hot, slot_ids - seg_start)


def plain_frame_meta(phone_lens, prompt_lens, target_lens, slot_count):
    slot_ids = jnp.arange(slot_count, dtype=jnp.int32)
    pre_seg, pre_hot, pre_off = plain_locate(phone_lens + prompt_lens, slot_ids)
    pre_phone = jnp.sum(pre_hot * phone_lens[None, :], 1, dtype=jnp.int32)
    prefix = (pre_seg, pre_off < pre_phone, pre_off - pre_phone)
    tgt_seg, tgt_hot, tgt_off = plain_locate(target_lens, slot_ids)
    tgt_pos = jnp.sum(tgt_hot * prompt_lens[None, :], 1, dtype=jnp.int32) + tgt_off
    targets = (tgt_seg, tgt_off < 0, tgt_pos)
    return (prefix, targets)


def plain_allowed(query_meta, key_meta):
    same_seg = query_meta[0][:, None] == key_meta[0][None, :]
    audio_ok = key_meta[1][None, :] | (key_meta[2][None, :] <= query_meta[2][:, None])
    return same_seg & jnp.where(query_meta[1][:, None], key_meta[1][None, :], audio_ok)


def plain_masked_scores(queries, key_rows, allowed_mask, score_scale):
    scores = (
        jnp.einsum("qhd,khd->hqk", queries, key_rows, preferred_element_type=jnp.float32)
        * score_scale
    )
    return jnp.where(allowed_mask[None], scores, -1e30)


def plain_attention_forward(queries, key_rows, value_rows, allowed_mask, score_scale):
    scores = plain_masked_scores(queries, key_rows, allowed_mask, score_scale)
    peak = jnp.max(scores, -1, keepdims=True)
    exp_scores = jnp.exp(scores - peak)
    row_total = jnp.sum(exp_scores, -1, keepdims=True)
    probs = (exp_scores / row_total).astype(jnp.bfloat16)
    mixed = jnp.einsum("hqk,khd->qhd", probs, value_rows, preferred_element_type=jnp.float32)
    return (mixed.astype(jnp.bfloat16), peak + jnp.log(row_total))


def plain_attention_backward(
    queries, key_rows, value_rows, allowed_mask, log_total, grad_mixed, score_scale
):
    scores = plain_masked_scores(queries, key_rows, allowed_mask, score_scale)
    probs = jnp.where(allowed_mask[None], jnp.exp(scores - log_total), 0.0)
    grad_probs = jnp.einsum(
        "qhd,khd->hqk", grad_mixed, value_rows, preferred_element_type=jnp.float32
    )
    grad_values = jnp.einsum(
        "hqk,qhd->khd", probs.astype(jnp.bfloat16), grad_mixed, preferred_element_type=jnp.float32
    )
    inner = jnp.sum(grad_probs * probs, -1, keepdims=True)
    grad_scores = (probs * (grad_probs - inner)).astype(jnp.bfloat16)
    grad_queries = (
        jnp.einsum("hqk,khd->qhd", grad_scores, key_rows, preferred_element_type=jnp.float32)
        * score_scale
    )
    grad_keys = (
        jnp.einsum("hqk,qhd->khd", grad_scores, queries, preferred_element_type=jnp.float32)
        * score_scale
    )
    return (grad_queries, grad_keys, grad_values)


def plain_add_up(summed, fresh):
    if summed is None:
        return fresh
    return jax.tree.map(lambda summed_part, fresh_part: summed_part + fresh_part, summed, fresh)


def plain_fetch_forward(params):
    return (
        lax.all_gather(params[0], ("pair", "rows"), axis=0, tiled=True),
        lax.all_gather(params[1], ("pair", "rows"), axis=0, tiled=True),
        lax.all_gather(params[2], ("pair", "rows"), axis=0, tiled=True),
        lax.all_gather(params[3], ("pair", "rows"), axis=0, tiled=True),
        lax.all_gather(params[4], ("pair", "rows"), axis=0, tiled=True),
        lax.all_gather(params[5], ("pair", "rows"), axis=0, tiled=True),
        lax.all_gather(params[6], ("pair", "rows"), axis=0, tiled=True),
        lax.all_gather(params[7], ("pair", "rows"), axis=0, tiled=True),
        lax.all_gather(params[8], ("pair", "rows"), axis=0, tiled=True),
    )


def plain_shards(
    inputs,
    cotangent,
    phone_len,
    prompt_len,
    target_len,
    ln1_gain,
    ln1_bias,
    w_qkv,
    w_out,
    ln2_gain,
    ln2_bias,
    w_up,
    up_bias,
    w_down,
):
    half_index = lax.axis_index("pair")
    score_scale = HEAD ** (-0.5)
    params = (ln1_gain, ln1_bias, w_qkv, w_out, ln2_gain, ln2_bias, w_up, up_bias, w_down)
    out_blocks = []
    grad_blocks = []
    summed = None
    for batch_index in range(MICRO):
        gathered = plain_fetch_forward(params)
        (
            gain_one,
            bias_one,
            qkv_weight,
            out_weight,
            gain_two,
            bias_two,
            up_weight,
            up_shift,
            down_weight,
        ) = gathered
        gain_one_f = gain_one.astype(jnp.float32)
        bias_one_f = bias_one.astype(jnp.float32)
        gain_two_f = gain_two.astype(jnp.float32)
        bias_two_f = bias_two.astype(jnp.float32)
        prefix, targets = plain_frame_meta(
            phone_len[batch_index, 0], prompt_len[batch_index, 0], target_len[batch_index, 0], ROW
        )
        query_meta = tuple(
            (
                jnp.where(half_index == 0, pre_field, tgt_field)
                for pre_field, tgt_field in zip(prefix, targets)
            )
        )
        remote_mask = plain_allowed(query_meta, prefix) & (half_index == 1)
        allowed_mask = jnp.concatenate([remote_mask, plain_allowed(query_meta, query_meta)], 1)
        resident = inputs[batch_index, 0, 0].astype(jnp.float32)
        normed = plain_layer_norm(resident, gain_one_f, bias_one_f).astype(jnp.bfloat16)
        qkv_rows = jnp.dot(normed, qkv_weight, preferred_element_type=jnp.float32).astype(
            jnp.bfloat16
        )
        own_kv = qkv_rows[:, D:]
        remote_kv = plain_passed_along(own_kv, "pair", 1)
        queries = qkv_rows[:, :D].reshape(ROW, HEADS, HEAD)
        key_rows = jnp.concatenate([remote_kv[:, :D], own_kv[:, :D]], 0).reshape(
            2 * ROW, HEADS, HEAD
        )
        value_rows = jnp.concatenate([remote_kv[:, D:], own_kv[:, D:]], 0).reshape(
            2 * ROW, HEADS, HEAD
        )
        mixed, log_total = plain_attention_forward(
            queries, key_rows, value_rows, allowed_mask, score_scale
        )
        mixed_flat = mixed.reshape(ROW, D)
        hidden_res = resident + jnp.dot(mixed_flat, out_weight, preferred_element_type=jnp.float32)
        normed_two = plain_layer_norm(hidden_res, gain_two_f, bias_two_f).astype(jnp.bfloat16)
        pre_act = jnp.dot(
            normed_two, up_weight, preferred_element_type=jnp.float32
        ) + up_shift.astype(jnp.float32)
        activ = jax.nn.gelu(pre_act, approximate=True).astype(jnp.bfloat16)
        result = hidden_res + jnp.dot(activ, down_weight, preferred_element_type=jnp.float32)
        out_blocks.append(result.astype(jnp.bfloat16))
        gathered = (
            lax.all_gather(params[0], ("pair", "rows"), axis=0, tiled=True),
            lax.all_gather(params[1], ("pair", "rows"), axis=0, tiled=True),
            lax.all_gather(params[2], ("pair", "rows"), axis=0, tiled=True),
            lax.all_gather(params[3], ("pair", "rows"), axis=0, tiled=True),
            lax.all_gather(params[4], ("pair", "rows"), axis=0, tiled=True),
            lax.all_gather(params[5], ("pair", "rows"), axis=0, tiled=True),
            lax.all_gather(params[6], ("pair", "rows"), axis=0, tiled=True),
            lax.all_gather(params[7], ("pair", "rows"), axis=0, tiled=True),
            lax.all_gather(params[8], ("pair", "rows"), axis=0, tiled=True),
        )
        (
            gain_one,
            bias_one,
            qkv_weight,
            out_weight,
            gain_two,
            bias_two,
            up_weight,
            up_shift,
            down_weight,
        ) = gathered
        gain_one_f = gain_one.astype(jnp.float32)
        bias_one_f = bias_one.astype(jnp.float32)
        gain_two_f = gain_two.astype(jnp.float32)
        bias_two_f = bias_two.astype(jnp.float32)
        grad_result = cotangent[batch_index, 0, 0]
        grad_down = plain_transposed_times(activ, grad_result)
        grad_activ = plain_times_transposed(grad_result, down_weight)
        _, gelu_back = jax.vjp(lambda pre_value: jax.nn.gelu(pre_value, approximate=True), pre_act)
        grad_pre = gelu_back(grad_activ)[0].astype(jnp.bfloat16)
        grad_up = plain_transposed_times(normed_two, grad_pre)
        grad_up_bias = jnp.sum(grad_pre.astype(jnp.float32), 0)
        grad_normed_two = plain_times_transposed(grad_pre, up_weight)
        _, norm_back_two = jax.vjp(plain_layer_norm, hidden_res, gain_two_f, bias_two_f)
        grad_hidden_ln, grad_gain_two, grad_bias_two = norm_back_two(grad_normed_two)
        grad_hidden = grad_result.astype(jnp.float32) + grad_hidden_ln
        grad_hidden_low = grad_hidden.astype(jnp.bfloat16)
        grad_out_w = plain_transposed_times(mixed_flat, grad_hidden_low)
        grad_mixed = (
            plain_times_transposed(grad_hidden_low, out_weight)
            .astype(jnp.bfloat16)
            .reshape(ROW, HEADS, HEAD)
        )
        grad_queries, grad_keys, grad_values = plain_attention_backward(
            queries, key_rows, value_rows, allowed_mask, log_total, grad_mixed, score_scale
        )
        remote_grads = jnp.concatenate(
            [grad_keys[:ROW].reshape(ROW, D), grad_values[:ROW].reshape(ROW, D)], 1
        )
        returned = plain_passed_along(remote_grads.astype(jnp.bfloat16), "pair", -1).astype(
            remote_grads.dtype
        )
        grad_qkv_rows = jnp.concatenate(
            [
                grad_queries.reshape(ROW, D),
                grad_keys[ROW:].reshape(ROW, D) + returned[:, :D],
                grad_values[ROW:].reshape(ROW, D) + returned[:, D:],
            ],
            1,
        ).astype(jnp.bfloat16)
        grad_qkv_w = plain_transposed_times(normed, grad_qkv_rows)
        grad_normed = plain_times_transposed(grad_qkv_rows, qkv_weight)
        _, norm_back_one = jax.vjp(plain_layer_norm, resident, gain_one_f, bias_one_f)
        grad_resident_ln, grad_gain_one, grad_bias_one = norm_back_one(grad_normed)
        grad_blocks.append(grad_hidden + grad_resident_ln)
        local_grads = (
            grad_gain_one,
            grad_bias_one,
            grad_qkv_w,
            grad_out_w,
            grad_gain_two,
            grad_bias_two,
            grad_up,
            grad_up_bias,
            grad_down,
        )
        shard_part = (
            lax.psum_scatter(local_grads[0], ("pair", "rows"), scatter_dimension=0, tiled=True),
            lax.psum_scatter(local_grads[1], ("pair", "rows"), scatter_dimension=0, tiled=True),
            lax.psum_scatter(local_grads[2], ("pair", "rows"), scatter_dimension=0, tiled=True),
            lax.psum_scatter(local_grads[3], ("pair", "rows"), scatter_dimension=0, tiled=True),
            lax.psum_scatter(local_grads[4], ("pair", "rows"), scatter_dimension=0, tiled=True),
            lax.psum_scatter(local_grads[5], ("pair", "rows"), scatter_dimension=0, tiled=True),
            lax.psum_scatter(local_grads[6], ("pair", "rows"), scatter_dimension=0, tiled=True),
            lax.psum_scatter(local_grads[7], ("pair", "rows"), scatter_dimension=0, tiled=True),
            lax.psum_scatter(local_grads[8], ("pair", "rows"), scatter_dimension=0, tiled=True),
        )
        summed = plain_add_up(summed, shard_part)
    block_shape = (MICRO, 1, 1, ROW, D)
    out_stack = jnp.stack(out_blocks, 0).reshape(block_shape)
    grad_stack = jnp.stack(grad_blocks, 0).reshape(block_shape)
    return (
        out_stack,
        grad_stack,
        summed[0],
        summed[1],
        summed[2],
        summed[3],
        summed[4],
        summed[5],
        summed[6],
        summed[7],
        summed[8],
    )


def solution(mesh):
    rows = P(None, "rows", "pair", None, None)
    line = P(("pair", "rows"))
    flat = P(("pair", "rows"), None)
    lens = P(None, "rows", None)
    return jax.shard_map(
        shards if mesh.shape["rows"] == 16 else plain_shards,
        mesh=mesh,
        in_specs=(rows, rows, lens, lens, lens, line, line, flat, flat, line, line, flat, line, flat),
        out_specs=(rows, rows, line, line, flat, flat, line, line, flat, line, flat),
        check_vma=False,
    )
```

```python
import functools

import jax
import jax.numpy as jnp
from jax import lax
from jax.experimental import pallas as pl
from jax.experimental.pallas import tpu as pltpu
from jax.sharding import PartitionSpec as P

D = 1024
HEADS = 16
HEAD = 64
FF = 4096
ROW = 256
MICRO = 2
BF = jnp.bfloat16
F32 = jnp.float32
NEG = -1e30


def position():
    row = lax.axis_index("rows")
    return lax.axis_index("pair"), row // 4, (row // 2) % 2, row % 2


def depth():
    return lax.axis_size("rows") // 4


def swap(block, way):
    if way == "y":
        return lax.ppermute(block, "pair", [(i, i ^ 1) for i in range(2)])
    count = lax.axis_size("rows")
    return lax.ppermute(block, "rows", [(i, i ^ way) for i in range(count)])


def after(block, *others):
    return lax.optimization_barrier((block, *others))[0]


class Chain:
    def __init__(self):
        self.last = None

    def __call__(self, step, *args):
        if self.last is not None:
            args, _ = lax.optimization_barrier((args, self.last))
        out = step(*args)
        self.last = out
        return out


def z_groups():
    count = lax.axis_size("rows")
    return [[z * 4 + low for z in range(count // 4)] for low in range(4)]


def z_gather(block):
    return lax.all_gather(block, "rows", axis_index_groups=z_groups())


def z_scatter(column):
    return lax.psum_scatter(column, "rows", scatter_dimension=0, axis_index_groups=z_groups())


def join_planes(left, left_in, right, right_in):
    half, rows, cols = left.shape

    def kernel(a_ref, b_ref, c_ref, d_ref, left_ref, right_ref):
        left_ref[0] = a_ref[0]
        left_ref[1] = b_ref[0]
        right_ref[0] = c_ref[0]
        right_ref[1] = d_ref[0]

    part = pl.BlockSpec((1, rows, cols), lambda i: (i, 0, 0))
    both = pl.BlockSpec((2, None, rows, cols), lambda i: (0, i, 0, 0))
    made = pl.pallas_call(
        kernel,
        grid=(half,),
        out_shape=[jax.ShapeDtypeStruct((2, half, rows, cols), BF)] * 2,
        in_specs=[part] * 4,
        out_specs=[both] * 2,
        compiler_params=pltpu.CompilerParams(vmem_limit_bytes=16 << 20),
        cost_estimate=pl.CostEstimate(flops=1 << 20, bytes_accessed=1 << 10, transcendentals=0),
        name="join_planes",
    )(left, left_in, right, right_in)
    return [v.reshape(2 * half, rows, cols) for v in made]


class Gather:
    def __init__(self, chain, by_permutes):
        self.chain = chain
        self.rel_z = by_permutes and depth() == 4

    def over_z(self, block, *first):
        block = after(block, *first)
        if self.rel_z:
            self.column = [block[None]] + [swap(block[None], 4 * k) for k in range(1, 4)]
            return self.column[1:]
        self.column = [z_gather(block)]
        return self.column

    def one(self, *first, extras=()):
        half = depth() // 2

        def halves(column, extras):
            if self.rel_z:
                left, right = jnp.concatenate(column[:2], 0), jnp.concatenate(column[2:], 0)
            else:
                left, right = column[0][:half], column[0][half:]
            return beside((left, right), extras)

        self.halves = self.chain(halves, self.column, extras)
        return self.send(*first)

    def one_halves(self):
        half = depth() // 2
        self.halves = self.chain(lambda v: (v[:half], v[half:]), self.column[0])

    def send(self, *first):
        left, right = lax.optimization_barrier((self.halves, first))[0]
        self.sides = swap(left, 2), swap(right, "y")
        return list(self.sides)

    def two(self, *first, extras=()):
        rows, cols = self.column[0].shape[-2:]
        block = (depth() // 2, rows, cols)

        def planes(halves, sides):
            left, right = halves
            left_x, right_y = sides
            if not extras:
                return join_planes(left, left_x, right, right_y)
            main = [v[:, :cols].reshape(block) for v in (left, left_x, right, right_y)]
            more = [v[:, cols:].reshape(extras) for v in (left, left_x, right, right_y)]
            return (
                jnp.concatenate(main[:2], 0),
                jnp.concatenate(main[2:], 0),
                jnp.stack(more, 0),
            )

        sides = lax.optimization_barrier((self.sides, first))[0]
        self.planes = self.chain(planes, self.halves, sides)
        left, right = self.planes[:2]
        left_y, right_x = swap(left, "y"), swap(right, 2)
        half = depth() // 2
        low, high = range(half), range(half, 2 * half)
        self.pieces = [
            (left, [(0, i, 0) for i in low] + [(0, i, 1) for i in low]),
            (left_y, [(1, i, 0) for i in low] + [(1, i, 1) for i in low]),
            (right, [(0, i, 0) for i in high] + [(1, i, 0) for i in high]),
            (right_x, [(0, i, 1) for i in high] + [(1, i, 1) for i in high]),
        ]
        return [left_y, right_x]


def beside(blocks, extras):
    if not extras:
        return tuple(blocks)
    out = []
    for block, extra in zip(blocks, extras):
        rows = block.shape[0] * block.shape[1]
        out.append(
            jnp.concatenate([block.reshape(rows, -1), extra.reshape(rows, -1)], 1)
        )
    return tuple(out)


class GatherXZY:
    def __init__(self, chain):
        self.chain = chain

    def over_z(self, lines, *first):
        self.column = z_gather(after(lines, *first))
        return self.column

    def two(self, *first):
        def cut(column):
            shape = (2 * depth(), *column.shape[2:])
            return column[:, :2].reshape(shape), column[:, 2:].reshape(shape)

        upper, lower = self.chain(cut, after(self.column, *first))
        upper_y, lower_x = swap(upper, "y"), swap(lower, 2)
        ids = range(depth())
        self.pieces = [
            (upper, [(0, i, j) for i in ids for j in range(2)]),
            (upper_y, [(1, i, j) for i in ids for j in range(2)]),
            (lower, [(j, i, 0) for i in ids for j in range(2)]),
            (lower_x, [(j, i, 1) for i in ids for j in range(2)]),
        ]
        return [upper_y, lower_x]


def chip_slot(chip, where, rel_z):
    jy, jz, jx = chip
    y, z, x, _ = where
    z_at = (z ^ jz) if rel_z else jz
    return ((y ^ jy) * depth() + z_at) * 2 + (x ^ jx)


def layout_yzx():
    ids = range(depth())
    return [
        [(1, i, j) for i in ids for j in range(2)],
        [(0, i, j) for i in ids for j in range(2)],
        [(j, i, 1) for i in ids for j in range(2)],
        [(j, i, 0) for i in ids for j in range(2)],
    ]


def layout_yxz():
    half = depth() // 2
    low, high = range(half), range(half, 2 * half)
    return [
        [(1, i, j) for j in range(2) for i in low],
        [(0, i, j) for j in range(2) for i in low],
        [(j, i, 1) for j in range(2) for i in high],
        [(j, i, 0) for j in range(2) for i in high],
    ]


def plus(left, right):
    return (left.astype(F32) + right.astype(F32)).astype(left.dtype)


def add_halves(left, left_in, right, right_in, extras):
    count, rows, cols = left.shape
    half = count // 2
    more = extras[0].shape[2] if extras else 0
    extras = list(extras) * 2

    def kernel(*refs):
        ins, outs = refs[: 8 + len(extras)], refs[8 + len(extras) :]
        for side in range(2):
            a, b, c, d = ins[4 * side : 4 * side + 4]
            own, send = outs[2 + side], outs[side]
            own[...] = (a[...].astype(F32) + b[...].astype(F32)).astype(BF)
            total = (c[0].astype(F32) + d[0].astype(F32)).astype(BF)
            if extras:
                send[:, :cols] = total
                send[:, cols:] = ins[8 + side][0]
            else:
                send[0] = total

    low = pl.BlockSpec((1, rows, cols), lambda i: (i, 0, 0))
    high = pl.BlockSpec((1, rows, cols), lambda i: (i + half, 0, 0))
    wide = pl.BlockSpec((rows, cols + more), lambda i: (i, 0))
    send = jax.ShapeDtypeStruct((half * rows, cols + more) if extras else (half, rows, cols), BF)
    own = jax.ShapeDtypeStruct((half, rows, cols), BF)
    return pl.pallas_call(
        kernel,
        grid=(half,),
        out_shape=[send, send, own, own],
        in_specs=[low, low, high, high] * 2
        + [pl.BlockSpec((1, rows, more), lambda i, n=n: (n, i, 0)) for n in (1, 3)[: len(extras)]],
        out_specs=[wide if extras else low] * 2 + [low] * 2,
        compiler_params=pltpu.CompilerParams(vmem_limit_bytes=16 << 20),
        cost_estimate=pl.CostEstimate(flops=1 << 35, bytes_accessed=1 << 10, transcendentals=0),
        name="add_halves",
    )(left, left_in, left, left_in, right, right_in, right, right_in, *extras)


def add_column(left, left_in, right, right_in):
    half, rows, cols = left.shape

    def kernel(a_ref, b_ref, c_ref, d_ref, out_ref):
        out_ref[0] = (a_ref[0].astype(F32) + b_ref[0].astype(F32)).astype(BF)
        out_ref[1] = (c_ref[0].astype(F32) + d_ref[0].astype(F32)).astype(BF)

    part = pl.BlockSpec((1, rows, cols), lambda i: (i, 0, 0))
    return pl.pallas_call(
        kernel,
        grid=(half,),
        out_shape=jax.ShapeDtypeStruct((2, half, rows, cols), BF),
        in_specs=[part] * 4,
        out_specs=pl.BlockSpec((2, None, rows, cols), lambda i: (0, i, 0, 0)),
        compiler_params=pltpu.CompilerParams(vmem_limit_bytes=16 << 20),
        cost_estimate=pl.CostEstimate(flops=1 << 20, bytes_accessed=1 << 10, transcendentals=0),
        name="add_column",
    )(left, left_in, right, right_in).reshape(2 * half, rows, cols)


class Scatter:
    def __init__(self, chain, by_permutes):
        self.chain = chain
        self.rel_z = by_permutes and depth() == 4

    def one(self, parts, *first):
        self.parts = parts
        left, _, right, _ = parts
        self.sides = swap(after(left, *first), "y"), swap(after(right, *first), 2)
        return list(self.sides)

    def two(self, *first, extras=()):
        _, left, _, right = self.parts
        left_in, right_in = lax.optimization_barrier((self.sides, first))[0]
        self.sums = self.chain(add_halves, left, left_in, right, right_in, extras)
        self.ends = swap(self.sums[0], 2), swap(self.sums[1], "y")
        return list(self.ends)

    def over_z(self, *first):
        _, _, left, right = self.sums
        left_in, right_in = self.ends

        def add(left, left_in, right, right_in):
            left_in, right_in = (
                v if v.ndim == 3 else v[:, : left.shape[2]].reshape(left.shape)
                for v in (left_in, right_in)
            )
            if self.rel_z:
                return (
                    plus(left[1], left_in[1]),
                    *plus(right, right_in),
                    left[0].astype(F32) + left_in[0].astype(F32),
                )
            return add_column(left, left_in, right, right_in)

        made = self.chain(add, left, left_in, right, right_in)
        if not self.rel_z:
            return z_scatter(after(made, *first))
        one, two, three, own = made
        return own, swap(one, 4), swap(two, 8), swap(three, 12)

    def total(self, parts):
        if not self.rel_z:
            return parts.astype(F32)
        own, *arrived = parts

        def add(own, *arrived):
            for part in arrived:
                own = own + part.astype(F32)
            return own

        return self.chain(add, own, *arrived)


class ScatterYZX:
    def __init__(self, chain):
        self.chain = chain

    def one(self, parts, *first):
        self.parts = parts
        left, _, right, _ = parts
        self.sides = swap(after(left, *first), "y"), swap(after(right, *first), 2)
        return list(self.sides)

    def over_z(self, *first):
        def add(left, left_in, right, right_in):
            shape = (depth(), 2, *left.shape[1:])
            upper, lower = plus(left, left_in).reshape(shape), plus(right, right_in).reshape(shape)
            return jnp.concatenate([upper, lower], 1)

        _, left, _, right = self.parts
        self.lines = z_scatter(self.chain(add, left, self.sides[0], right, self.sides[1]))
        return self.lines


def ordered(flag, own, other, axis):
    return jnp.where(
        flag == 0,
        jnp.concatenate([own, other], axis),
        jnp.concatenate([other, own], axis),
    )


def frames(index, phone, prompt, target, segs):
    pre_end = ends_of([phone[s] + prompt[s] for s in range(segs)])
    tgt_end = ends_of([target[s] for s in range(segs)])
    is_target = index >= ROW
    local = jnp.where(is_target, index - ROW, index)
    seg = jnp.zeros_like(index)
    for s in range(segs):
        edge = jnp.where(is_target, tgt_end[s], pre_end[s])
        seg = seg + jnp.where(local >= edge, 1, 0)
    start = jnp.zeros_like(index)
    phones = jnp.zeros_like(index)
    prompts = jnp.zeros_like(index)
    for s in range(segs):
        pick = seg == s
        pre_start = pre_end[s] - phone[s] - prompt[s]
        tgt_start = tgt_end[s] - target[s]
        start = jnp.where(pick, jnp.where(is_target, tgt_start, pre_start), start)
        phones = jnp.where(pick, phone[s], phones)
        prompts = jnp.where(pick, prompt[s], prompts)
    off = local - start
    is_phone = jnp.where(is_target, 0, jnp.where(off < phones, 1, 0))
    pos = jnp.where(is_target, prompts + off, off - phones)
    return seg, is_phone, pos


def ends_of(lengths):
    out, total = [], 0
    for length in lengths:
        total = total + length
        out.append(total)
    return out


def bias_of(query, key):
    q_seg, q_phone, q_pos = query
    k_seg, k_phone, k_pos = key
    audio = (k_phone == 1) | (k_pos <= q_pos)
    good = (q_seg == k_seg) & (((q_phone == 1) & (k_phone == 1)) | ((q_phone == 0) & audio))
    return jnp.where(good, 0.0, NEG)


def bdot(left, right, dims):
    return lax.dot_general(left, right, (dims, ((), ())), preferred_element_type=F32)


NT = ((1,), (1,))
NN = ((1,), (0,))
TN = ((0,), (0,))


def attention_forward(qkv, phone, prompt, target):
    segs = phone.shape[0]
    group = 2

    def kernel(
        phone_ref, prompt_ref, target_ref, q_ref, k_ref, v_ref, out_ref, log_ref, bias_ref
    ):
        @pl.when(pl.program_id(0) == 0)
        def _():
            ph = [phone_ref[s] for s in range(segs)]
            pr = [prompt_ref[s] for s in range(segs)]
            tg = [target_ref[s] for s in range(segs)]
            rows = lax.broadcasted_iota(jnp.int32, (2 * ROW, 1), 0)
            cols = lax.broadcasted_iota(jnp.int32, (1, 2 * ROW), 1)
            bias_ref[...] = bias_of(
                frames(cols, ph, pr, tg, segs), frames(rows, ph, pr, tg, segs)
            )

        lane = lax.broadcasted_iota(jnp.int32, (1, 2 * HEAD), 1)
        zero = jnp.zeros((), BF)
        scale = jnp.asarray(HEAD**-0.5, BF)
        for pair in range(group):
            cols = slice(pair * 2 * HEAD, (pair + 1) * 2 * HEAD)
            for rows, keys in ((0, ROW), (ROW, 2 * ROW)):
                at = slice(rows, rows + ROW)
                outs = []
                for j in range(2):
                    q = jnp.where((lane // HEAD) == j, q_ref[at, cols] * scale, zero)
                    s = bdot(k_ref[:keys, cols], q, NT) + bias_ref[:keys, at]
                    peak = jnp.max(s, 0, keepdims=True)
                    e = jnp.exp(s - peak)
                    total = jnp.sum(e, 0, keepdims=True)
                    log_ref[0, 2 * pair + j : 2 * pair + j + 1, at] = peak + jnp.log(total)
                    p = (e * (1.0 / total)).astype(BF)
                    outs.append(bdot(v_ref[:keys, cols], p, TN)[j * HEAD : (j + 1) * HEAD])
                out_ref[at, cols] = jnp.transpose(jnp.concatenate(outs, 0)).astype(BF)

    steps = HEADS // 2 // group
    smem = pl.BlockSpec(memory_space=pltpu.SMEM)
    part = (2 * ROW, 2 * HEAD * group)
    return pl.pallas_call(
        kernel,
        grid=(steps,),
        out_shape=[
            jax.ShapeDtypeStruct((2 * ROW, D), BF),
            jax.ShapeDtypeStruct((steps, 2 * group, 2 * ROW), F32),
        ],
        in_specs=[
            smem,
            smem,
            smem,
            pl.BlockSpec(part, lambda h: (0, h)),
            pl.BlockSpec(part, lambda h: (0, h + steps)),
            pl.BlockSpec(part, lambda h: (0, h + 2 * steps)),
        ],
        out_specs=[
            pl.BlockSpec(part, lambda h: (0, h)),
            pl.BlockSpec((1, 2 * group, 2 * ROW), lambda h: (h, 0, 0)),
        ],
        scratch_shapes=[pltpu.VMEM((2 * ROW, 2 * ROW), F32)],
        compiler_params=pltpu.CompilerParams(vmem_limit_bytes=16 << 20),
        cost_estimate=pl.CostEstimate(flops=1 << 20, bytes_accessed=1 << 10, transcendentals=0),
        name="attention_forward",
    )(phone, prompt, target, qkv, qkv, qkv)


def attention_backward(qkv, grad_mixed, logs, phone, prompt, target):
    segs = phone.shape[0]
    group = 2

    def kernel(
        phone_ref, prompt_ref, target_ref, q_ref, k_ref, v_ref, g_ref, log_ref, out_ref, bias_ref
    ):
        @pl.when(pl.program_id(0) == 0)
        def _():
            ph = [phone_ref[s] for s in range(segs)]
            pr = [prompt_ref[s] for s in range(segs)]
            tg = [target_ref[s] for s in range(segs)]
            rows = lax.broadcasted_iota(jnp.int32, (2 * ROW, 1), 0)
            cols = lax.broadcasted_iota(jnp.int32, (1, 2 * ROW), 1)
            bias_ref[...] = bias_of(
                frames(cols, ph, pr, tg, segs), frames(rows, ph, pr, tg, segs)
            )

        lane = lax.broadcasted_iota(jnp.int32, (1, 2 * HEAD), 1)
        zero = jnp.zeros((), BF)
        scale = HEAD**-0.5
        for pair in range(group):
            cols = slice(pair * 2 * HEAD, (pair + 1) * 2 * HEAD)
            dks, dvs = {}, {}
            for rows, keys in ((0, ROW), (ROW, 2 * ROW)):
                at = slice(rows, rows + ROW)
                dqs = []
                for j in range(2):
                    sel = (lane // HEAD) == j
                    q_all, g_all = q_ref[at, cols], g_ref[at, cols]
                    q = jnp.where(sel, q_all * jnp.asarray(scale, BF), zero)
                    g = jnp.where(sel, g_all, zero)
                    k, v = k_ref[:keys, cols], v_ref[:keys, cols]
                    s = bdot(k, q, NT) + bias_ref[:keys, at]
                    dp = bdot(v, g, NT)
                    p = jnp.exp(s - log_ref[0, 2 * pair + j : 2 * pair + j + 1, at])
                    inner = jnp.sum(dp * p, 0, keepdims=True)
                    ds = (p * (dp - inner)).astype(BF)
                    dvs[rows, j] = bdot(p.astype(BF), g_all, NN)
                    dks[rows, j] = bdot(ds, q_all, NN)
                    dqs.append(bdot(k, ds, TN)[j * HEAD : (j + 1) * HEAD])
                dq = jnp.transpose(jnp.concatenate(dqs, 0)) * scale
                out_ref[0, at, cols] = dq.astype(BF)
            low = lane < HEAD
            for place, part, factor in ((1, dks, scale), (2, dvs, 1.0)):
                early = jnp.where(low, part[0, 0], part[0, 1])
                late = jnp.where(low, part[ROW, 0], part[ROW, 1])
                out_ref[place, :ROW, cols] = ((early + late[:ROW]) * factor).astype(BF)
                out_ref[place, ROW:, cols] = (late[ROW:] * factor).astype(BF)

    steps = HEADS // 2 // group
    smem = pl.BlockSpec(memory_space=pltpu.SMEM)
    block = (2 * ROW, 2 * HEAD * group)
    return pl.pallas_call(
        kernel,
        grid=(steps,),
        out_shape=jax.ShapeDtypeStruct((3, 2 * ROW, D), BF),
        in_specs=[
            smem,
            smem,
            smem,
            pl.BlockSpec(block, lambda h: (0, h)),
            pl.BlockSpec(block, lambda h: (0, h + steps)),
            pl.BlockSpec(block, lambda h: (0, h + 2 * steps)),
            pl.BlockSpec(block, lambda h: (0, h)),
            pl.BlockSpec((1, 2 * group, 2 * ROW), lambda h: (h, 0, 0)),
        ],
        out_specs=pl.BlockSpec((3, *block), lambda h: (0, 0, h)),
        scratch_shapes=[pltpu.VMEM((2 * ROW, 2 * ROW), F32)],
        compiler_params=pltpu.CompilerParams(vmem_limit_bytes=16 << 20),
        cost_estimate=pl.CostEstimate(flops=1 << 20, bytes_accessed=1 << 10, transcendentals=0),
        name="attention_backward",
    )(phone, prompt, target, qkv, qkv, qkv, grad_mixed, logs)


VMEM = pl.BlockSpec(memory_space=pltpu.VMEM)
SMEM = pl.BlockSpec(memory_space=pltpu.SMEM)
ANY = pl.BlockSpec(memory_space=pl.ANY)


def shape_of(shape, dtype=BF):
    return jax.ShapeDtypeStruct(shape, dtype)


def call(name, kernel, outs, args, specs=None, scratch=(), megabytes=12, long=False):
    return pl.pallas_call(
        kernel,
        out_shape=outs,
        in_specs=[VMEM] * len(args) if specs is None else specs,
        out_specs=[VMEM] * len(outs),
        scratch_shapes=list(scratch),
        compiler_params=pltpu.CompilerParams(vmem_limit_bytes=megabytes << 20),
        cost_estimate=pl.CostEstimate(
            flops=1 << (35 if long else 20), bytes_accessed=1 << 10, transcendentals=0
        ),
        name=name,
    )(*args)


def block(ref, slot, size):
    return ref[:, pl.ds(pl.multiple_of(slot * size, size), size)]


def pack(w_qkv, w_out, vectors):
    rows = w_qkv.shape[0]
    sizes = [v.shape[0] for v in vectors]
    wide = max(sizes)
    table = jnp.stack([jnp.pad(v, (0, wide - v.shape[0])) for v in vectors], 0)

    def kernel(table_ref, qkv_ref, out_ref, to, sems):
        copies = [
            pltpu.make_async_copy(qkv_ref, to.at[:, pl.ds(0, 3 * D)], sems.at[0]),
            pltpu.make_async_copy(out_ref, to.at[:, pl.ds(3 * D, D)], sems.at[1]),
        ]
        for copy in copies:
            copy.start()
        row = lax.broadcasted_iota(jnp.int32, (rows, wide), 0)
        column = lax.broadcasted_iota(jnp.int32, (rows, wide), 1)
        lane = lax.broadcasted_iota(jnp.int32, (rows, 128), 1)
        total, place = jnp.zeros((rows, 128), F32), 0
        for n, size in enumerate(sizes):
            value = table_ref[n : n + 1, :].astype(F32)
            for start in range(0, size, rows):
                picked = jnp.sum(jnp.where(column == row + start, value, 0.0), 1, keepdims=True)
                total = total + jnp.where(lane == place, picked, 0.0)
                place += 1
        to[:, 4 * D :] = total.astype(BF)
        for copy in copies:
            copy.wait()

    return call(
        "pack",
        kernel,
        [shape_of((rows, 4 * D + 128))],
        (table, w_qkv, w_out),
        [VMEM, ANY, ANY],
        [pltpu.SemaphoreType.DMA((2,))],
    )[0]


def unpack(own, other, rel_z, count):
    chips, rows = 4 * depth(), own[0][0].shape[1]
    flat = [(core, p) for core, part in enumerate((own, other)) for p in part]
    arrays = [p[0] for _, p in flat]
    cuts = [(0, 3 * D), (3 * D, D), (4 * D, 128)]

    def kernel(*refs):
        ins = refs[: len(arrays)]
        qkv_ref, out_ref, vec_ref, small_ref, sems = refs[len(arrays) :]
        where = position()
        copies = []
        for n in (2, 0, 1):
            to = (qkv_ref, out_ref, small_ref)[n]
            start, width = cuts[n]
            for ref, (core, (_, names)) in zip(ins, flat):
                at = where[3] ^ core
                for i, name in enumerate(names):
                    copy = pltpu.make_async_copy(
                        ref.at[i, :, pl.ds(start, width)],
                        to.at[chip_slot(name, where, rel_z), at],
                        sems.at[len(copies)],
                    )
                    copy.start()
                    copies.append(copy)
        for copy in copies[: len(copies) // 3]:
            copy.wait()
        small = small_ref[...].reshape(2 * chips * rows, 128).astype(F32)
        vec_ref[...] = jnp.transpose(small)[:count]
        for copy in copies[len(copies) // 3 :]:
            copy.wait()

    shapes = [(chips, 2, rows, w) for _, w in cuts]
    qkv, out, vec = call(
        "unpack",
        kernel,
        [shape_of(shapes[0]), shape_of(shapes[1]), shape_of((count, D), F32)],
        arrays,
        [ANY] * len(arrays),
        [pltpu.VMEM(shapes[2], BF), pltpu.SemaphoreType.DMA((6 * chips,))],
    )
    return qkv.reshape(D, 3 * D), out.reshape(D, D), vec


def normal_of(values):
    center = values - jnp.mean(values, -1, keepdims=True)
    inv = lax.rsqrt(jnp.mean(center * center, -1, keepdims=True) + 1e-05)
    return center * inv, inv


def norm_back(grad, normal, inv, gain):
    e = grad * gain
    return inv * (
        e - jnp.mean(e, -1, keepdims=True) - normal * jnp.mean(e * normal, -1, keepdims=True)
    )


def project(resident, vec, weight):
    def kernel(x_ref, vec_ref, w_ref, normed_ref, qkv_ref):
        for r in range(0, 2 * ROW, ROW):
            normal, _ = normal_of(x_ref[r : r + ROW, :].astype(F32))
            normed_ref[r : r + ROW, :] = (normal * vec_ref[0:1, :] + vec_ref[1:2, :]).astype(BF)
        for n in range(0, 3 * D, 512):
            qkv_ref[:, n : n + 512] = bdot(normed_ref[...], w_ref[:, n : n + 512], NN).astype(BF)

    outs = [shape_of((2 * ROW, D)), shape_of((2 * ROW, 3 * D))]
    return call("project", kernel, outs, (resident, vec, weight))


def attend(mixed, weight, resident, vec):
    def kernel(m_ref, w_ref, x_ref, vec_ref, normed_ref, hidden_ref):
        for r in range(0, 2 * ROW, ROW):
            rows = slice(r, r + ROW)
            hidden = x_ref[rows, :].astype(F32) + bdot(m_ref[rows, :], w_ref[...], NN)
            hidden_ref[rows, :] = hidden
            normal, _ = normal_of(hidden)
            normed_ref[rows, :] = (normal * vec_ref[2:3, :] + vec_ref[3:4, :]).astype(BF)

    outs = [shape_of((2 * ROW, D)), shape_of((2 * ROW, D), F32)]
    return call("attend", kernel, outs, (mixed, weight, resident, vec))


def gelu_both(v):
    c = (2.0 / jnp.pi) ** 0.5
    square = v * v
    t = jnp.tanh(v * (c + (c * 0.044715) * square))
    half = 0.5 + 0.5 * t
    return v * half, half + 0.5 * v * (1.0 - t * t) * (c + (3 * c * 0.044715) * square)


def feed_step(n_ref, w_ref, shift_ref, act_ref, slope_ref, start, size):
    cols = slice(start, start + size)
    pre = bdot(n_ref[...], w_ref[:, cols], NN) + shift_ref[:, cols]
    act, slope = gelu_both(pre)
    act_ref[:, cols] = act.astype(BF)
    slope_ref[:, cols] = slope.astype(BF)


def feed_first(normed, pieces, shift):
    chips, (rows, wide) = 4 * depth(), pieces[0][0].shape[1:]
    arrays = [p[0] for p in pieces]
    size = 512

    def kernel(n_ref, shift_ref, *refs):
        ins = refs[: len(arrays)]
        act_ref, slope_ref, w_ref, sems = refs[len(arrays) :]
        where = position()
        copies = []
        for start in range(0, wide, size):
            for ref, (_, names) in zip(ins, pieces):
                for i, name in enumerate(names):
                    to = pl.multiple_of(chip_slot(name, where, False) * rows, rows)
                    copy = pltpu.make_async_copy(
                        ref.at[i, :, pl.ds(start, size)],
                        w_ref.at[pl.ds(to, rows), pl.ds(start, size)],
                        sems.at[len(copies)],
                    )
                    copy.start()
                    copies.append(copy)
        for n, start in enumerate(range(0, wide, size)):
            for copy in copies[n * chips : (n + 1) * chips]:
                copy.wait()
            feed_step(n_ref, w_ref, shift_ref, act_ref, slope_ref, start, size)

    part = shape_of((2 * ROW, wide))
    return call(
        "feed_first",
        kernel,
        [part, part, shape_of((chips * rows, wide))],
        (normed, shift, *arrays),
        [VMEM, VMEM] + [ANY] * len(arrays),
        [pltpu.SemaphoreType.DMA((chips * (wide // size),))],
        long=True,
    )


def feed_second(normed, weight, shift):
    def kernel(n_ref, w_ref, shift_ref, act_ref, slope_ref):
        for start in range(0, weight.shape[1], 512):
            feed_step(n_ref, w_ref, shift_ref, act_ref, slope_ref, start, 512)

    part = shape_of((2 * ROW, weight.shape[1]))
    return call("feed_second", kernel, [part, part], (normed, weight, shift))


def down_grad(acts, cts):
    lists = layout_yzx()
    chips = 4 * depth()
    size = acts[0].shape[1] // chips
    half = size // 2
    group = 4

    def kernel(a0, a1, c0, c1, *outs):
        where = position()
        for jy in range(2):
            for jx in range(2):
                for z in range(0, depth(), group):
                    names = [(jy, z + i, jx) for i in range(group)]
                    slots = [chip_slot(name, where, False) for name in names]
                    total = 0.0
                    for a, ct in ((a0, c0), (a1, c1)):
                        left = jnp.concatenate([block(a, slot, size) for slot in slots], 1)
                        total = total + bdot(left, ct[...], TN)
                    total = total.astype(BF).reshape(group, size, D)
                    for i, name in enumerate(names):
                        upper, lower = outs[1 - jy], outs[3 - jx]
                        upper[lists[1 - jy].index(name)] = total[i, :half]
                        lower[lists[3 - jx].index(name)] = total[i, half:]

    outs = [shape_of((len(v), half, D)) for v in lists]
    return call("down_grad", kernel, outs, (*acts, *cts))


def back_act(cts, pieces, slopes):
    wide = slopes[0].shape[1]
    chips = 4 * depth()
    size = wide // chips
    arrays = [p[0] for p in pieces]
    half = size // 2

    def kernel(c0, c1, s0, s1, *refs):
        ins, (g0, g1, sum_ref, w_ref) = refs[: len(arrays)], refs[len(arrays) :]
        where = position()
        for z in range(depth()):
            for jy in range(2):
                for n, (_, names) in enumerate(pieces):
                    for i, name in enumerate(names):
                        if name[:2] == (jy, z):
                            slot = chip_slot(name, where, False)
                            row = pl.multiple_of(slot * size + (n // 2) * half, half)
                            w_ref[pl.ds(row, half), :] = ins[n][i]
        for j in range(chips // 2):
            at = slice(j * 2 * size, (j + 1) * 2 * size)
            sums = 0.0
            for ct, slope, out in ((c0, s0, g0), (c1, s1, g1)):
                grad = bdot(ct[...], w_ref[at, :], NT) * slope[:, at].astype(F32)
                grad = grad.astype(BF)
                sums = sums + jnp.sum(grad.astype(F32), 0, keepdims=True)
                out[:, at] = grad
            sum_ref[:, at] = sums

    part = shape_of((2 * ROW, wide))
    return call(
        "back_act",
        kernel,
        [part, part, shape_of((1, wide), F32), shape_of((wide, D))],
        (*cts, *slopes, *arrays),
    )


def back_up(grad, weight, dtype):
    def kernel(g_ref, w_ref, out_ref):
        for n in range(0, D, 256):
            out_ref[:, n : n + 256] = bdot(g_ref[...], w_ref[n : n + 256, :], NT).astype(dtype)

    outs = [shape_of((2 * ROW, D), dtype)]
    return call("back_up", kernel, outs, (grad, weight), long=dtype == F32)[0]


def up_grad(normeds, grads, out_own, out_in):
    lists = layout_yxz()
    half, wide = depth() // 2, grads[0].shape[1]
    rows = D // (4 * depth())
    extra = rows // 4

    def kernel(n0, n1, g0, g1, a_ref, b_ref, *outs_and_scratch):
        outs, part_ref = outs_and_scratch[:4], outs_and_scratch[4]
        where = position()
        for out, names in zip(outs, lists):
            for i, name in enumerate(names):
                slot = chip_slot(name, where, False)
                total = (a_ref[slot].astype(F32) + b_ref[slot].astype(F32)).astype(BF)
                out[i, rows:, :D] = total[:extra]
                out[i, rows:, D:] = total[extra:]
        for side in range(2):
            for jy in range(2):
                base = (where[0] ^ jy) * depth() + side * half
                for n in range(0, wide, 512):
                    total = 0.0
                    for normed, grad in ((n0, g0), (n1, g1)):
                        left = jnp.concatenate(
                            [block(normed, base + i, 2 * rows) for i in range(half)], 1
                        )
                        total = total + bdot(left, grad[:, n : n + 512], TN)
                    part_ref[:, :, :, n : n + 512] = total.astype(BF).reshape(half, 2, rows, 512)
                for jx in range(2):
                    for i in range(half):
                        if side == 0:
                            out, at = outs[1 - jy], jx * half + i
                        else:
                            out, at = outs[3 - jx], jy * half + i
                        out[at, :rows] = part_ref[i, where[2] ^ jx]

    outs = [shape_of((len(v), rows + extra, wide)) for v in lists]
    scratch = [pltpu.VMEM((half, 2, rows, wide), BF)]
    return call("up_grad", kernel, outs, (*normeds, *grads, out_own, out_in), None, scratch)


def out_grad(mixed, low):
    chips = 4 * depth()
    rows = D // (2 * chips)
    group = 256 // (2 * rows)

    def kernel(m_ref, l_ref, send_ref, keep_ref):
        core = position()[3]
        for g in range(D // 256):
            at, cols = slice(g * group, (g + 1) * group), slice(g * 256, (g + 1) * 256)
            total = bdot(m_ref[:, cols], l_ref[...], TN).astype(BF).reshape(group, 2, rows, D)
            first, second = total[:, 0], total[:, 1]
            send_ref[at] = jnp.where(core == 0, second, first)
            keep_ref[at] = jnp.where(core == 0, first, second)

    outs = [shape_of((chips, rows, D))] * 2
    return call("out_grad", kernel, outs, (mixed, low))


def back_norm(own, other, hidden, vec, ct, weight):
    def kernel(a_ref, b_ref, h_ref, vec_ref, ct_ref, w_ref, mixed_ref, low_ref, grad_ref, sum_ref):
        first, second = 0.0, 0.0
        for r in range(0, 2 * ROW, ROW):
            rows = slice(r, r + ROW)
            normal, inv = normal_of(h_ref[rows, :])
            grad = a_ref[rows, :] + b_ref[rows, :].astype(F32)
            first = first + jnp.sum(grad * normal, 0, keepdims=True)
            second = second + jnp.sum(grad, 0, keepdims=True)
            total = ct_ref[rows, :].astype(F32) + norm_back(grad, normal, inv, vec_ref[2:3, :])
            grad_ref[rows, :] = total
            low_ref[rows, :] = total.astype(BF)
            mixed_ref[rows, :] = bdot(low_ref[rows, :], w_ref[...], NT).astype(BF)
        sum_ref[0:1, :] = first
        sum_ref[1:2, :] = second

    part = shape_of((2 * ROW, D))
    outs = [part, part, shape_of((2 * ROW, D), F32), shape_of((2, D), F32)]
    return call("back_norm", kernel, outs, (own, other, hidden, vec, ct, weight))


def attn_grad(normed, grads):
    chips = 4 * depth()
    rows = D // (2 * chips)
    group = 256 // (2 * rows)

    def kernel(n_ref, g_ref, send_ref, keep_ref):
        core = position()[3]
        for g in range(D // 256):
            at, cols = slice(g * group, (g + 1) * group), slice(g * 256, (g + 1) * 256)
            for part in range(3):
                total = bdot(n_ref[:, cols], g_ref[part], TN).astype(BF)
                total = total.reshape(group, 2, rows, D)
                first, second = total[:, 0], total[:, 1]
                to = slice(part * D, (part + 1) * D)
                send_ref[at, :, to] = jnp.where(core == 0, second, first)
                keep_ref[at, :, to] = jnp.where(core == 0, first, second)

    outs = [shape_of((chips, rows, 3 * D))] * 2
    return call("attn_grad", kernel, outs, (normed, grads))


def core_sum(own, arrived, sums, sums_in, rel_z):
    lists = layout_yxz()
    chips, rows, wide = own.shape
    lines = sums.shape[0]

    def kernel(a_ref, b_ref, s_ref, t_ref, *rest):
        outs, pad_ref, small_ref = rest[:4], rest[4], rest[5]
        where = position()
        pad_ref[...] = jnp.zeros_like(pad_ref)
        pad_ref[:lines, :] = s_ref[...] + t_ref[...]
        small_ref[...] = jnp.transpose(pad_ref[...]).astype(BF).reshape(chips, 2, rows, 128)
        for out, names in zip(outs, lists):
            for i, name in enumerate(names):
                slot = chip_slot(name, where, rel_z)
                total = a_ref[slot].astype(F32) + b_ref[slot].astype(F32)
                out[i, :, :wide] = total.astype(BF)
                out[i, :, wide:] = small_ref[slot, where[3]]

    outs = [shape_of((len(v), rows, wide + 128)) for v in lists]
    scratch = [pltpu.VMEM((128, D), F32), pltpu.VMEM((chips, 2, rows, 128), BF)]
    return call("core_sum", kernel, outs, (own, arrived, sums, sums_in), None, scratch)


def back_first(grads, weight, resident, vec, hidden_grad):
    def kernel(g_ref, w_ref, x_ref, vec_ref, h_ref, own_ref, send_ref, sum_ref):
        first, second = 0.0, 0.0
        y = position()[0]
        for half, out_ref in ((y, own_ref), (1 - y, send_ref)):
            rows = pl.ds(pl.multiple_of(half * ROW, ROW), ROW)
            normal, inv = normal_of(x_ref[rows, :].astype(F32))
            grad = 0.0
            for part in range(3):
                grad = grad + bdot(g_ref[part, rows, :], w_ref[:, part * D : (part + 1) * D], NT)
            first = first + jnp.sum(grad * normal, 0, keepdims=True)
            second = second + jnp.sum(grad, 0, keepdims=True)
            total = h_ref[rows, :] + norm_back(grad, normal, inv, vec_ref[0:1, :])
            out_ref[...] = total.astype(BF)
        sum_ref[0:1, :] = first
        sum_ref[1:2, :] = second

    outs = [shape_of((ROW, D)), shape_of((ROW, D)), shape_of((2, D), F32)]
    args = (grads, weight, resident, vec, hidden_grad)
    return call("back_first", kernel, outs, args)


def down_back(act, weight, dtype, hidden=None):
    extra = () if hidden is None else (hidden,)

    def kernel(a_ref, w_ref, *refs):
        out_ref = refs[-1]
        for n in range(0, D, 256):
            total = bdot(a_ref[...], w_ref[:, n : n + 256], NN)
            if hidden is not None:
                total = total + refs[0][:, n : n + 256]
            out_ref[:, n : n + 256] = total.astype(dtype)

    outs = [shape_of((2 * ROW, D), dtype)]
    return call("down_back", kernel, outs, (act, weight, *extra))[0]


def result_of(own, other):
    def kernel(a_ref, b_ref, own_ref, send_ref):
        y = position()[0]
        for half, out_ref in ((y, own_ref), (1 - y, send_ref)):
            rows = pl.ds(pl.multiple_of(half * ROW, ROW), ROW)
            out_ref[...] = (a_ref[rows, :] + b_ref[rows, :].astype(F32)).astype(BF)

    return call("result_of", kernel, [shape_of((ROW, D))] * 2, (own, other))


def home(out_own, out_other, grad_own, grad_other):
    lines = ROW // 2

    def kernel(a_ref, b_ref, c_ref, d_ref, out_ref, grad_ref):
        mine = pl.program_id(1) == position()[0]

        @pl.when(mine)
        def _():
            out_ref[0] = a_ref[...]
            grad_ref[0] = c_ref[...].astype(F32)

        @pl.when(jnp.logical_not(mine))
        def _():
            out_ref[0] = b_ref[...]
            grad_ref[0] = d_ref[...].astype(F32)

    part = pl.BlockSpec((lines, D), lambda i, m: (i, 0))
    return pl.pallas_call(
        kernel,
        grid=(2, MICRO),
        out_shape=[
            jax.ShapeDtypeStruct((MICRO, ROW, D), BF),
            jax.ShapeDtypeStruct((MICRO, ROW, D), F32),
        ],
        in_specs=[part] * 4,
        out_specs=[pl.BlockSpec((1, lines, D), lambda i, m: (m, i, 0))] * 2,
        compiler_params=pltpu.CompilerParams(vmem_limit_bytes=16 << 20),
        cost_estimate=pl.CostEstimate(flops=1 << 20, bytes_accessed=1 << 10, transcendentals=0),
        name="home",
    )(out_own, out_other, grad_own, grad_other)


def interleave(own, other):
    rows, wide = own.shape
    size = wide // (4 * depth())

    def kernel(a_ref, b_ref, out_ref):
        core = position()[3]
        for n in range(wide // size):
            cols = slice(n * size, (n + 1) * size)
            for ref, at in ((a_ref, core), (b_ref, 1 - core)):
                to = pl.multiple_of((2 * n + at) * size, size)
                out_ref[:, pl.ds(to, size)] = ref[:, cols]

    return call("interleave", kernel, [shape_of((rows, 2 * wide), F32)], (own, other))[0]


def shards(
    inputs,
    cotangent,
    phone_len,
    prompt_len,
    target_len,
    ln1_gain,
    ln1_bias,
    w_qkv,
    w_out,
    ln2_gain,
    ln2_bias,
    w_up,
    up_bias,
    w_down,
):
    y, z, x, c = position()
    count = depth()
    chips = 4 * count
    row_w = w_qkv.shape[0]
    row_f = w_down.shape[0]

    chain = Chain()

    def split_halves(blocks):
        return (
            lax.dynamic_index_in_dim(blocks, 1 - y, 0, keepdims=False),
            lax.dynamic_index_in_dim(blocks, y, 0, keepdims=False),
        )

    attn_g, up_g, down_g = Gather(chain, True), Gather(chain, False), GatherXZY(chain)
    down_s, up_s, attn_s = ScatterYZX(chain), Scatter(chain, False), Scatter(chain, True)

    vectors = (ln1_gain, ln1_bias, ln2_gain, ln2_bias, up_bias)
    attn_z = attn_g.over_z(chain(pack, w_qkv, w_out, vectors))
    def split_both(inputs, cotangent):
        x_send, x_own = split_halves(inputs)
        ct_send, ct_own = split_halves(cotangent)
        return jnp.stack([x_send, ct_send], 0), x_own, ct_own

    both_send, x_own, ct_own = chain(split_both, inputs[:, 0, 0], cotangent[:, 0, 0])
    both_other = swap(both_send, "y")
    lengths = tuple(
        lax.dynamic_index_in_dim(v, y, 0, keepdims=False)[0]
        for v in (phone_len, prompt_len, target_len)
    )

    def split_up(w_up):
        split = w_up.reshape(row_w, chips, 2, FF // chips // 2)
        return tuple(
            lax.dynamic_index_in_dim(split, i, 2, keepdims=False).reshape(row_w, FF // 2)
            for i in (1 - c, c)
        )

    up_send, up_own = chain(split_up, w_up)
    up_other = swap(up_send, 1)
    up_shard = chain(lambda own, other: ordered(c, own, other, 0), up_own, up_other)
    half_f = row_f // 2

    def join_both(x_own, ct_own, other):
        return ordered(y, x_own, other[0], 0), ordered(y, ct_own, other[1], 0)

    resident, grad_result = chain(join_both, x_own, ct_own, both_other)
    attn_one = attn_g.one(extras=(w_down[:half_f], w_down[half_f:]))
    up_z = up_g.over_z(up_shard, *attn_z)


    attn_two = attn_g.two(extras=(half_f, D))
    early = [(swap(array, 1), rels) for array, rels in attn_g.pieces[::2]]
    down_z = down_g.over_z(attn_g.planes[2], *up_z)
    up_g.one_halves()
    late = [(swap(after(array, *up_g.halves), 1), rels) for array, rels in attn_g.pieces[1::2]]
    up_one = up_g.send(*[v[0] for v in early + late])
    lines = 4 + row_f // row_w
    attn_core = early + late
    many = len(attn_core)

    def unpack_pieces(*arrays):
        own = [(a, p[1]) for a, p in zip(arrays[:many], attn_g.pieces)]
        other = [(a, p[1]) for a, p in zip(arrays[many:], attn_core)]
        return unpack(own, other, attn_g.rel_z, lines)

    qkv_weight, out_weight, vec = chain(
        unpack_pieces, *[p[0] for p in attn_g.pieces + attn_core]
    )
    shift = vec[4:].reshape(row_f // row_w, chips, 2, row_w)
    shift = lax.dynamic_index_in_dim(shift, c, 2, keepdims=False)
    shift = shift.transpose(1, 0, 2).reshape(1, FF // 2)

    normed, qkv = chain(project, resident, vec, qkv_weight)
    up_two = up_g.two()
    mixed, logs = chain(lambda v: attention_forward(v, *lengths), qkv)
    normed_two, hidden = chain(attend, mixed, out_weight, resident, vec)
    ct_sent = swap(grad_result, 1)
    normed_sent = swap(normed_two, 1)

    def with_pieces(step, pieces):
        def run(*args):
            arrays, rest = args[: len(pieces)], args[len(pieces) :]
            return step([(a, p[1]) for a, p in zip(arrays, pieces)], *rest)

        return run

    up_arrays = [p[0] for p in up_g.pieces]
    down_two = down_g.two(*up_two)
    act_own, slope_own, up_weight = chain(
        with_pieces(lambda p, n, s: feed_first(n, p, s), up_g.pieces), *up_arrays, normed_two, shift
    )
    act_other, slope_other = chain(feed_second, normed_sent, up_weight, shift)
    down_sone = down_s.one(
        chain(
            lambda a, b, p, q: down_grad((a, b), (p, q)), act_own, act_other, grad_result, ct_sent
        ),
    )

    pre_own, pre_other, grad_shift, down_weight = chain(
        with_pieces(lambda p, a, b, s, t: back_act((a, b), p, (s, t)), down_g.pieces),
        *[p[0] for p in down_g.pieces],
        grad_result,
        ct_sent,
        slope_own,
        slope_other,
    )
    two_other = swap(chain(lambda g, w: back_up(g, w, BF), pre_other, up_weight), 1)
    two_own = chain(lambda g, w: back_up(g, w, F32), pre_own, up_weight)
    grad_mixed, grad_low, grad_hidden, sums_two = chain(
        back_norm, two_own, two_other, hidden, vec, grad_result, out_weight
    )
    out_send, out_keep = chain(out_grad, mixed, grad_low)
    out_in = swap(out_send, 1)
    down_sz = down_s.over_z()
    up_sone = up_s.one(
        chain(
            lambda a, b, p, q, o, i: up_grad((a, b), (p, q), o, i),
            normed_two,
            normed_sent,
            pre_own,
            pre_other,
            out_keep,
            out_in,
        )
    )
    grads = chain(lambda a, b, v: attention_backward(a, b, v, *lengths), qkv, grad_mixed, logs)
    attn_send, attn_keep = chain(attn_grad, normed, grads)
    attn_in = swap(attn_send, 1)
    gx_own, gx_send, sums_one = chain(back_first, grads, qkv_weight, resident, vec, grad_hidden)

    def small_lines(one, two, shift):
        last = shift.reshape(chips, row_f // row_w, row_w).transpose(1, 0, 2)[:, :, None]
        last = ordered(c, last, jnp.zeros_like(last), 2).reshape(-1, D)
        return jnp.concatenate([one, two, last], 0)

    sums = chain(small_lines, sums_one, sums_two, grad_shift)
    sums_in = swap(sums, 1)
    up_stwo = up_s.two()
    attn_parts = chain(
        lambda a, b, p, q: core_sum(a, b, p, q, attn_s.rel_z), attn_keep, attn_in, sums, sums_in
    )
    attn_sone = attn_s.one(attn_parts, *up_stwo)
    down_sent = swap(chain(lambda a, w: down_back(a, w, BF), act_other, down_weight), 1)
    down_own = chain(lambda a, w, h: down_back(a, w, F32, h), act_own, down_weight, hidden)
    up_sz = up_s.over_z()

    down_sz = down_sz.reshape(4, half_f, D)
    attn_stwo = attn_s.two(extras=(down_sz,))
    res_own, res_send = chain(result_of, down_own, down_sent)
    sum_up = chain(up_s.total, up_sz)
    sum_up = sum_up.reshape(-1, FF // 2)
    out_rows = sum_up[2 * row_w :]
    sum_out = jnp.concatenate([out_rows[:, :D], out_rows[:, D:]], 0)
    up_rows = sum_up[: 2 * row_w].reshape(2, row_w, FF // 2)
    up_mine = lax.dynamic_index_in_dim(up_rows, c, 0, keepdims=False)
    up_theirs = swap(lax.dynamic_index_in_dim(up_rows, 1 - c, 0, keepdims=False), 1)
    attn_sz = attn_s.over_z()
    gx_other = swap(after(gx_send, *attn_stwo), "y")
    out_other = swap(after(res_send, *attn_stwo), "y")

    def sum_of_down(lines, from_x, from_y):
        upper, lower = lines[0], lines[2]
        from_x, from_y = (v[:, 3 * D + 128 :].reshape(half_f, D) for v in (from_x, from_y))
        return jnp.concatenate([plus(upper.astype(F32), from_x), plus(lower.astype(F32), from_y)], 0)

    sum_down = chain(sum_of_down, down_sz, *attn_stwo)

    up_final = chain(interleave, up_mine, up_theirs)
    out_stack, grad_stack = chain(home, res_own, out_other, gx_own, gx_other)
    out_stack, grad_stack = (v.reshape(MICRO, 1, 1, ROW, D) for v in (out_stack, grad_stack))
    sum_attn = attn_s.total(attn_sz)
    small_sum = sum_attn[:, 3 * D : 3 * D + lines].T.reshape(-1)
    edges = [i * row_w for i in range(5)]
    small_out = [small_sum[a:b] for a, b in zip(edges[:4], edges[1:])]
    return (
        out_stack,
        grad_stack,
        small_out[0],
        small_out[1],
        sum_attn[:, : 3 * D],
        sum_out,
        small_out[2],
        small_out[3],
        up_final.reshape(row_w, FF),
        small_sum[4 * row_w : 4 * row_w + row_f],
        sum_down,
    )


def plain_passed_along(block, axis, distance):
    devices = range(lax.axis_size(axis))
    route = [(i - distance, i) for i in devices if i - distance in devices]
    return lax.ppermute(block, axis, route)


def plain_times_transposed(left, right):
    return lax.dot_general(
        left, right, (((1,), (1,)), ((), ())), preferred_element_type=jnp.float32
    )


def plain_transposed_times(left, right):
    return lax.dot_general(
        left, right, (((0,), (0,)), ((), ())), preferred_element_type=jnp.float32
    )


def plain_layer_norm(values, gain, bias):
    center = values - jnp.mean(values, -1, keepdims=True)
    spread = jnp.mean(center * center, -1, keepdims=True)
    return center * lax.rsqrt(spread + 1e-05) * gain + bias


def plain_locate(lengths, slot_ids):
    count = jnp.arange(lengths.shape[0])
    seg_ends = jnp.sum(jnp.where(count[None, :] <= count[:, None], lengths[None, :], 0), 1, dtype=jnp.int32)
    seg_ids = jnp.sum(
        (slot_ids[:, None] >= seg_ends[None, :]).astype(jnp.int32), 1, dtype=jnp.int32
    )
    one_hot = (seg_ids[:, None] == jnp.arange(lengths.shape[0], dtype=jnp.int32)[None, :]).astype(
        jnp.int32
    )
    seg_start = jnp.sum(one_hot * (seg_ends - lengths)[None, :], 1, dtype=jnp.int32)
    return (seg_ids, one_hot, slot_ids - seg_start)


def plain_frame_meta(phone_lens, prompt_lens, target_lens, slot_count):
    slot_ids = jnp.arange(slot_count, dtype=jnp.int32)
    pre_seg, pre_hot, pre_off = plain_locate(phone_lens + prompt_lens, slot_ids)
    pre_phone = jnp.sum(pre_hot * phone_lens[None, :], 1, dtype=jnp.int32)
    prefix = (pre_seg, pre_off < pre_phone, pre_off - pre_phone)
    tgt_seg, tgt_hot, tgt_off = plain_locate(target_lens, slot_ids)
    tgt_pos = jnp.sum(tgt_hot * prompt_lens[None, :], 1, dtype=jnp.int32) + tgt_off
    targets = (tgt_seg, tgt_off < 0, tgt_pos)
    return (prefix, targets)


def plain_allowed(query_meta, key_meta):
    same_seg = query_meta[0][:, None] == key_meta[0][None, :]
    audio_ok = key_meta[1][None, :] | (key_meta[2][None, :] <= query_meta[2][:, None])
    return same_seg & jnp.where(query_meta[1][:, None], key_meta[1][None, :], audio_ok)


def plain_masked_scores(queries, key_rows, allowed_mask, score_scale):
    scores = (
        jnp.einsum("qhd,khd->hqk", queries, key_rows, preferred_element_type=jnp.float32)
        * score_scale
    )
    return jnp.where(allowed_mask[None], scores, -1e30)


def plain_attention_forward(queries, key_rows, value_rows, allowed_mask, score_scale):
    scores = plain_masked_scores(queries, key_rows, allowed_mask, score_scale)
    peak = jnp.max(scores, -1, keepdims=True)
    exp_scores = jnp.exp(scores - peak)
    row_total = jnp.sum(exp_scores, -1, keepdims=True)
    probs = (exp_scores / row_total).astype(jnp.bfloat16)
    mixed = jnp.einsum("hqk,khd->qhd", probs, value_rows, preferred_element_type=jnp.float32)
    return (mixed.astype(jnp.bfloat16), peak + jnp.log(row_total))


def plain_attention_backward(
    queries, key_rows, value_rows, allowed_mask, log_total, grad_mixed, score_scale
):
    scores = plain_masked_scores(queries, key_rows, allowed_mask, score_scale)
    probs = jnp.where(allowed_mask[None], jnp.exp(scores - log_total), 0.0)
    grad_probs = jnp.einsum(
        "qhd,khd->hqk", grad_mixed, value_rows, preferred_element_type=jnp.float32
    )
    grad_values = jnp.einsum(
        "hqk,qhd->khd", probs.astype(jnp.bfloat16), grad_mixed, preferred_element_type=jnp.float32
    )
    inner = jnp.sum(grad_probs * probs, -1, keepdims=True)
    grad_scores = (probs * (grad_probs - inner)).astype(jnp.bfloat16)
    grad_queries = (
        jnp.einsum("hqk,khd->qhd", grad_scores, key_rows, preferred_element_type=jnp.float32)
        * score_scale
    )
    grad_keys = (
        jnp.einsum("hqk,qhd->khd", grad_scores, queries, preferred_element_type=jnp.float32)
        * score_scale
    )
    return (grad_queries, grad_keys, grad_values)


def plain_add_up(summed, fresh):
    if summed is None:
        return fresh
    return jax.tree.map(lambda summed_part, fresh_part: summed_part + fresh_part, summed, fresh)


def plain_fetch_forward(params):
    return (
        lax.all_gather(params[0], ("pair", "rows"), axis=0, tiled=True),
        lax.all_gather(params[1], ("pair", "rows"), axis=0, tiled=True),
        lax.all_gather(params[2], ("pair", "rows"), axis=0, tiled=True),
        lax.all_gather(params[3], ("pair", "rows"), axis=0, tiled=True),
        lax.all_gather(params[4], ("pair", "rows"), axis=0, tiled=True),
        lax.all_gather(params[5], ("pair", "rows"), axis=0, tiled=True),
        lax.all_gather(params[6], ("pair", "rows"), axis=0, tiled=True),
        lax.all_gather(params[7], ("pair", "rows"), axis=0, tiled=True),
        lax.all_gather(params[8], ("pair", "rows"), axis=0, tiled=True),
    )


def plain_shards(
    inputs,
    cotangent,
    phone_len,
    prompt_len,
    target_len,
    ln1_gain,
    ln1_bias,
    w_qkv,
    w_out,
    ln2_gain,
    ln2_bias,
    w_up,
    up_bias,
    w_down,
):
    half_index = lax.axis_index("pair")
    score_scale = HEAD ** (-0.5)
    params = (ln1_gain, ln1_bias, w_qkv, w_out, ln2_gain, ln2_bias, w_up, up_bias, w_down)
    out_blocks = []
    grad_blocks = []
    summed = None
    for batch_index in range(MICRO):
        gathered = plain_fetch_forward(params)
        (
            gain_one,
            bias_one,
            qkv_weight,
            out_weight,
            gain_two,
            bias_two,
            up_weight,
            up_shift,
            down_weight,
        ) = gathered
        gain_one_f = gain_one.astype(jnp.float32)
        bias_one_f = bias_one.astype(jnp.float32)
        gain_two_f = gain_two.astype(jnp.float32)
        bias_two_f = bias_two.astype(jnp.float32)
        prefix, targets = plain_frame_meta(
            phone_len[batch_index, 0], prompt_len[batch_index, 0], target_len[batch_index, 0], ROW
        )
        query_meta = tuple(
            (
                jnp.where(half_index == 0, pre_field, tgt_field)
                for pre_field, tgt_field in zip(prefix, targets)
            )
        )
        remote_mask = plain_allowed(query_meta, prefix) & (half_index == 1)
        allowed_mask = jnp.concatenate([remote_mask, plain_allowed(query_meta, query_meta)], 1)
        resident = inputs[batch_index, 0, 0].astype(jnp.float32)
        normed = plain_layer_norm(resident, gain_one_f, bias_one_f).astype(jnp.bfloat16)
        qkv_rows = jnp.dot(normed, qkv_weight, preferred_element_type=jnp.float32).astype(
            jnp.bfloat16
        )
        own_kv = qkv_rows[:, D:]
        remote_kv = plain_passed_along(own_kv, "pair", 1)
        queries = qkv_rows[:, :D].reshape(ROW, HEADS, HEAD)
        key_rows = jnp.concatenate([remote_kv[:, :D], own_kv[:, :D]], 0).reshape(
            2 * ROW, HEADS, HEAD
        )
        value_rows = jnp.concatenate([remote_kv[:, D:], own_kv[:, D:]], 0).reshape(
            2 * ROW, HEADS, HEAD
        )
        mixed, log_total = plain_attention_forward(
            queries, key_rows, value_rows, allowed_mask, score_scale
        )
        mixed_flat = mixed.reshape(ROW, D)
        hidden_res = resident + jnp.dot(mixed_flat, out_weight, preferred_element_type=jnp.float32)
        normed_two = plain_layer_norm(hidden_res, gain_two_f, bias_two_f).astype(jnp.bfloat16)
        pre_act = jnp.dot(
            normed_two, up_weight, preferred_element_type=jnp.float32
        ) + up_shift.astype(jnp.float32)
        activ = jax.nn.gelu(pre_act, approximate=True).astype(jnp.bfloat16)
        result = hidden_res + jnp.dot(activ, down_weight, preferred_element_type=jnp.float32)
        out_blocks.append(result.astype(jnp.bfloat16))
        gathered = (
            lax.all_gather(params[0], ("pair", "rows"), axis=0, tiled=True),
            lax.all_gather(params[1], ("pair", "rows"), axis=0, tiled=True),
            lax.all_gather(params[2], ("pair", "rows"), axis=0, tiled=True),
            lax.all_gather(params[3], ("pair", "rows"), axis=0, tiled=True),
            lax.all_gather(params[4], ("pair", "rows"), axis=0, tiled=True),
            lax.all_gather(params[5], ("pair", "rows"), axis=0, tiled=True),
            lax.all_gather(params[6], ("pair", "rows"), axis=0, tiled=True),
            lax.all_gather(params[7], ("pair", "rows"), axis=0, tiled=True),
            lax.all_gather(params[8], ("pair", "rows"), axis=0, tiled=True),
        )
        (
            gain_one,
            bias_one,
            qkv_weight,
            out_weight,
            gain_two,
            bias_two,
            up_weight,
            up_shift,
            down_weight,
        ) = gathered
        gain_one_f = gain_one.astype(jnp.float32)
        bias_one_f = bias_one.astype(jnp.float32)
        gain_two_f = gain_two.astype(jnp.float32)
        bias_two_f = bias_two.astype(jnp.float32)
        grad_result = cotangent[batch_index, 0, 0]
        grad_down = plain_transposed_times(activ, grad_result)
        grad_activ = plain_times_transposed(grad_result, down_weight)
        _, gelu_back = jax.vjp(lambda pre_value: jax.nn.gelu(pre_value, approximate=True), pre_act)
        grad_pre = gelu_back(grad_activ)[0].astype(jnp.bfloat16)
        grad_up = plain_transposed_times(normed_two, grad_pre)
        grad_up_bias = jnp.sum(grad_pre.astype(jnp.float32), 0)
        grad_normed_two = plain_times_transposed(grad_pre, up_weight)
        _, norm_back_two = jax.vjp(plain_layer_norm, hidden_res, gain_two_f, bias_two_f)
        grad_hidden_ln, grad_gain_two, grad_bias_two = norm_back_two(grad_normed_two)
        grad_hidden = grad_result.astype(jnp.float32) + grad_hidden_ln
        grad_hidden_low = grad_hidden.astype(jnp.bfloat16)
        grad_out_w = plain_transposed_times(mixed_flat, grad_hidden_low)
        grad_mixed = (
            plain_times_transposed(grad_hidden_low, out_weight)
            .astype(jnp.bfloat16)
            .reshape(ROW, HEADS, HEAD)
        )
        grad_queries, grad_keys, grad_values = plain_attention_backward(
            queries, key_rows, value_rows, allowed_mask, log_total, grad_mixed, score_scale
        )
        remote_grads = jnp.concatenate(
            [grad_keys[:ROW].reshape(ROW, D), grad_values[:ROW].reshape(ROW, D)], 1
        )
        returned = plain_passed_along(remote_grads.astype(jnp.bfloat16), "pair", -1).astype(
            remote_grads.dtype
        )
        grad_qkv_rows = jnp.concatenate(
            [
                grad_queries.reshape(ROW, D),
                grad_keys[ROW:].reshape(ROW, D) + returned[:, :D],
                grad_values[ROW:].reshape(ROW, D) + returned[:, D:],
            ],
            1,
        ).astype(jnp.bfloat16)
        grad_qkv_w = plain_transposed_times(normed, grad_qkv_rows)
        grad_normed = plain_times_transposed(grad_qkv_rows, qkv_weight)
        _, norm_back_one = jax.vjp(plain_layer_norm, resident, gain_one_f, bias_one_f)
        grad_resident_ln, grad_gain_one, grad_bias_one = norm_back_one(grad_normed)
        grad_blocks.append(grad_hidden + grad_resident_ln)
        local_grads = (
            grad_gain_one,
            grad_bias_one,
            grad_qkv_w,
            grad_out_w,
            grad_gain_two,
            grad_bias_two,
            grad_up,
            grad_up_bias,
            grad_down,
        )
        shard_part = (
            lax.psum_scatter(local_grads[0], ("pair", "rows"), scatter_dimension=0, tiled=True),
            lax.psum_scatter(local_grads[1], ("pair", "rows"), scatter_dimension=0, tiled=True),
            lax.psum_scatter(local_grads[2], ("pair", "rows"), scatter_dimension=0, tiled=True),
            lax.psum_scatter(local_grads[3], ("pair", "rows"), scatter_dimension=0, tiled=True),
            lax.psum_scatter(local_grads[4], ("pair", "rows"), scatter_dimension=0, tiled=True),
            lax.psum_scatter(local_grads[5], ("pair", "rows"), scatter_dimension=0, tiled=True),
            lax.psum_scatter(local_grads[6], ("pair", "rows"), scatter_dimension=0, tiled=True),
            lax.psum_scatter(local_grads[7], ("pair", "rows"), scatter_dimension=0, tiled=True),
            lax.psum_scatter(local_grads[8], ("pair", "rows"), scatter_dimension=0, tiled=True),
        )
        summed = plain_add_up(summed, shard_part)
    block_shape = (MICRO, 1, 1, ROW, D)
    out_stack = jnp.stack(out_blocks, 0).reshape(block_shape)
    grad_stack = jnp.stack(grad_blocks, 0).reshape(block_shape)
    return (
        out_stack,
        grad_stack,
        summed[0],
        summed[1],
        summed[2],
        summed[3],
        summed[4],
        summed[5],
        summed[6],
        summed[7],
        summed[8],
    )


def solution(mesh):
    rows = P(None, "rows", "pair", None, None)
    line = P(("pair", "rows"))
    flat = P(("pair", "rows"), None)
    lens = P(None, "rows", None)
    return jax.shard_map(
        shards if mesh.shape["rows"] == 16 else plain_shards,
        mesh=mesh,
        in_specs=(rows, rows, lens, lens, lens, line, line, flat, flat, line, line, flat, line, flat),
        out_specs=(rows, rows, line, line, flat, flat, line, line, flat, line, flat),
        check_vma=False,
    )
```

```python
import functools

import jax
import jax.numpy as jnp
from jax import lax
from jax.experimental import pallas as pl
from jax.experimental.pallas import tpu as pltpu
from jax.sharding import PartitionSpec as P

D = 1024
HEADS = 16
HEAD = 64
FF = 4096
ROW = 256
MICRO = 2
BF = jnp.bfloat16
F32 = jnp.float32
NEG = -1e30


def position():
    row = lax.axis_index("rows")
    return lax.axis_index("pair"), row // 4, (row // 2) % 2, row % 2


def depth():
    return lax.axis_size("rows") // 4


def swap(block, way):
    if way == "y":
        return lax.ppermute(block, "pair", [(i, i ^ 1) for i in range(2)])
    count = lax.axis_size("rows")
    return lax.ppermute(block, "rows", [(i, i ^ way) for i in range(count)])


def after(block, *others):
    return lax.optimization_barrier((block, *others))[0]


class Chain:
    def __init__(self):
        self.last = None

    def __call__(self, step, *args):
        if self.last is not None:
            args, _ = lax.optimization_barrier((args, self.last))
        out = step(*args)
        self.last = out
        return out


def z_groups():
    count = lax.axis_size("rows")
    return [[z * 4 + low for z in range(count // 4)] for low in range(4)]


def z_gather(block):
    return lax.all_gather(block, "rows", axis_index_groups=z_groups())


def z_scatter(column):
    return lax.psum_scatter(column, "rows", scatter_dimension=0, axis_index_groups=z_groups())


def join_planes(left, left_in, right, right_in):
    half, rows, cols = left.shape

    def kernel(a_ref, b_ref, c_ref, d_ref, left_ref, right_ref):
        left_ref[0] = a_ref[0]
        left_ref[1] = b_ref[0]
        right_ref[0] = c_ref[0]
        right_ref[1] = d_ref[0]

    part = pl.BlockSpec((1, rows, cols), lambda i: (i, 0, 0))
    both = pl.BlockSpec((2, None, rows, cols), lambda i: (0, i, 0, 0))
    made = pl.pallas_call(
        kernel,
        grid=(half,),
        out_shape=[jax.ShapeDtypeStruct((2, half, rows, cols), BF)] * 2,
        in_specs=[part] * 4,
        out_specs=[both] * 2,
        compiler_params=pltpu.CompilerParams(vmem_limit_bytes=16 << 20),
        cost_estimate=pl.CostEstimate(flops=1 << 20, bytes_accessed=1 << 10, transcendentals=0),
        name="join_planes",
    )(left, left_in, right, right_in)
    return [v.reshape(2 * half, rows, cols) for v in made]


class Gather:
    def __init__(self, chain, by_permutes):
        self.chain = chain
        self.rel_z = by_permutes and depth() == 4

    def over_z(self, block, *first):
        block = after(block, *first)
        if self.rel_z:
            self.column = [block[None]] + [swap(block[None], 4 * k) for k in range(1, 4)]
            return self.column[1:]
        self.column = [z_gather(block)]
        return self.column

    def one(self, *first, extras=()):
        half = depth() // 2

        def halves(column, extras):
            if self.rel_z:
                left, right = jnp.concatenate(column[:2], 0), jnp.concatenate(column[2:], 0)
            else:
                left, right = column[0][:half], column[0][half:]
            return beside((left, right), extras)

        self.halves = self.chain(halves, self.column, extras)
        return self.send(*first)

    def one_halves(self):
        half = depth() // 2
        self.halves = self.chain(lambda v: (v[:half], v[half:]), self.column[0])

    def send(self, *first):
        left, right = lax.optimization_barrier((self.halves, first))[0]
        self.sides = swap(left, 2), swap(right, "y")
        return list(self.sides)

    def two(self, *first, extras=()):
        rows, cols = self.column[0].shape[-2:]
        block = (depth() // 2, rows, cols)

        def planes(halves, sides):
            left, right = halves
            left_x, right_y = sides
            if not extras:
                return join_planes(left, left_x, right, right_y)
            main = [v[:, :cols].reshape(block) for v in (left, left_x, right, right_y)]
            more = [v[:, cols:].reshape(extras) for v in (left, left_x, right, right_y)]
            return (
                jnp.concatenate(main[:2], 0),
                jnp.concatenate(main[2:], 0),
                jnp.stack(more, 0),
            )

        sides = lax.optimization_barrier((self.sides, first))[0]
        self.planes = self.chain(planes, self.halves, sides)
        left, right = self.planes[:2]
        left_y, right_x = swap(left, "y"), swap(right, 2)
        half = depth() // 2
        low, high = range(half), range(half, 2 * half)
        self.pieces = [
            (left, [(0, i, 0) for i in low] + [(0, i, 1) for i in low]),
            (left_y, [(1, i, 0) for i in low] + [(1, i, 1) for i in low]),
            (right, [(0, i, 0) for i in high] + [(1, i, 0) for i in high]),
            (right_x, [(0, i, 1) for i in high] + [(1, i, 1) for i in high]),
        ]
        return [left_y, right_x]


def beside(blocks, extras):
    if not extras:
        return tuple(blocks)
    out = []
    for block, extra in zip(blocks, extras):
        rows = block.shape[0] * block.shape[1]
        out.append(
            jnp.concatenate([block.reshape(rows, -1), extra.reshape(rows, -1)], 1)
        )
    return tuple(out)


class GatherXZY:
    def __init__(self, chain):
        self.chain = chain

    def over_z(self, lines, *first):
        self.column = z_gather(after(lines, *first))
        return self.column

    def two(self, *first):
        def cut(column):
            shape = (2 * depth(), *column.shape[2:])
            return column[:, :2].reshape(shape), column[:, 2:].reshape(shape)

        upper, lower = self.chain(cut, after(self.column, *first))
        upper_y, lower_x = swap(upper, "y"), swap(lower, 2)
        ids = range(depth())
        self.pieces = [
            (upper, [(0, i, j) for i in ids for j in range(2)]),
            (upper_y, [(1, i, j) for i in ids for j in range(2)]),
            (lower, [(j, i, 0) for i in ids for j in range(2)]),
            (lower_x, [(j, i, 1) for i in ids for j in range(2)]),
        ]
        return [upper_y, lower_x]


def chip_slot(chip, where, rel_z):
    jy, jz, jx = chip
    y, z, x, _ = where
    z_at = (z ^ jz) if rel_z else jz
    return ((y ^ jy) * depth() + z_at) * 2 + (x ^ jx)


def layout_yzx():
    ids = range(depth())
    return [
        [(1, i, j) for i in ids for j in range(2)],
        [(0, i, j) for i in ids for j in range(2)],
        [(j, i, 1) for i in ids for j in range(2)],
        [(j, i, 0) for i in ids for j in range(2)],
    ]


def layout_yxz():
    half = depth() // 2
    low, high = range(half), range(half, 2 * half)
    return [
        [(1, i, j) for j in range(2) for i in low],
        [(0, i, j) for j in range(2) for i in low],
        [(j, i, 1) for j in range(2) for i in high],
        [(j, i, 0) for j in range(2) for i in high],
    ]


def plus(left, right):
    return (left.astype(F32) + right.astype(F32)).astype(left.dtype)


def add_halves(left, left_in, right, right_in, extras):
    count, rows, cols = left.shape
    half = count // 2
    more = extras[0].shape[2] if extras else 0
    extras = list(extras) * 2

    def kernel(*refs):
        ins, outs = refs[: 8 + len(extras)], refs[8 + len(extras) :]
        for side in range(2):
            a, b, c, d = ins[4 * side : 4 * side + 4]
            own, send = outs[2 + side], outs[side]
            own[...] = (a[...].astype(F32) + b[...].astype(F32)).astype(BF)
            total = (c[0].astype(F32) + d[0].astype(F32)).astype(BF)
            if extras:
                send[:, :cols] = total
                send[:, cols:] = ins[8 + side][0]
            else:
                send[0] = total

    low = pl.BlockSpec((1, rows, cols), lambda i: (i, 0, 0))
    high = pl.BlockSpec((1, rows, cols), lambda i: (i + half, 0, 0))
    wide = pl.BlockSpec((rows, cols + more), lambda i: (i, 0))
    send = jax.ShapeDtypeStruct((half * rows, cols + more) if extras else (half, rows, cols), BF)
    own = jax.ShapeDtypeStruct((half, rows, cols), BF)
    return pl.pallas_call(
        kernel,
        grid=(half,),
        out_shape=[send, send, own, own],
        in_specs=[low, low, high, high] * 2
        + [pl.BlockSpec((1, rows, more), lambda i, n=n: (n, i, 0)) for n in (1, 3)[: len(extras)]],
        out_specs=[wide if extras else low] * 2 + [low] * 2,
        compiler_params=pltpu.CompilerParams(vmem_limit_bytes=16 << 20),
        cost_estimate=pl.CostEstimate(flops=1 << 35, bytes_accessed=1 << 10, transcendentals=0),
        name="add_halves",
    )(left, left_in, left, left_in, right, right_in, right, right_in, *extras)


def add_column(left, left_in, right, right_in):
    half, rows, cols = left.shape

    def kernel(a_ref, b_ref, c_ref, d_ref, out_ref):
        out_ref[0] = (a_ref[0].astype(F32) + b_ref[0].astype(F32)).astype(BF)
        out_ref[1] = (c_ref[0].astype(F32) + d_ref[0].astype(F32)).astype(BF)

    part = pl.BlockSpec((1, rows, cols), lambda i: (i, 0, 0))
    return pl.pallas_call(
        kernel,
        grid=(half,),
        out_shape=jax.ShapeDtypeStruct((2, half, rows, cols), BF),
        in_specs=[part] * 4,
        out_specs=pl.BlockSpec((2, None, rows, cols), lambda i: (0, i, 0, 0)),
        compiler_params=pltpu.CompilerParams(vmem_limit_bytes=16 << 20),
        cost_estimate=pl.CostEstimate(flops=1 << 20, bytes_accessed=1 << 10, transcendentals=0),
        name="add_column",
    )(left, left_in, right, right_in).reshape(2 * half, rows, cols)


class Scatter:
    def __init__(self, chain, by_permutes):
        self.chain = chain
        self.rel_z = by_permutes and depth() == 4

    def one(self, parts, *first):
        self.parts = parts
        left, _, right, _ = parts
        self.sides = swap(after(left, *first), "y"), swap(after(right, *first), 2)
        return list(self.sides)

    def two(self, *first, extras=()):
        _, left, _, right = self.parts
        left_in, right_in = lax.optimization_barrier((self.sides, first))[0]
        self.sums = self.chain(add_halves, left, left_in, right, right_in, extras)
        self.ends = swap(self.sums[0], 2), swap(self.sums[1], "y")
        return list(self.ends)

    def over_z(self, *first):
        _, _, left, right = self.sums
        left_in, right_in = self.ends

        def add(left, left_in, right, right_in):
            left_in, right_in = (
                v if v.ndim == 3 else v[:, : left.shape[2]].reshape(left.shape)
                for v in (left_in, right_in)
            )
            if self.rel_z:
                return (
                    plus(left[1], left_in[1]),
                    *plus(right, right_in),
                    left[0].astype(F32) + left_in[0].astype(F32),
                )
            return add_column(left, left_in, right, right_in)

        made = self.chain(add, left, left_in, right, right_in)
        if not self.rel_z:
            return z_scatter(after(made, *first))
        one, two, three, own = made
        return own, swap(one, 4), swap(two, 8), swap(three, 12)

    def total(self, parts):
        if not self.rel_z:
            return parts.astype(F32)
        own, *arrived = parts

        def add(own, *arrived):
            for part in arrived:
                own = own + part.astype(F32)
            return own

        return self.chain(add, own, *arrived)


class ScatterYZX:
    def __init__(self, chain):
        self.chain = chain

    def one(self, parts, *first):
        self.parts = parts
        left, _, right, _ = parts
        self.sides = swap(after(left, *first), "y"), swap(after(right, *first), 2)
        return list(self.sides)

    def over_z(self, *first):
        def add(left, left_in, right, right_in):
            shape = (depth(), 2, *left.shape[1:])
            upper, lower = plus(left, left_in).reshape(shape), plus(right, right_in).reshape(shape)
            return jnp.concatenate([upper, lower], 1)

        _, left, _, right = self.parts
        self.lines = z_scatter(self.chain(add, left, self.sides[0], right, self.sides[1]))
        return self.lines


def ordered(flag, own, other, axis):
    return jnp.where(
        flag == 0,
        jnp.concatenate([own, other], axis),
        jnp.concatenate([other, own], axis),
    )


def frames(index, phone, prompt, target, segs):
    pre_end = ends_of([phone[s] + prompt[s] for s in range(segs)])
    tgt_end = ends_of([target[s] for s in range(segs)])
    is_target = index >= ROW
    local = jnp.where(is_target, index - ROW, index)
    seg = jnp.zeros_like(index)
    for s in range(segs):
        edge = jnp.where(is_target, tgt_end[s], pre_end[s])
        seg = seg + jnp.where(local >= edge, 1, 0)
    start = jnp.zeros_like(index)
    phones = jnp.zeros_like(index)
    prompts = jnp.zeros_like(index)
    for s in range(segs):
        pick = seg == s
        pre_start = pre_end[s] - phone[s] - prompt[s]
        tgt_start = tgt_end[s] - target[s]
        start = jnp.where(pick, jnp.where(is_target, tgt_start, pre_start), start)
        phones = jnp.where(pick, phone[s], phones)
        prompts = jnp.where(pick, prompt[s], prompts)
    off = local - start
    is_phone = jnp.where(is_target, 0, jnp.where(off < phones, 1, 0))
    pos = jnp.where(is_target, prompts + off, off - phones)
    return seg, is_phone, pos


def ends_of(lengths):
    out, total = [], 0
    for length in lengths:
        total = total + length
        out.append(total)
    return out


def bias_of(query, key):
    q_seg, q_phone, q_pos = query
    k_seg, k_phone, k_pos = key
    audio = (k_phone == 1) | (k_pos <= q_pos)
    good = (q_seg == k_seg) & (((q_phone == 1) & (k_phone == 1)) | ((q_phone == 0) & audio))
    return jnp.where(good, 0.0, NEG)


def bdot(left, right, dims):
    return lax.dot_general(left, right, (dims, ((), ())), preferred_element_type=F32)


NT = ((1,), (1,))
NN = ((1,), (0,))
TN = ((0,), (0,))


def attention_forward(qkv, phone, prompt, target):
    segs = phone.shape[0]
    group = 2

    def kernel(
        phone_ref, prompt_ref, target_ref, q_ref, k_ref, v_ref, out_ref, log_ref, bias_ref
    ):
        @pl.when(pl.program_id(0) == 0)
        def _():
            ph = [phone_ref[s] for s in range(segs)]
            pr = [prompt_ref[s] for s in range(segs)]
            tg = [target_ref[s] for s in range(segs)]
            rows = lax.broadcasted_iota(jnp.int32, (2 * ROW, 1), 0)
            cols = lax.broadcasted_iota(jnp.int32, (1, 2 * ROW), 1)
            bias_ref[...] = bias_of(
                frames(cols, ph, pr, tg, segs), frames(rows, ph, pr, tg, segs)
            )

        lane = lax.broadcasted_iota(jnp.int32, (1, 2 * HEAD), 1)
        zero = jnp.zeros((), BF)
        scale = jnp.asarray(HEAD**-0.5, BF)
        for pair in range(group):
            cols = slice(pair * 2 * HEAD, (pair + 1) * 2 * HEAD)
            for rows, keys in ((0, ROW), (ROW, 2 * ROW)):
                at = slice(rows, rows + ROW)
                outs = []
                for j in range(2):
                    q = jnp.where((lane // HEAD) == j, q_ref[at, cols] * scale, zero)
                    s = bdot(k_ref[:keys, cols], q, NT) + bias_ref[:keys, at]
                    peak = jnp.max(s, 0, keepdims=True)
                    e = jnp.exp(s - peak)
                    total = jnp.sum(e, 0, keepdims=True)
                    log_ref[0, 2 * pair + j : 2 * pair + j + 1, at] = peak + jnp.log(total)
                    p = (e * (1.0 / total)).astype(BF)
                    outs.append(bdot(v_ref[:keys, cols], p, TN)[j * HEAD : (j + 1) * HEAD])
                out_ref[at, cols] = jnp.transpose(jnp.concatenate(outs, 0)).astype(BF)

    steps = HEADS // 2 // group
    smem = pl.BlockSpec(memory_space=pltpu.SMEM)
    part = (2 * ROW, 2 * HEAD * group)
    return pl.pallas_call(
        kernel,
        grid=(steps,),
        out_shape=[
            jax.ShapeDtypeStruct((2 * ROW, D), BF),
            jax.ShapeDtypeStruct((steps, 2 * group, 2 * ROW), F32),
        ],
        in_specs=[
            smem,
            smem,
            smem,
            pl.BlockSpec(part, lambda h: (0, h)),
            pl.BlockSpec(part, lambda h: (0, h + steps)),
            pl.BlockSpec(part, lambda h: (0, h + 2 * steps)),
        ],
        out_specs=[
            pl.BlockSpec(part, lambda h: (0, h)),
            pl.BlockSpec((1, 2 * group, 2 * ROW), lambda h: (h, 0, 0)),
        ],
        scratch_shapes=[pltpu.VMEM((2 * ROW, 2 * ROW), F32)],
        compiler_params=pltpu.CompilerParams(vmem_limit_bytes=16 << 20),
        cost_estimate=pl.CostEstimate(flops=1 << 20, bytes_accessed=1 << 10, transcendentals=0),
        name="attention_forward",
    )(phone, prompt, target, qkv, qkv, qkv)


def attention_backward(qkv, grad_mixed, logs, phone, prompt, target):
    segs = phone.shape[0]
    group = 2

    def kernel(
        phone_ref, prompt_ref, target_ref, q_ref, k_ref, v_ref, g_ref, log_ref, out_ref, bias_ref
    ):
        @pl.when(pl.program_id(0) == 0)
        def _():
            ph = [phone_ref[s] for s in range(segs)]
            pr = [prompt_ref[s] for s in range(segs)]
            tg = [target_ref[s] for s in range(segs)]
            rows = lax.broadcasted_iota(jnp.int32, (2 * ROW, 1), 0)
            cols = lax.broadcasted_iota(jnp.int32, (1, 2 * ROW), 1)
            bias_ref[...] = bias_of(
                frames(cols, ph, pr, tg, segs), frames(rows, ph, pr, tg, segs)
            )

        lane = lax.broadcasted_iota(jnp.int32, (1, 2 * HEAD), 1)
        zero = jnp.zeros((), BF)
        scale = HEAD**-0.5
        for pair in range(group):
            cols = slice(pair * 2 * HEAD, (pair + 1) * 2 * HEAD)
            dks, dvs = {}, {}
            for rows, keys in ((0, ROW), (ROW, 2 * ROW)):
                at = slice(rows, rows + ROW)
                dqs = []
                for j in range(2):
                    sel = (lane // HEAD) == j
                    q_all, g_all = q_ref[at, cols], g_ref[at, cols]
                    q = jnp.where(sel, q_all * jnp.asarray(scale, BF), zero)
                    g = jnp.where(sel, g_all, zero)
                    k, v = k_ref[:keys, cols], v_ref[:keys, cols]
                    s = bdot(k, q, NT) + bias_ref[:keys, at]
                    dp = bdot(v, g, NT)
                    p = jnp.exp(s - log_ref[0, 2 * pair + j : 2 * pair + j + 1, at])
                    inner = jnp.sum(dp * p, 0, keepdims=True)
                    ds = (p * (dp - inner)).astype(BF)
                    dvs[rows, j] = bdot(p.astype(BF), g_all, NN)
                    dks[rows, j] = bdot(ds, q_all, NN)
                    dqs.append(bdot(k, ds, TN)[j * HEAD : (j + 1) * HEAD])
                dq = jnp.transpose(jnp.concatenate(dqs, 0)) * scale
                out_ref[0, at, cols] = dq.astype(BF)
            low = lane < HEAD
            for place, part, factor in ((1, dks, scale), (2, dvs, 1.0)):
                early = jnp.where(low, part[0, 0], part[0, 1])
                late = jnp.where(low, part[ROW, 0], part[ROW, 1])
                out_ref[place, :ROW, cols] = ((early + late[:ROW]) * factor).astype(BF)
                out_ref[place, ROW:, cols] = (late[ROW:] * factor).astype(BF)

    steps = HEADS // 2 // group
    smem = pl.BlockSpec(memory_space=pltpu.SMEM)
    block = (2 * ROW, 2 * HEAD * group)
    return pl.pallas_call(
        kernel,
        grid=(steps,),
        out_shape=jax.ShapeDtypeStruct((3, 2 * ROW, D), BF),
        in_specs=[
            smem,
            smem,
            smem,
            pl.BlockSpec(block, lambda h: (0, h)),
            pl.BlockSpec(block, lambda h: (0, h + steps)),
            pl.BlockSpec(block, lambda h: (0, h + 2 * steps)),
            pl.BlockSpec(block, lambda h: (0, h)),
            pl.BlockSpec((1, 2 * group, 2 * ROW), lambda h: (h, 0, 0)),
        ],
        out_specs=pl.BlockSpec((3, *block), lambda h: (0, 0, h)),
        scratch_shapes=[pltpu.VMEM((2 * ROW, 2 * ROW), F32)],
        compiler_params=pltpu.CompilerParams(vmem_limit_bytes=16 << 20),
        cost_estimate=pl.CostEstimate(flops=1 << 20, bytes_accessed=1 << 10, transcendentals=0),
        name="attention_backward",
    )(phone, prompt, target, qkv, qkv, qkv, grad_mixed, logs)


VMEM = pl.BlockSpec(memory_space=pltpu.VMEM)
SMEM = pl.BlockSpec(memory_space=pltpu.SMEM)
ANY = pl.BlockSpec(memory_space=pl.ANY)


def shape_of(shape, dtype=BF):
    return jax.ShapeDtypeStruct(shape, dtype)


def call(name, kernel, outs, args, specs=None, scratch=(), megabytes=12, long=False):
    return pl.pallas_call(
        kernel,
        out_shape=outs,
        in_specs=[VMEM] * len(args) if specs is None else specs,
        out_specs=[VMEM] * len(outs),
        scratch_shapes=list(scratch),
        compiler_params=pltpu.CompilerParams(vmem_limit_bytes=megabytes << 20),
        cost_estimate=pl.CostEstimate(
            flops=1 << (35 if long else 20), bytes_accessed=1 << 10, transcendentals=0
        ),
        name=name,
    )(*args)


def block(ref, slot, size):
    return ref[:, pl.ds(pl.multiple_of(slot * size, size), size)]


def pack(w_qkv, w_out, vectors):
    rows = w_qkv.shape[0]
    sizes = [v.shape[0] for v in vectors]
    wide = max(sizes)
    table = jnp.stack([jnp.pad(v, (0, wide - v.shape[0])) for v in vectors], 0)

    def kernel(table_ref, qkv_ref, out_ref, to, sems):
        copies = [
            pltpu.make_async_copy(qkv_ref, to.at[:, pl.ds(0, 3 * D)], sems.at[0]),
            pltpu.make_async_copy(out_ref, to.at[:, pl.ds(3 * D, D)], sems.at[1]),
        ]
        for copy in copies:
            copy.start()
        row = lax.broadcasted_iota(jnp.int32, (rows, wide), 0)
        column = lax.broadcasted_iota(jnp.int32, (rows, wide), 1)
        lane = lax.broadcasted_iota(jnp.int32, (rows, 128), 1)
        total, place = jnp.zeros((rows, 128), F32), 0
        for n, size in enumerate(sizes):
            value = table_ref[n : n + 1, :].astype(F32)
            for start in range(0, size, rows):
                picked = jnp.sum(jnp.where(column == row + start, value, 0.0), 1, keepdims=True)
                total = total + jnp.where(lane == place, picked, 0.0)
                place += 1
        to[:, 4 * D :] = total.astype(BF)
        for copy in copies:
            copy.wait()

    return call(
        "pack",
        kernel,
        [shape_of((rows, 4 * D + 128))],
        (table, w_qkv, w_out),
        [VMEM, ANY, ANY],
        [pltpu.SemaphoreType.DMA((2,))],
    )[0]


def unpack(own, other, rel_z, count):
    chips, rows = 4 * depth(), own[0][0].shape[1]
    flat = [(core, p) for core, part in enumerate((own, other)) for p in part]
    arrays = [p[0] for _, p in flat]
    cuts = [(0, 3 * D), (3 * D, D), (4 * D, 128)]

    def kernel(*refs):
        ins = refs[: len(arrays)]
        qkv_ref, out_ref, vec_ref, small_ref, sems = refs[len(arrays) :]
        where = position()
        copies = []
        for n in (2, 0, 1):
            to = (qkv_ref, out_ref, small_ref)[n]
            start, width = cuts[n]
            for ref, (core, (_, names)) in zip(ins, flat):
                at = where[3] ^ core
                for i, name in enumerate(names):
                    copy = pltpu.make_async_copy(
                        ref.at[i, :, pl.ds(start, width)],
                        to.at[chip_slot(name, where, rel_z), at],
                        sems.at[len(copies)],
                    )
                    copy.start()
                    copies.append(copy)
        for copy in copies[: len(copies) // 3]:
            copy.wait()
        small = small_ref[...].reshape(2 * chips * rows, 128).astype(F32)
        vec_ref[...] = jnp.transpose(small)[:count]
        for copy in copies[len(copies) // 3 :]:
            copy.wait()

    shapes = [(chips, 2, rows, w) for _, w in cuts]
    qkv, out, vec = call(
        "unpack",
        kernel,
        [shape_of(shapes[0]), shape_of(shapes[1]), shape_of((count, D), F32)],
        arrays,
        [ANY] * len(arrays),
        [pltpu.VMEM(shapes[2], BF), pltpu.SemaphoreType.DMA((6 * chips,))],
    )
    return qkv.reshape(D, 3 * D), out.reshape(D, D), vec


def normal_of(values):
    center = values - jnp.mean(values, -1, keepdims=True)
    inv = lax.rsqrt(jnp.mean(center * center, -1, keepdims=True) + 1e-05)
    return center * inv, inv


def norm_back(grad, normal, inv, gain):
    e = grad * gain
    return inv * (
        e - jnp.mean(e, -1, keepdims=True) - normal * jnp.mean(e * normal, -1, keepdims=True)
    )


def project(resident, vec, weight):
    def kernel(x_ref, vec_ref, w_ref, normed_ref, qkv_ref):
        for r in range(0, 2 * ROW, ROW):
            normal, _ = normal_of(x_ref[r : r + ROW, :].astype(F32))
            normed_ref[r : r + ROW, :] = (normal * vec_ref[0:1, :] + vec_ref[1:2, :]).astype(BF)
        for n in range(0, 3 * D, 512):
            qkv_ref[:, n : n + 512] = bdot(normed_ref[...], w_ref[:, n : n + 512], NN).astype(BF)

    outs = [shape_of((2 * ROW, D)), shape_of((2 * ROW, 3 * D))]
    return call("project", kernel, outs, (resident, vec, weight))


def attend(mixed, weight, resident, vec):
    def kernel(m_ref, w_ref, x_ref, vec_ref, normed_ref, hidden_ref):
        for r in range(0, 2 * ROW, ROW):
            rows = slice(r, r + ROW)
            hidden = x_ref[rows, :].astype(F32) + bdot(m_ref[rows, :], w_ref[...], NN)
            hidden_ref[rows, :] = hidden
            normal, _ = normal_of(hidden)
            normed_ref[rows, :] = (normal * vec_ref[2:3, :] + vec_ref[3:4, :]).astype(BF)

    outs = [shape_of((2 * ROW, D)), shape_of((2 * ROW, D), F32)]
    return call("attend", kernel, outs, (mixed, weight, resident, vec))


def gelu_both(v):
    c = (2.0 / jnp.pi) ** 0.5
    square = v * v
    t = jnp.tanh(v * (c + (c * 0.044715) * square))
    half = 0.5 + 0.5 * t
    return v * half, half + 0.5 * v * (1.0 - t * t) * (c + (3 * c * 0.044715) * square)


def feed_step(n_ref, w_ref, shift_ref, act_ref, slope_ref, start, size):
    cols = slice(start, start + size)
    pre = bdot(n_ref[...], w_ref[:, cols], NN) + shift_ref[:, cols]
    act, slope = gelu_both(pre)
    act_ref[:, cols] = act.astype(BF)
    slope_ref[:, cols] = slope.astype(BF)


def feed_first(normed, pieces, shift):
    chips, (rows, wide) = 4 * depth(), pieces[0][0].shape[1:]
    arrays = [p[0] for p in pieces]
    size = 512

    def kernel(n_ref, shift_ref, *refs):
        ins = refs[: len(arrays)]
        act_ref, slope_ref, w_ref, sems = refs[len(arrays) :]
        where = position()
        copies = []
        for start in range(0, wide, size):
            for ref, (_, names) in zip(ins, pieces):
                for i, name in enumerate(names):
                    to = pl.multiple_of(chip_slot(name, where, False) * rows, rows)
                    copy = pltpu.make_async_copy(
                        ref.at[i, :, pl.ds(start, size)],
                        w_ref.at[pl.ds(to, rows), pl.ds(start, size)],
                        sems.at[len(copies)],
                    )
                    copy.start()
                    copies.append(copy)
        for n, start in enumerate(range(0, wide, size)):
            for copy in copies[n * chips : (n + 1) * chips]:
                copy.wait()
            feed_step(n_ref, w_ref, shift_ref, act_ref, slope_ref, start, size)

    part = shape_of((2 * ROW, wide))
    return call(
        "feed_first",
        kernel,
        [part, part, shape_of((chips * rows, wide))],
        (normed, shift, *arrays),
        [VMEM, VMEM] + [ANY] * len(arrays),
        [pltpu.SemaphoreType.DMA((chips * (wide // size),))],
        long=True,
    )


def feed_second(normed, weight, shift):
    def kernel(n_ref, w_ref, shift_ref, act_ref, slope_ref):
        for start in range(0, weight.shape[1], 512):
            feed_step(n_ref, w_ref, shift_ref, act_ref, slope_ref, start, 512)

    part = shape_of((2 * ROW, weight.shape[1]))
    return call("feed_second", kernel, [part, part], (normed, weight, shift))


def down_grad(acts, cts):
    lists = layout_yzx()
    chips = 4 * depth()
    size = acts[0].shape[1] // chips
    half = size // 2
    group = 4

    def kernel(a0, a1, c0, c1, *outs):
        where = position()
        for jy in range(2):
            for jx in range(2):
                for z in range(0, depth(), group):
                    names = [(jy, z + i, jx) for i in range(group)]
                    slots = [chip_slot(name, where, False) for name in names]
                    total = 0.0
                    for a, ct in ((a0, c0), (a1, c1)):
                        left = jnp.concatenate([block(a, slot, size) for slot in slots], 1)
                        total = total + bdot(left, ct[...], TN)
                    total = total.astype(BF).reshape(group, size, D)
                    for i, name in enumerate(names):
                        upper, lower = outs[1 - jy], outs[3 - jx]
                        upper[lists[1 - jy].index(name)] = total[i, :half]
                        lower[lists[3 - jx].index(name)] = total[i, half:]

    outs = [shape_of((len(v), half, D)) for v in lists]
    return call("down_grad", kernel, outs, (*acts, *cts))


def back_act(cts, pieces, slopes):
    wide = slopes[0].shape[1]
    chips = 4 * depth()
    size = wide // chips
    arrays = [p[0] for p in pieces]
    half = size // 2

    def kernel(c0, c1, s0, s1, *refs):
        ins, (g0, g1, sum_ref, w_ref) = refs[: len(arrays)], refs[len(arrays) :]
        where = position()
        for z in range(depth()):
            for jy in range(2):
                for n, (_, names) in enumerate(pieces):
                    for i, name in enumerate(names):
                        if name[:2] == (jy, z):
                            slot = chip_slot(name, where, False)
                            row = pl.multiple_of(slot * size + (n // 2) * half, half)
                            w_ref[pl.ds(row, half), :] = ins[n][i]
        for j in range(chips // 2):
            at = slice(j * 2 * size, (j + 1) * 2 * size)
            sums = 0.0
            for ct, slope, out in ((c0, s0, g0), (c1, s1, g1)):
                grad = bdot(ct[...], w_ref[at, :], NT) * slope[:, at].astype(F32)
                grad = grad.astype(BF)
                sums = sums + jnp.sum(grad.astype(F32), 0, keepdims=True)
                out[:, at] = grad
            sum_ref[:, at] = sums

    part = shape_of((2 * ROW, wide))
    return call(
        "back_act",
        kernel,
        [part, part, shape_of((1, wide), F32), shape_of((wide, D))],
        (*cts, *slopes, *arrays),
    )


def back_up(grad, weight, dtype):
    def kernel(g_ref, w_ref, out_ref):
        for n in range(0, D, 256):
            out_ref[:, n : n + 256] = bdot(g_ref[...], w_ref[n : n + 256, :], NT).astype(dtype)

    outs = [shape_of((2 * ROW, D), dtype)]
    return call("back_up", kernel, outs, (grad, weight), long=dtype == F32)[0]


def up_grad(normeds, grads, out_own, out_in):
    lists = layout_yxz()
    half, wide = depth() // 2, grads[0].shape[1]
    rows = D // (4 * depth())
    extra = rows // 4

    def kernel(n0, n1, g0, g1, a_ref, b_ref, *outs_and_scratch):
        outs, part_ref = outs_and_scratch[:4], outs_and_scratch[4]
        where = position()
        for out, names in zip(outs, lists):
            for i, name in enumerate(names):
                slot = chip_slot(name, where, False)
                total = (a_ref[slot].astype(F32) + b_ref[slot].astype(F32)).astype(BF)
                out[i, rows:, :D] = total[:extra]
                out[i, rows:, D:] = total[extra:]
        for side in range(2):
            for jy in range(2):
                base = (where[0] ^ jy) * depth() + side * half
                for n in range(0, wide, 512):
                    total = 0.0
                    for normed, grad in ((n0, g0), (n1, g1)):
                        left = jnp.concatenate(
                            [block(normed, base + i, 2 * rows) for i in range(half)], 1
                        )
                        total = total + bdot(left, grad[:, n : n + 512], TN)
                    part_ref[:, :, :, n : n + 512] = total.astype(BF).reshape(half, 2, rows, 512)
                for jx in range(2):
                    for i in range(half):
                        if side == 0:
                            out, at = outs[1 - jy], jx * half + i
                        else:
                            out, at = outs[3 - jx], jy * half + i
                        out[at, :rows] = part_ref[i, where[2] ^ jx]

    outs = [shape_of((len(v), rows + extra, wide)) for v in lists]
    scratch = [pltpu.VMEM((half, 2, rows, wide), BF)]
    return call("up_grad", kernel, outs, (*normeds, *grads, out_own, out_in), None, scratch)


def out_grad(mixed, low):
    chips = 4 * depth()
    rows = D // (2 * chips)
    group = 256 // (2 * rows)

    def kernel(m_ref, l_ref, send_ref, keep_ref):
        core = position()[3]
        for g in range(D // 256):
            at, cols = slice(g * group, (g + 1) * group), slice(g * 256, (g + 1) * 256)
            total = bdot(m_ref[:, cols], l_ref[...], TN).astype(BF).reshape(group, 2, rows, D)
            first, second = total[:, 0], total[:, 1]
            send_ref[at] = jnp.where(core == 0, second, first)
            keep_ref[at] = jnp.where(core == 0, first, second)

    outs = [shape_of((chips, rows, D))] * 2
    return call("out_grad", kernel, outs, (mixed, low))


def back_norm(own, other, hidden, vec, ct, weight):
    def kernel(a_ref, b_ref, h_ref, vec_ref, ct_ref, w_ref, mixed_ref, low_ref, grad_ref, sum_ref):
        first, second = 0.0, 0.0
        for r in range(0, 2 * ROW, ROW):
            rows = slice(r, r + ROW)
            normal, inv = normal_of(h_ref[rows, :])
            grad = a_ref[rows, :] + b_ref[rows, :].astype(F32)
            first = first + jnp.sum(grad * normal, 0, keepdims=True)
            second = second + jnp.sum(grad, 0, keepdims=True)
            total = ct_ref[rows, :].astype(F32) + norm_back(grad, normal, inv, vec_ref[2:3, :])
            grad_ref[rows, :] = total
            low_ref[rows, :] = total.astype(BF)
            mixed_ref[rows, :] = bdot(low_ref[rows, :], w_ref[...], NT).astype(BF)
        sum_ref[0:1, :] = first
        sum_ref[1:2, :] = second

    part = shape_of((2 * ROW, D))
    outs = [part, part, shape_of((2 * ROW, D), F32), shape_of((2, D), F32)]
    return call("back_norm", kernel, outs, (own, other, hidden, vec, ct, weight))


def attn_grad(normed, grads):
    chips = 4 * depth()
    rows = D // (2 * chips)
    group = 256 // (2 * rows)

    def kernel(n_ref, g_ref, send_ref, keep_ref):
        core = position()[3]
        for g in range(D // 256):
            at, cols = slice(g * group, (g + 1) * group), slice(g * 256, (g + 1) * 256)
            for part in range(3):
                total = bdot(n_ref[:, cols], g_ref[part], TN).astype(BF)
                total = total.reshape(group, 2, rows, D)
                first, second = total[:, 0], total[:, 1]
                to = slice(part * D, (part + 1) * D)
                send_ref[at, :, to] = jnp.where(core == 0, second, first)
                keep_ref[at, :, to] = jnp.where(core == 0, first, second)

    outs = [shape_of((chips, rows, 3 * D))] * 2
    return call("attn_grad", kernel, outs, (normed, grads))


def core_sum(own, arrived, sums, sums_in, rel_z):
    lists = layout_yxz()
    chips, rows, wide = own.shape
    lines = sums.shape[0]

    def kernel(a_ref, b_ref, s_ref, t_ref, *rest):
        outs, pad_ref, small_ref = rest[:4], rest[4], rest[5]
        where = position()
        pad_ref[...] = jnp.zeros_like(pad_ref)
        pad_ref[:lines, :] = s_ref[...] + t_ref[...]
        small_ref[...] = jnp.transpose(pad_ref[...]).astype(BF).reshape(chips, 2, rows, 128)
        for out, names in zip(outs, lists):
            for i, name in enumerate(names):
                slot = chip_slot(name, where, rel_z)
                total = a_ref[slot].astype(F32) + b_ref[slot].astype(F32)
                out[i, :, :wide] = total.astype(BF)
                out[i, :, wide:] = small_ref[slot, where[3]]

    outs = [shape_of((len(v), rows, wide + 128)) for v in lists]
    scratch = [pltpu.VMEM((128, D), F32), pltpu.VMEM((chips, 2, rows, 128), BF)]
    return call("core_sum", kernel, outs, (own, arrived, sums, sums_in), None, scratch)


def back_first(grads, weight, resident, vec, hidden_grad):
    def kernel(g_ref, w_ref, x_ref, vec_ref, h_ref, own_ref, send_ref, sum_ref):
        first, second = 0.0, 0.0
        y = position()[0]
        for half, out_ref in ((y, own_ref), (1 - y, send_ref)):
            rows = pl.ds(pl.multiple_of(half * ROW, ROW), ROW)
            normal, inv = normal_of(x_ref[rows, :].astype(F32))
            grad = 0.0
            for part in range(3):
                grad = grad + bdot(g_ref[part, rows, :], w_ref[:, part * D : (part + 1) * D], NT)
            first = first + jnp.sum(grad * normal, 0, keepdims=True)
            second = second + jnp.sum(grad, 0, keepdims=True)
            total = h_ref[rows, :] + norm_back(grad, normal, inv, vec_ref[0:1, :])
            out_ref[...] = total.astype(BF)
        sum_ref[0:1, :] = first
        sum_ref[1:2, :] = second

    outs = [shape_of((ROW, D)), shape_of((ROW, D)), shape_of((2, D), F32)]
    args = (grads, weight, resident, vec, hidden_grad)
    return call("back_first", kernel, outs, args)


def down_back(act, weight, dtype, hidden=None):
    extra = () if hidden is None else (hidden,)

    def kernel(a_ref, w_ref, *refs):
        out_ref = refs[-1]
        for n in range(0, D, 256):
            total = bdot(a_ref[...], w_ref[:, n : n + 256], NN)
            if hidden is not None:
                total = total + refs[0][:, n : n + 256]
            out_ref[:, n : n + 256] = total.astype(dtype)

    outs = [shape_of((2 * ROW, D), dtype)]
    return call("down_back", kernel, outs, (act, weight, *extra))[0]


def result_of(own, other):
    def kernel(a_ref, b_ref, own_ref, send_ref):
        y = position()[0]
        for half, out_ref in ((y, own_ref), (1 - y, send_ref)):
            rows = pl.ds(pl.multiple_of(half * ROW, ROW), ROW)
            out_ref[...] = (a_ref[rows, :] + b_ref[rows, :].astype(F32)).astype(BF)

    return call("result_of", kernel, [shape_of((ROW, D))] * 2, (own, other))


def home(out_own, out_other, grad_own, grad_other):
    lines = ROW // 2

    def kernel(a_ref, b_ref, c_ref, d_ref, out_ref, grad_ref):
        mine = pl.program_id(1) == position()[0]

        @pl.when(mine)
        def _():
            out_ref[0] = a_ref[...]
            grad_ref[0] = c_ref[...].astype(F32)

        @pl.when(jnp.logical_not(mine))
        def _():
            out_ref[0] = b_ref[...]
            grad_ref[0] = d_ref[...].astype(F32)

    part = pl.BlockSpec((lines, D), lambda i, m: (i, 0))
    return pl.pallas_call(
        kernel,
        grid=(2, MICRO),
        out_shape=[
            jax.ShapeDtypeStruct((MICRO, ROW, D), BF),
            jax.ShapeDtypeStruct((MICRO, ROW, D), F32),
        ],
        in_specs=[part] * 4,
        out_specs=[pl.BlockSpec((1, lines, D), lambda i, m: (m, i, 0))] * 2,
        compiler_params=pltpu.CompilerParams(vmem_limit_bytes=16 << 20),
        cost_estimate=pl.CostEstimate(flops=1 << 20, bytes_accessed=1 << 10, transcendentals=0),
        name="home",
    )(out_own, out_other, grad_own, grad_other)


def interleave(own, other):
    rows, wide = own.shape
    size = wide // (4 * depth())

    def kernel(a_ref, b_ref, out_ref):
        core = position()[3]
        for n in range(wide // size):
            cols = slice(n * size, (n + 1) * size)
            for ref, at in ((a_ref, core), (b_ref, 1 - core)):
                to = pl.multiple_of((2 * n + at) * size, size)
                out_ref[:, pl.ds(to, size)] = ref[:, cols]

    return call("interleave", kernel, [shape_of((rows, 2 * wide), F32)], (own, other))[0]


def shards(
    inputs,
    cotangent,
    phone_len,
    prompt_len,
    target_len,
    ln1_gain,
    ln1_bias,
    w_qkv,
    w_out,
    ln2_gain,
    ln2_bias,
    w_up,
    up_bias,
    w_down,
):
    y, z, x, c = position()
    count = depth()
    chips = 4 * count
    row_w = w_qkv.shape[0]
    row_f = w_down.shape[0]

    chain = Chain()

    def split_halves(blocks):
        return (
            lax.dynamic_index_in_dim(blocks, 1 - y, 0, keepdims=False),
            lax.dynamic_index_in_dim(blocks, y, 0, keepdims=False),
        )

    attn_g, up_g, down_g = Gather(chain, True), Gather(chain, False), GatherXZY(chain)
    down_s, up_s, attn_s = ScatterYZX(chain), Scatter(chain, False), Scatter(chain, True)

    vectors = (ln1_gain, ln1_bias, ln2_gain, ln2_bias, up_bias)
    attn_z = attn_g.over_z(chain(pack, w_qkv, w_out, vectors))
    def split_both(inputs, cotangent):
        x_send, x_own = split_halves(inputs)
        ct_send, ct_own = split_halves(cotangent)
        return jnp.stack([x_send, ct_send], 0), x_own, ct_own

    both_send, x_own, ct_own = chain(split_both, inputs[:, 0, 0], cotangent[:, 0, 0])
    both_other = swap(both_send, "y")
    lengths = tuple(
        lax.dynamic_index_in_dim(v, y, 0, keepdims=False)[0]
        for v in (phone_len, prompt_len, target_len)
    )

    def split_up(w_up):
        split = w_up.reshape(row_w, chips, 2, FF // chips // 2)
        return tuple(
            lax.dynamic_index_in_dim(split, i, 2, keepdims=False).reshape(row_w, FF // 2)
            for i in (1 - c, c)
        )

    up_send, up_own = chain(split_up, w_up)
    up_other = swap(up_send, 1)
    up_shard = chain(lambda own, other: ordered(c, own, other, 0), up_own, up_other)
    half_f = row_f // 2

    def join_both(x_own, ct_own, other):
        return ordered(y, x_own, other[0], 0), ordered(y, ct_own, other[1], 0)

    resident, grad_result = chain(join_both, x_own, ct_own, both_other)
    attn_one = attn_g.one(extras=(w_down[:half_f], w_down[half_f:]))
    up_z = up_g.over_z(up_shard, *attn_z)


    attn_two = attn_g.two(extras=(half_f, D))
    early = [(swap(array, 1), rels) for array, rels in attn_g.pieces[::2]]
    down_z = down_g.over_z(attn_g.planes[2], *up_z)
    up_g.one_halves()
    late = [(swap(after(array, *up_g.halves), 1), rels) for array, rels in attn_g.pieces[1::2]]
    up_one = up_g.send(*[v[0] for v in early + late])
    lines = 4 + row_f // row_w
    attn_core = early + late
    many = len(attn_core)

    def unpack_pieces(*arrays):
        own = [(a, p[1]) for a, p in zip(arrays[:many], attn_g.pieces)]
        other = [(a, p[1]) for a, p in zip(arrays[many:], attn_core)]
        return unpack(own, other, attn_g.rel_z, lines)

    qkv_weight, out_weight, vec = chain(
        unpack_pieces, *[p[0] for p in attn_g.pieces + attn_core]
    )
    shift = vec[4:].reshape(row_f // row_w, chips, 2, row_w)
    shift = lax.dynamic_index_in_dim(shift, c, 2, keepdims=False)
    shift = shift.transpose(1, 0, 2).reshape(1, FF // 2)

    normed, qkv = chain(project, resident, vec, qkv_weight)
    up_two = up_g.two()
    mixed, logs = chain(lambda v: attention_forward(v, *lengths), qkv)
    normed_two, hidden = chain(attend, mixed, out_weight, resident, vec)
    ct_sent = swap(grad_result, 1)
    normed_sent = swap(normed_two, 1)

    def with_pieces(step, pieces):
        def run(*args):
            arrays, rest = args[: len(pieces)], args[len(pieces) :]
            return step([(a, p[1]) for a, p in zip(arrays, pieces)], *rest)

        return run

    up_arrays = [p[0] for p in up_g.pieces]
    down_two = down_g.two(*up_two)
    act_own, slope_own, up_weight = chain(
        with_pieces(lambda p, n, s: feed_first(n, p, s), up_g.pieces), *up_arrays, normed_two, shift
    )
    act_other, slope_other = chain(feed_second, normed_sent, up_weight, shift)
    down_sone = down_s.one(
        chain(
            lambda a, b, p, q: down_grad((a, b), (p, q)), act_own, act_other, grad_result, ct_sent
        ),
    )

    pre_own, pre_other, grad_shift, down_weight = chain(
        with_pieces(lambda p, a, b, s, t: back_act((a, b), p, (s, t)), down_g.pieces),
        *[p[0] for p in down_g.pieces],
        grad_result,
        ct_sent,
        slope_own,
        slope_other,
    )
    two_other = swap(chain(lambda g, w: back_up(g, w, BF), pre_other, up_weight), 1)
    two_own = chain(lambda g, w: back_up(g, w, F32), pre_own, up_weight)
    grad_mixed, grad_low, grad_hidden, sums_two = chain(
        back_norm, two_own, two_other, hidden, vec, grad_result, out_weight
    )
    out_send, out_keep = chain(out_grad, mixed, grad_low)
    out_in = swap(out_send, 1)
    down_sz = down_s.over_z()
    up_sone = up_s.one(
        chain(
            lambda a, b, p, q, o, i: up_grad((a, b), (p, q), o, i),
            normed_two,
            normed_sent,
            pre_own,
            pre_other,
            out_keep,
            out_in,
        )
    )
    grads = chain(lambda a, b, v: attention_backward(a, b, v, *lengths), qkv, grad_mixed, logs)
    attn_send, attn_keep = chain(attn_grad, normed, grads)
    attn_in = swap(attn_send, 1)
    gx_own, gx_send, sums_one = chain(back_first, grads, qkv_weight, resident, vec, grad_hidden)

    def small_lines(one, two, shift):
        last = shift.reshape(chips, row_f // row_w, row_w).transpose(1, 0, 2)[:, :, None]
        last = ordered(c, last, jnp.zeros_like(last), 2).reshape(-1, D)
        return jnp.concatenate([one, two, last], 0)

    up_stwo = up_s.two()
    sums = chain(small_lines, sums_one, sums_two, grad_shift)
    sums_in = swap(sums, 1)
    attn_parts = chain(
        lambda a, b, p, q: core_sum(a, b, p, q, attn_s.rel_z), attn_keep, attn_in, sums, sums_in
    )
    attn_sone = attn_s.one(attn_parts, *up_stwo)
    down_sent = swap(chain(lambda a, w: down_back(a, w, BF), act_other, down_weight), 1)
    down_own = chain(lambda a, w, h: down_back(a, w, F32, h), act_own, down_weight, hidden)
    up_sz = up_s.over_z()

    down_sz = down_sz.reshape(4, half_f, D)
    attn_stwo = attn_s.two(extras=(down_sz,))
    res_own, res_send = chain(result_of, down_own, down_sent)
    sum_up = chain(up_s.total, up_sz)
    sum_up = sum_up.reshape(-1, FF // 2)
    out_rows = sum_up[2 * row_w :]
    sum_out = jnp.concatenate([out_rows[:, :D], out_rows[:, D:]], 0)
    up_rows = sum_up[: 2 * row_w].reshape(2, row_w, FF // 2)
    up_mine = lax.dynamic_index_in_dim(up_rows, c, 0, keepdims=False)
    up_theirs = swap(lax.dynamic_index_in_dim(up_rows, 1 - c, 0, keepdims=False), 1)
    attn_sz = attn_s.over_z()
    gx_other = swap(after(gx_send, *attn_stwo), "y")
    out_other = swap(after(res_send, *attn_stwo), "y")

    def sum_of_down(lines, from_x, from_y):
        upper, lower = lines[0], lines[2]
        from_x, from_y = (v[:, 3 * D + 128 :].reshape(half_f, D) for v in (from_x, from_y))
        return jnp.concatenate([plus(upper.astype(F32), from_x), plus(lower.astype(F32), from_y)], 0)

    sum_down = chain(sum_of_down, down_sz, *attn_stwo)

    up_final = chain(interleave, up_mine, up_theirs)
    out_stack, grad_stack = chain(home, res_own, out_other, gx_own, gx_other)
    out_stack, grad_stack = (v.reshape(MICRO, 1, 1, ROW, D) for v in (out_stack, grad_stack))
    sum_attn = attn_s.total(attn_sz)
    small_sum = sum_attn[:, 3 * D : 3 * D + lines].T.reshape(-1)
    edges = [i * row_w for i in range(5)]
    small_out = [small_sum[a:b] for a, b in zip(edges[:4], edges[1:])]
    return (
        out_stack,
        grad_stack,
        small_out[0],
        small_out[1],
        sum_attn[:, : 3 * D],
        sum_out,
        small_out[2],
        small_out[3],
        up_final.reshape(row_w, FF),
        small_sum[4 * row_w : 4 * row_w + row_f],
        sum_down,
    )


def plain_passed_along(block, axis, distance):
    devices = range(lax.axis_size(axis))
    route = [(i - distance, i) for i in devices if i - distance in devices]
    return lax.ppermute(block, axis, route)


def plain_times_transposed(left, right):
    return lax.dot_general(
        left, right, (((1,), (1,)), ((), ())), preferred_element_type=jnp.float32
    )


def plain_transposed_times(left, right):
    return lax.dot_general(
        left, right, (((0,), (0,)), ((), ())), preferred_element_type=jnp.float32
    )


def plain_layer_norm(values, gain, bias):
    center = values - jnp.mean(values, -1, keepdims=True)
    spread = jnp.mean(center * center, -1, keepdims=True)
    return center * lax.rsqrt(spread + 1e-05) * gain + bias


def plain_locate(lengths, slot_ids):
    count = jnp.arange(lengths.shape[0])
    seg_ends = jnp.sum(jnp.where(count[None, :] <= count[:, None], lengths[None, :], 0), 1, dtype=jnp.int32)
    seg_ids = jnp.sum(
        (slot_ids[:, None] >= seg_ends[None, :]).astype(jnp.int32), 1, dtype=jnp.int32
    )
    one_hot = (seg_ids[:, None] == jnp.arange(lengths.shape[0], dtype=jnp.int32)[None, :]).astype(
        jnp.int32
    )
    seg_start = jnp.sum(one_hot * (seg_ends - lengths)[None, :], 1, dtype=jnp.int32)
    return (seg_ids, one_hot, slot_ids - seg_start)


def plain_frame_meta(phone_lens, prompt_lens, target_lens, slot_count):
    slot_ids = jnp.arange(slot_count, dtype=jnp.int32)
    pre_seg, pre_hot, pre_off = plain_locate(phone_lens + prompt_lens, slot_ids)
    pre_phone = jnp.sum(pre_hot * phone_lens[None, :], 1, dtype=jnp.int32)
    prefix = (pre_seg, pre_off < pre_phone, pre_off - pre_phone)
    tgt_seg, tgt_hot, tgt_off = plain_locate(target_lens, slot_ids)
    tgt_pos = jnp.sum(tgt_hot * prompt_lens[None, :], 1, dtype=jnp.int32) + tgt_off
    targets = (tgt_seg, tgt_off < 0, tgt_pos)
    return (prefix, targets)


def plain_allowed(query_meta, key_meta):
    same_seg = query_meta[0][:, None] == key_meta[0][None, :]
    audio_ok = key_meta[1][None, :] | (key_meta[2][None, :] <= query_meta[2][:, None])
    return same_seg & jnp.where(query_meta[1][:, None], key_meta[1][None, :], audio_ok)


def plain_masked_scores(queries, key_rows, allowed_mask, score_scale):
    scores = (
        jnp.einsum("qhd,khd->hqk", queries, key_rows, preferred_element_type=jnp.float32)
        * score_scale
    )
    return jnp.where(allowed_mask[None], scores, -1e30)


def plain_attention_forward(queries, key_rows, value_rows, allowed_mask, score_scale):
    scores = plain_masked_scores(queries, key_rows, allowed_mask, score_scale)
    peak = jnp.max(scores, -1, keepdims=True)
    exp_scores = jnp.exp(scores - peak)
    row_total = jnp.sum(exp_scores, -1, keepdims=True)
    probs = (exp_scores / row_total).astype(jnp.bfloat16)
    mixed = jnp.einsum("hqk,khd->qhd", probs, value_rows, preferred_element_type=jnp.float32)
    return (mixed.astype(jnp.bfloat16), peak + jnp.log(row_total))


def plain_attention_backward(
    queries, key_rows, value_rows, allowed_mask, log_total, grad_mixed, score_scale
):
    scores = plain_masked_scores(queries, key_rows, allowed_mask, score_scale)
    probs = jnp.where(allowed_mask[None], jnp.exp(scores - log_total), 0.0)
    grad_probs = jnp.einsum(
        "qhd,khd->hqk", grad_mixed, value_rows, preferred_element_type=jnp.float32
    )
    grad_values = jnp.einsum(
        "hqk,qhd->khd", probs.astype(jnp.bfloat16), grad_mixed, preferred_element_type=jnp.float32
    )
    inner = jnp.sum(grad_probs * probs, -1, keepdims=True)
    grad_scores = (probs * (grad_probs - inner)).astype(jnp.bfloat16)
    grad_queries = (
        jnp.einsum("hqk,khd->qhd", grad_scores, key_rows, preferred_element_type=jnp.float32)
        * score_scale
    )
    grad_keys = (
        jnp.einsum("hqk,qhd->khd", grad_scores, queries, preferred_element_type=jnp.float32)
        * score_scale
    )
    return (grad_queries, grad_keys, grad_values)


def plain_add_up(summed, fresh):
    if summed is None:
        return fresh
    return jax.tree.map(lambda summed_part, fresh_part: summed_part + fresh_part, summed, fresh)


def plain_fetch_forward(params):
    return (
        lax.all_gather(params[0], ("pair", "rows"), axis=0, tiled=True),
        lax.all_gather(params[1], ("pair", "rows"), axis=0, tiled=True),
        lax.all_gather(params[2], ("pair", "rows"), axis=0, tiled=True),
        lax.all_gather(params[3], ("pair", "rows"), axis=0, tiled=True),
        lax.all_gather(params[4], ("pair", "rows"), axis=0, tiled=True),
        lax.all_gather(params[5], ("pair", "rows"), axis=0, tiled=True),
        lax.all_gather(params[6], ("pair", "rows"), axis=0, tiled=True),
        lax.all_gather(params[7], ("pair", "rows"), axis=0, tiled=True),
        lax.all_gather(params[8], ("pair", "rows"), axis=0, tiled=True),
    )


def plain_shards(
    inputs,
    cotangent,
    phone_len,
    prompt_len,
    target_len,
    ln1_gain,
    ln1_bias,
    w_qkv,
    w_out,
    ln2_gain,
    ln2_bias,
    w_up,
    up_bias,
    w_down,
):
    half_index = lax.axis_index("pair")
    score_scale = HEAD ** (-0.5)
    params = (ln1_gain, ln1_bias, w_qkv, w_out, ln2_gain, ln2_bias, w_up, up_bias, w_down)
    out_blocks = []
    grad_blocks = []
    summed = None
    for batch_index in range(MICRO):
        gathered = plain_fetch_forward(params)
        (
            gain_one,
            bias_one,
            qkv_weight,
            out_weight,
            gain_two,
            bias_two,
            up_weight,
            up_shift,
            down_weight,
        ) = gathered
        gain_one_f = gain_one.astype(jnp.float32)
        bias_one_f = bias_one.astype(jnp.float32)
        gain_two_f = gain_two.astype(jnp.float32)
        bias_two_f = bias_two.astype(jnp.float32)
        prefix, targets = plain_frame_meta(
            phone_len[batch_index, 0], prompt_len[batch_index, 0], target_len[batch_index, 0], ROW
        )
        query_meta = tuple(
            (
                jnp.where(half_index == 0, pre_field, tgt_field)
                for pre_field, tgt_field in zip(prefix, targets)
            )
        )
        remote_mask = plain_allowed(query_meta, prefix) & (half_index == 1)
        allowed_mask = jnp.concatenate([remote_mask, plain_allowed(query_meta, query_meta)], 1)
        resident = inputs[batch_index, 0, 0].astype(jnp.float32)
        normed = plain_layer_norm(resident, gain_one_f, bias_one_f).astype(jnp.bfloat16)
        qkv_rows = jnp.dot(normed, qkv_weight, preferred_element_type=jnp.float32).astype(
            jnp.bfloat16
        )
        own_kv = qkv_rows[:, D:]
        remote_kv = plain_passed_along(own_kv, "pair", 1)
        queries = qkv_rows[:, :D].reshape(ROW, HEADS, HEAD)
        key_rows = jnp.concatenate([remote_kv[:, :D], own_kv[:, :D]], 0).reshape(
            2 * ROW, HEADS, HEAD
        )
        value_rows = jnp.concatenate([remote_kv[:, D:], own_kv[:, D:]], 0).reshape(
            2 * ROW, HEADS, HEAD
        )
        mixed, log_total = plain_attention_forward(
            queries, key_rows, value_rows, allowed_mask, score_scale
        )
        mixed_flat = mixed.reshape(ROW, D)
        hidden_res = resident + jnp.dot(mixed_flat, out_weight, preferred_element_type=jnp.float32)
        normed_two = plain_layer_norm(hidden_res, gain_two_f, bias_two_f).astype(jnp.bfloat16)
        pre_act = jnp.dot(
            normed_two, up_weight, preferred_element_type=jnp.float32
        ) + up_shift.astype(jnp.float32)
        activ = jax.nn.gelu(pre_act, approximate=True).astype(jnp.bfloat16)
        result = hidden_res + jnp.dot(activ, down_weight, preferred_element_type=jnp.float32)
        out_blocks.append(result.astype(jnp.bfloat16))
        gathered = (
            lax.all_gather(params[0], ("pair", "rows"), axis=0, tiled=True),
            lax.all_gather(params[1], ("pair", "rows"), axis=0, tiled=True),
            lax.all_gather(params[2], ("pair", "rows"), axis=0, tiled=True),
            lax.all_gather(params[3], ("pair", "rows"), axis=0, tiled=True),
            lax.all_gather(params[4], ("pair", "rows"), axis=0, tiled=True),
            lax.all_gather(params[5], ("pair", "rows"), axis=0, tiled=True),
            lax.all_gather(params[6], ("pair", "rows"), axis=0, tiled=True),
            lax.all_gather(params[7], ("pair", "rows"), axis=0, tiled=True),
            lax.all_gather(params[8], ("pair", "rows"), axis=0, tiled=True),
        )
        (
            gain_one,
            bias_one,
            qkv_weight,
            out_weight,
            gain_two,
            bias_two,
            up_weight,
            up_shift,
            down_weight,
        ) = gathered
        gain_one_f = gain_one.astype(jnp.float32)
        bias_one_f = bias_one.astype(jnp.float32)
        gain_two_f = gain_two.astype(jnp.float32)
        bias_two_f = bias_two.astype(jnp.float32)
        grad_result = cotangent[batch_index, 0, 0]
        grad_down = plain_transposed_times(activ, grad_result)
        grad_activ = plain_times_transposed(grad_result, down_weight)
        _, gelu_back = jax.vjp(lambda pre_value: jax.nn.gelu(pre_value, approximate=True), pre_act)
        grad_pre = gelu_back(grad_activ)[0].astype(jnp.bfloat16)
        grad_up = plain_transposed_times(normed_two, grad_pre)
        grad_up_bias = jnp.sum(grad_pre.astype(jnp.float32), 0)
        grad_normed_two = plain_times_transposed(grad_pre, up_weight)
        _, norm_back_two = jax.vjp(plain_layer_norm, hidden_res, gain_two_f, bias_two_f)
        grad_hidden_ln, grad_gain_two, grad_bias_two = norm_back_two(grad_normed_two)
        grad_hidden = grad_result.astype(jnp.float32) + grad_hidden_ln
        grad_hidden_low = grad_hidden.astype(jnp.bfloat16)
        grad_out_w = plain_transposed_times(mixed_flat, grad_hidden_low)
        grad_mixed = (
            plain_times_transposed(grad_hidden_low, out_weight)
            .astype(jnp.bfloat16)
            .reshape(ROW, HEADS, HEAD)
        )
        grad_queries, grad_keys, grad_values = plain_attention_backward(
            queries, key_rows, value_rows, allowed_mask, log_total, grad_mixed, score_scale
        )
        remote_grads = jnp.concatenate(
            [grad_keys[:ROW].reshape(ROW, D), grad_values[:ROW].reshape(ROW, D)], 1
        )
        returned = plain_passed_along(remote_grads.astype(jnp.bfloat16), "pair", -1).astype(
            remote_grads.dtype
        )
        grad_qkv_rows = jnp.concatenate(
            [
                grad_queries.reshape(ROW, D),
                grad_keys[ROW:].reshape(ROW, D) + returned[:, :D],
                grad_values[ROW:].reshape(ROW, D) + returned[:, D:],
            ],
            1,
        ).astype(jnp.bfloat16)
        grad_qkv_w = plain_transposed_times(normed, grad_qkv_rows)
        grad_normed = plain_times_transposed(grad_qkv_rows, qkv_weight)
        _, norm_back_one = jax.vjp(plain_layer_norm, resident, gain_one_f, bias_one_f)
        grad_resident_ln, grad_gain_one, grad_bias_one = norm_back_one(grad_normed)
        grad_blocks.append(grad_hidden + grad_resident_ln)
        local_grads = (
            grad_gain_one,
            grad_bias_one,
            grad_qkv_w,
            grad_out_w,
            grad_gain_two,
            grad_bias_two,
            grad_up,
            grad_up_bias,
            grad_down,
        )
        shard_part = (
            lax.psum_scatter(local_grads[0], ("pair", "rows"), scatter_dimension=0, tiled=True),
            lax.psum_scatter(local_grads[1], ("pair", "rows"), scatter_dimension=0, tiled=True),
            lax.psum_scatter(local_grads[2], ("pair", "rows"), scatter_dimension=0, tiled=True),
            lax.psum_scatter(local_grads[3], ("pair", "rows"), scatter_dimension=0, tiled=True),
            lax.psum_scatter(local_grads[4], ("pair", "rows"), scatter_dimension=0, tiled=True),
            lax.psum_scatter(local_grads[5], ("pair", "rows"), scatter_dimension=0, tiled=True),
            lax.psum_scatter(local_grads[6], ("pair", "rows"), scatter_dimension=0, tiled=True),
            lax.psum_scatter(local_grads[7], ("pair", "rows"), scatter_dimension=0, tiled=True),
            lax.psum_scatter(local_grads[8], ("pair", "rows"), scatter_dimension=0, tiled=True),
        )
        summed = plain_add_up(summed, shard_part)
    block_shape = (MICRO, 1, 1, ROW, D)
    out_stack = jnp.stack(out_blocks, 0).reshape(block_shape)
    grad_stack = jnp.stack(grad_blocks, 0).reshape(block_shape)
    return (
        out_stack,
        grad_stack,
        summed[0],
        summed[1],
        summed[2],
        summed[3],
        summed[4],
        summed[5],
        summed[6],
        summed[7],
        summed[8],
    )


def solution(mesh):
    rows = P(None, "rows", "pair", None, None)
    line = P(("pair", "rows"))
    flat = P(("pair", "rows"), None)
    lens = P(None, "rows", None)
    return jax.shard_map(
        shards if mesh.shape["rows"] == 16 else plain_shards,
        mesh=mesh,
        in_specs=(rows, rows, lens, lens, lens, line, line, flat, flat, line, line, flat, line, flat),
        out_specs=(rows, rows, line, line, flat, flat, line, line, flat, line, flat),
        check_vma=False,
    )
```
